128 devices in a mesh: gx: 16 (over z, y), gy: 8 (over x, core).
Axes of the slice: x: 4, y: 4, z: 4, core: 2. Of those that a mesh axis runs over, the one named last changes fastest.
Arguments:
- nest_field: float32 [96, 256, 1024], P(None, 'gx', 'gy'), may hold values from -6 to 6
- courant_x: float32 [96, 256, 1024], P(None, 'gx', 'gy'), may hold values from -0.35 to 0.35
- courant_y: float32 [96, 256, 1024], P(None, 'gx', 'gy'), may hold values from -0.35 to 0.35
- courant_z: float32 [96, 256, 1024], P(None, 'gx', 'gy'), may hold values from -0.25 to 0.25
- terrain: int32 [256, 1024], P('gx', 'gy'), may hold values from 0 to 31
- relax: float32 [256, 1024], P('gx', 'gy'), may hold values from 0.1 to 0.6
- interp_index: int32 [4, 256, 1024], P(None, 'gx', 'gy'), may hold values from 0 to 32767, as said below
- interp_weight: float32 [4, 256, 1024], P(None, 'gx', 'gy'), may hold values from 0.05 to 0.5
- send_slots: int32 [128, 256], P(('gx', 'gy')), may hold values from 0 to 32, as said below
- parent_field: float32 [96, 512, 1024], P(None, 'gx', 'gy'), may hold values from -6 to 6
- parent_cx: float32 [96, 512, 1024], P(None, 'gx', 'gy'), may hold values from -0.45 to 0.45
- parent_cy: float32 [96, 512, 1024], P(None, 'gx', 'gy'), may hold values from -0.45 to 0.45
- fb_index: int32 [128, 256, 81], P(('gx', 'gy')), may hold values from 0 to 2047
- fb_slot: int32 [128, 512], P(('gx', 'gy')), may hold values from 0 to 256, as said below
- fb_target: int32 [128, 512], P(('gx', 'gy')), may hold values from 0 to 4096, as said below
Outputs:
- nest_out: float32 [96, 256, 1024], P(None, 'gx', 'gy')
- parent_out: float32 [96, 512, 1024], P(None, 'gx', 'gy')
The draws below stay inside these ranges and needn't reach their ends.
Inputs may be any that keep to these rules, and one draw needn't show every extreme that they name: `send_slots`: index 32 marks an empty slot; the rest name slabs of the sender. Slots to one owner are filled from the first. One busy nest owner gets all 2 slots full from every device; each device sends at least one slab to itself. `interp_index`: every index points at a column of a filled slot received by the column's own device; the four indices of a column lie in one slot, at consecutive columns of the slab (cyclically). `fb_slot`: index 256 marks an empty slot; each of a device's rows stands in at most one slot. One busy parent owner receives all 4 slots full from every device. `fb_target`: A slot's target is 4096 exactly where the sender left that slot empty; targets may repeat.
All inputs are finite; a program needn't handle non-finite values.
Results may differ from the reference program's by a relative error of at most 0.0003.
Values sent between devices are 32-bit elements; how exact they have to be, the bound alone decides.
A program may use at most 128 MiB of HBM per device.

```python
import jax
import jax.numpy as jnp
from jax import lax

LEV = 96
PX = 32
PY = 128
NXD = 16
NYD = 128
TILE = 128
CAP = 2
FCAP = 4
R = 81
SUBSTEPS = 3
FB_DEV = 256
TILES_DEV = 32
PCOL = 4096
PXG = 512
PYG = 1024
NXG = 256
NYG = 1024
N_GX = 16
N_GY = 8
DEVICES = 128


def boundary_plan(key):
    key = jax.random.fold_in(key, 101)
    first, second, third = jax.random.split(key, 3)
    busy = jax.random.randint(first, (), 0, DEVICES)
    counts = jax.random.randint(second, (DEVICES, DEVICES), 0, CAP + 1)
    source = lax.broadcasted_iota(jnp.int32, (DEVICES, DEVICES), 0)
    target = lax.broadcasted_iota(jnp.int32, (DEVICES, DEVICES), 1)
    counts = jnp.where(target == busy, CAP, counts)
    counts = jnp.where(source == target, jnp.maximum(counts, 1), counts)
    filled = jnp.arange(CAP, dtype=jnp.int32)[None, None, :] < counts[:, :, None]
    slabs = jax.random.randint(third, (DEVICES, DEVICES, CAP), 0, TILES_DEV)
    return (filled, jnp.where(filled, slabs, TILES_DEV).astype(jnp.int32))


def feedback_plan(key):
    key = jax.random.fold_in(key, 202)
    first, second, third = jax.random.split(key, 3)
    busy = jax.random.randint(first, (), 0, DEVICES)
    width = DEVICES * FCAP
    place = jnp.arange(width, dtype=jnp.int32)
    inbusy = place // FCAP == busy
    keep = jax.random.randint(third, (DEVICES, width), 0, 2) == 1
    allowed = inbusy[None] | keep
    noise = jax.random.randint(second, (DEVICES, width), 1, 2 ** 18) * (2 * width) + place[None]
    scores = jnp.where(inbusy[None], place[None], jnp.where(allowed, noise, 2 ** 29 + place[None]))
    order = jnp.argsort(scores, axis=1)
    ranks = jnp.argsort(order, axis=1).astype(jnp.int32)
    return jnp.where(allowed & (ranks < FB_DEV), ranks, FB_DEV).astype(jnp.int32)


def draw_send_slots(key, part):
    filled, slots = boundary_plan(key)
    return slots.reshape(DEVICES, DEVICES * CAP)


def draw_interp_index(key, part):
    filled, slots = boundary_plan(key)
    key = jax.random.fold_in(key, 7)
    first, second = jax.random.split(key)
    per_dest = filled.transpose(1, 0, 2).reshape(DEVICES, DEVICES * CAP)
    place = jnp.arange(DEVICES * CAP, dtype=jnp.int32)
    scores = jnp.where(per_dest, 0, DEVICES * CAP) + place[None]
    order = jnp.argsort(scores, axis=1).astype(jnp.int32)
    count = jnp.sum(per_dest.astype(jnp.int32), axis=1)
    columns = NXD * NYD
    pick = jax.random.randint(first, (DEVICES, columns), 0, 2 ** 20) % count[:, None]
    slot = jnp.take_along_axis(order, pick, axis=1)
    start = jax.random.randint(second, (DEVICES, columns), 0, TILE)
    offsets = jnp.arange(4, dtype=jnp.int32)[None, :, None]
    index = slot[:, None, :] * TILE + (start[:, None, :] + offsets) % TILE
    index = index.reshape(N_GX, N_GY, 4, NXD, NYD).transpose(2, 0, 3, 1, 4)
    return index.reshape(4, N_GX * NXD, N_GY * NYD).astype(jnp.int32)


def draw_fb_slot(key, part):
    return feedback_plan(key)


def draw_fb_target(key, part):
    slots = feedback_plan(key)
    key = jax.random.fold_in(key, 9)
    back = slots.reshape(DEVICES, DEVICES, FCAP).transpose(1, 0, 2).reshape(DEVICES, DEVICES * FCAP)
    columns = jax.random.randint(key, (DEVICES, DEVICES * FCAP), 0, PX * PY)
    return jnp.where(back < FB_DEV, columns, PX * PY).astype(jnp.int32)


def plant(result, stream_key, least, high):
    longest = result.shape.index(max(result.shape))
    spots = []
    for shift in (0, 1):
        where = [jax.random.randint(jax.random.fold_in(stream_key, axis), (), 0, length) for axis, length in enumerate(result.shape)]
        where[longest] = (where[longest] + shift) % result.shape[longest]
        spots.append(tuple(where))
    return result.at[spots[0]].set(least).at[spots[1]].set(high)


def block_levels(own_key, extent, shards, least, largest):
    def one(axis_at, shards_of):
        draws = jax.random.uniform(jax.random.fold_in(jax.random.fold_in(own_key, 6), axis_at), (shards_of,), jnp.float32, least / len(shards), largest / len(shards))
        return jnp.repeat(jnp.exp(draws), extent[axis_at] // shards_of).reshape((-1,) + (1,) * (len(extent) - axis_at - 1))

    loudness = one(*shards[0])
    for cut in shards[1:]:
        loudness = loudness * one(*cut)
    return loudness


def normal_values(own_key, extent, spread, bound, shards=(), kind=jnp.bfloat16):
    array = spread * jax.random.normal(own_key, extent, jnp.float32)
    if shards:
        array = array * block_levels(own_key, extent, shards, -0.22, 0.18)
    return jnp.clip(array, -bound, bound).astype(kind)


def setup_inputs(seed: int = 0) -> dict:
    seeds = jax.random.split(jax.random.key(seed), 16)
    return {
        "nest_field": normal_values(seeds[0], (LEV, NXG, NYG), 1.0, 6.0, ((1, 16), (2, 8)), jnp.float32),
        "courant_x": jnp.clip(jax.random.uniform(seeds[1], (LEV, NXG, NYG), jnp.float32, -0.35, 0.35) * block_levels(seeds[1], (LEV, NXG, NYG), ((1, 16), (2, 8)), -0.4, 0.0), -0.35, 0.35),
        "courant_y": jnp.clip(jax.random.uniform(seeds[2], (LEV, NXG, NYG), jnp.float32, -0.35, 0.35) * block_levels(seeds[2], (LEV, NXG, NYG), ((1, 16), (2, 8)), -0.4, 0.0), -0.35, 0.35),
        "courant_z": jnp.clip(jax.random.uniform(seeds[3], (LEV, NXG, NYG), jnp.float32, -0.25, 0.25) * block_levels(seeds[3], (LEV, NXG, NYG), ((1, 16), (2, 8)), -0.4, 0.0), -0.25, 0.25),
        "terrain": plant(jax.random.randint(seeds[4], (NXG, NYG), 0, LEV // 3), jax.random.fold_in(seeds[4], 1), 0, (LEV // 3) - 1).astype(jnp.int32),
        "relax": jnp.clip(0.1 + 0.5 * jax.random.uniform(seeds[5], (NXG, NYG), jnp.float32) ** block_levels(seeds[5], (NXG, NYG), ((0, 16), (1, 8)), -0.2, 0.2), 0.1, 0.6),
        "interp_index": draw_interp_index(jax.random.fold_in(seeds[15], 71), 0),
        "interp_weight": jnp.clip(0.05 + 0.45 * jax.random.uniform(seeds[7], (4, NXG, NYG), jnp.float32) ** block_levels(seeds[7], (4, NXG, NYG), ((1, 16), (2, 8)), -0.2, 0.2), 0.05, 0.5),
        "send_slots": draw_send_slots(jax.random.fold_in(seeds[15], 71), 0),
        "parent_field": normal_values(seeds[9], (LEV, PXG, PYG), 1.0, 6.0, ((1, 16), (2, 8)), jnp.float32),
        "parent_cx": jnp.clip(jax.random.uniform(seeds[10], (LEV, PXG, PYG), jnp.float32, -0.45, 0.45) * block_levels(seeds[10], (LEV, PXG, PYG), ((1, 16), (2, 8)), -0.4, 0.0), -0.45, 0.45),
        "parent_cy": jnp.clip(jax.random.uniform(seeds[11], (LEV, PXG, PYG), jnp.float32, -0.45, 0.45) * block_levels(seeds[11], (LEV, PXG, PYG), ((1, 16), (2, 8)), -0.4, 0.0), -0.45, 0.45),
        "fb_index": plant(jax.random.randint(seeds[12], (DEVICES, FB_DEV, R), 0, NXD * NYD), jax.random.fold_in(seeds[12], 1), 0, (NXD * NYD) - 1).astype(jnp.int32),
        "fb_slot": draw_fb_slot(jax.random.fold_in(seeds[15], 71), 0),
        "fb_target": draw_fb_target(jax.random.fold_in(seeds[15], 71), 0),
    }


blend_rate = 0.5


def to_devices(field, nx, ny):
    lead = field.shape[0]
    blocks = field.reshape(lead, N_GX, nx, N_GY, ny).transpose(1, 3, 0, 2, 4)
    return blocks.reshape(N_GX * N_GY, lead, nx * ny)


def from_devices(blocks, nx, ny):
    lead = blocks.shape[1]
    grid = blocks.reshape(N_GX, N_GY, lead, nx, ny).transpose(2, 0, 3, 1, 4)
    return grid.reshape(lead, N_GX * nx, N_GY * ny)


def horizontal(field, cx, cy):
    padded = jnp.pad(field, ((0, 0), (1, 1), (1, 1)))
    west = padded[:, :-2, 1:-1]
    east = padded[:, 2:, 1:-1]
    south = padded[:, 1:-1, :-2]
    north = padded[:, 1:-1, 2:]
    return cx * jnp.where(cx > 0, field - west, east - field) + cy * jnp.where(cy > 0, field - south, north - field)


def vertical(field, cz, mask):
    below = jnp.concatenate([field[:1], field[:-1]], axis=0)
    mask_below = jnp.concatenate([jnp.zeros_like(mask[:1]), mask[:-1]], axis=0)
    below = jnp.where(mask_below, below, field)
    above = jnp.concatenate([field[1:], field[-1:]], axis=0)
    return cz * jnp.where(cz > 0, field - below, above - field)


def reference(nest_field, courant_x, courant_y, courant_z, terrain, relax, interp_index, interp_weight, send_slots, parent_field, parent_cx, parent_cy, fb_index, fb_slot, fb_target):
    devices = N_GX * N_GY
    levels = lax.broadcasted_iota(jnp.int32, (LEV, 1, 1), 0)
    mask = levels >= terrain[None]
    slabs = to_devices(parent_field, PX, PY).reshape(devices, LEV, TILES_DEV, TILE)
    slabs = jnp.concatenate([slabs, jnp.zeros((devices, LEV, 1, TILE), jnp.float32)], axis=2)
    slots = send_slots.reshape(devices, devices, CAP)
    index_dev = to_devices(interp_index, NXD, NYD)
    weight_dev = to_devices(interp_weight, NXD, NYD)

    def boundary_of(dest):
        chosen = slots[:, dest, :]
        got = jax.vmap(lambda slab, pick: jnp.take(slab, pick, axis=1))(slabs, chosen)
        flat = got.transpose(1, 0, 2, 3).reshape(LEV, -1)
        idx = index_dev[dest]
        wts = weight_dev[dest]
        total = wts[0][None] * jnp.take(flat, idx[0], axis=1)
        for j in range(1, 4):
            total = total + wts[j][None] * jnp.take(flat, idx[j], axis=1)
        return total

    boundary = lax.map(boundary_of, jnp.arange(devices, dtype=jnp.int32))
    boundary = from_devices(boundary, NXD, NYD)
    field = jnp.where(mask, nest_field, 0.0)
    for step in range(SUBSTEPS):
        adv = field - horizontal(field, courant_x, courant_y) - vertical(field, courant_z, mask)
        field = jnp.where(mask, adv + relax[None] * (boundary - adv), 0.0)
    nest_out = field
    advected = parent_field - horizontal(parent_field, parent_cx, parent_cy)

    nest_dev = to_devices(nest_out, NXD, NYD)

    def rows_of(item):
        local, ind = item
        cols = jnp.take(local, ind.reshape(-1), axis=1).reshape(LEV, FB_DEV, R)
        return jnp.mean(cols, axis=2).T

    rows = lax.map(rows_of, (nest_dev, fb_index))
    rows = jnp.concatenate([rows, jnp.zeros((devices, 1, LEV), jnp.float32)], axis=1)
    fslots = fb_slot.reshape(devices, devices * FCAP)
    sent = jax.vmap(lambda r, s: jnp.take(r, s, axis=0).reshape(devices, FCAP, LEV))(rows, fslots)
    recv = sent.transpose(1, 0, 2, 3).reshape(devices, devices * FCAP, LEV)
    parent_dev = to_devices(advected, PX, PY)

    def apply(local, values, target):
        current = jnp.take(local, jnp.minimum(target, PCOL - 1), axis=1)
        delta = blend_rate * (values.T - current)
        return local.at[:, target].add(delta, mode="drop")

    parent_dev = jax.vmap(apply)(parent_dev, recv, fb_target)
    parent_out = from_devices(parent_dev, PX, PY)
    return nest_out, parent_out
```

```python
import functools

import jax
import jax.numpy as jnp
from jax import lax
from jax.experimental import pallas as pl
from jax.experimental.pallas import tpu as pltpu
from jax.sharding import PartitionSpec as P

TILE = 128
CAP = 2
FCAP = 4
SUBSTEPS = 3


blend_rate = 0.5


def extended(block, sides, width):
    for axis, dim in sides:
        count = lax.axis_size(axis)
        forward = [(i, i + 1) for i in range(count - 1)]
        backward = [(target, source) for source, target in forward]
        low = lax.ppermute(
            lax.slice_in_dim(block, block.shape[dim] - width, None, axis=dim), axis, forward
        )
        high = lax.ppermute(lax.slice_in_dim(block, 0, width, axis=dim), axis, backward)
        block = jnp.concatenate([low, block, high], axis=dim)
    return block


def upwind(padded, field, cx, cy):
    west = padded[:, :-2, 1:-1]
    east = padded[:, 2:, 1:-1]
    south = padded[:, 1:-1, :-2]
    north = padded[:, 1:-1, 2:]
    return cx * jnp.where(cx > 0, field - west, east - field) + cy * jnp.where(
        cy > 0, field - south, north - field
    )


def vertical(field, cz, mask):
    below = jnp.concatenate([field[:1], field[:-1]], axis=0)
    mask_below = jnp.concatenate([jnp.zeros_like(mask[:1]), mask[:-1]], axis=0)
    below = jnp.where(mask_below, below, field)
    above = jnp.concatenate([field[1:], field[-1:]], axis=0)
    return cz * jnp.where(cz > 0, field - below, above - field)


def dense_step(
    nest_field,
    courant_x,
    courant_y,
    courant_z,
    terrain,
    relax,
    interp_index,
    interp_weight,
    send_slots,
    parent_field,
    parent_cx,
    parent_cy,
    fb_index,
    fb_slot,
    fb_target,
):
    n_east = lax.axis_size("gx")
    n_north = lax.axis_size("gy")
    devices = n_east * n_north
    levels, nest_x, nest_y = nest_field.shape
    parent_x, parent_y = (parent_field.shape[1], parent_field.shape[2])
    parent_cols = parent_x * parent_y
    nest_cols = nest_x * nest_y
    slabs = parent_field
    slabs = jnp.concatenate([slabs, jnp.zeros((levels, 1, TILE), jnp.float32)], axis=1)
    picked = jnp.take(slabs, send_slots[0], axis=1)
    outgoing = picked.reshape(levels, devices, CAP, TILE)
    incoming = lax.all_to_all(outgoing, ("gx", "gy"), split_axis=1, concat_axis=1, tiled=True)
    received_cols = incoming.reshape(levels, -1).T
    padded_parent = extended(parent_field, (("gx", 1), ("gy", 2)), 1)
    advected = parent_field - upwind(padded_parent, parent_field, parent_cx, parent_cy)
    index_flat = interp_index.reshape(4, -1)
    weight_flat = interp_weight.reshape(4, -1)
    boundary_cols = weight_flat[0][:, None] * jnp.take(received_cols, index_flat[0], axis=0)
    for j in range(1, 4):
        boundary_cols = boundary_cols + weight_flat[j][:, None] * jnp.take(
            received_cols, index_flat[j], axis=0
        )
    boundary = boundary_cols.T.reshape(levels, nest_x, nest_y)
    level_ids = lax.broadcasted_iota(jnp.int32, (levels, 1, 1), 0)
    mask = level_ids >= terrain[None]
    field = jnp.where(mask, nest_field, 0.0)
    for step in range(SUBSTEPS):
        padded = extended(field, (("gx", 1), ("gy", 2)), 1)
        adv = field - upwind(padded, field, courant_x, courant_y) - vertical(field, courant_z, mask)
        field = jnp.where(mask, adv + relax[None] * (boundary - adv), 0.0)
    flat_nest = field.reshape(levels, nest_cols)
    row_count = fb_index.shape[1]
    averaged = fb_index.shape[2]
    row_ids = lax.broadcasted_iota(jnp.int32, (row_count, averaged), 0)
    averaging = jnp.zeros((row_count + 1, nest_cols), jnp.float32)
    averaging = averaging.at[row_ids, fb_index[0]].add(1.0 / averaged)
    slot_weights = jnp.take(averaging, fb_slot[0], axis=0)
    chosen_rows = lax.dot_general(
        slot_weights,
        flat_nest,
        (((1,), (1,)), ((), ())),
        precision=lax.Precision.HIGHEST,
        preferred_element_type=jnp.float32,
    )
    sending = chosen_rows.reshape(devices, FCAP * levels)
    arrived = lax.all_to_all(sending, ("gx", "gy"), split_axis=0, concat_axis=0, tiled=True)
    values = arrived.reshape(-1, levels)
    flat_parent = advected.reshape(levels, parent_cols)
    target = fb_target[0]
    current = jnp.take(flat_parent, jnp.minimum(target, parent_cols - 1), axis=1)
    delta = blend_rate * (values.T - current)
    updated = flat_parent.at[:, target].add(delta, mode="drop")
    return (field, updated.reshape(levels, parent_x, parent_y))


MESH = pl.DeviceIdType.MESH
LEV = 96
NX = 16
PXN = 32
KREQ = 64
GROUPS = 8
F32 = jnp.float32
BF16 = jnp.bfloat16
NT = (((1,), (1,)), ((), ()))


def halves(value):
    high = value.astype(BF16)
    return high, (value - high.astype(F32)).astype(BF16)


def step_kernel(
    slots_ref,
    nest_ref,
    cx_ref,
    cy_ref,
    cz_ref,
    terrain_ref,
    relax_ref,
    index_ref,
    weight_ref,
    parent_ref,
    pcx_ref,
    pcy_ref,
    fbi_ref,
    fbs_ref,
    fbt_ref,
    nest_out,
    parent_out,
    flag_out,
    q0,
    q1,
    q2,
    ybuf,
    ypack,
    adv1,
    bound,
    pq,
    pys,
    pyk,
    keep,
    shi,
    slo,
    pos,
    racc,
    req,
    reqin,
    ans,
    ansin,
    xmat,
    counts,
    cmat,
    qmat,
    tmat,
    fbsend,
    fbin,
    run,
    sem_req_s,
    sem_req_r,
    sem_ans_s,
    sem_ans_r,
    sem_fb_s,
    sem_fb_r,
    hs,
    hr,
):
    gx = lax.axis_index("gx")
    gy = lax.axis_index("gy")
    mz, my, mx, mc = lax.div(gx, 4), lax.rem(gx, 4), lax.div(gy, 2), lax.rem(gy, 2)
    me = gx * 8 + gy

    def chip(n, sign):
        dz, dy, dx = lax.div(n, 16), lax.rem(lax.div(n, 4), 4), lax.rem(n, 4)
        if sign < 0:
            dz, dy, dx = 4 - dz, 4 - dy, 4 - dx
        z, y, x = lax.rem(mz + dz, 4), lax.rem(my + dy, 4), lax.rem(mx + dx, 4)
        return z * 4 + y, x * 2

    barrier = pltpu.get_barrier_semaphore()

    def greet(n, carry):
        tx, ty = chip(n, 1)
        for core in range(2):
            pl.semaphore_signal(barrier, inc=1, device_id=(tx, ty + core), device_id_type=MESH)
        return carry

    lax.fori_loop(1, 64, greet, 0)
    pl.semaphore_signal(barrier, inc=1, device_id=(gx, mx * 2 + 1 - mc), device_id_type=MESH)

    lane1 = lax.broadcasted_iota(jnp.int32, (1, 128), 1)
    sub128 = lax.broadcasted_iota(jnp.int32, (128, 128), 0)
    lane128 = lax.broadcasted_iota(jnp.int32, (128, 128), 1)
    sub64 = lax.broadcasted_iota(jnp.int32, (KREQ, 128), 0)

    before = jnp.concatenate(
        [jnp.where(sub128 < lane128, 1.0, 0.0), jnp.ones((128, 128), F32)], axis=1
    ).astype(BF16)
    run[...] = jnp.zeros_like(run)
    racc[...] = jnp.zeros_like(racc)

    def pack(x, top):
        idx = [index_ref[j, pl.ds(x, 1), :] for j in range(4)]
        src = idx[0] >> 8
        rel = (
            ((((src >> 5) - mz) & 3) << 5)
            | ((((src >> 3) & 3) - my) & 3) << 3
            | ((((src >> 1) & 3) - mx) & 3) << 1
            | (src & 1)
        )
        hot = jnp.where(sub128 == rel, 1.0, 0.0)
        hotb = hot.astype(BF16)
        both = jnp.dot(hotb, before, preferred_element_type=F32)
        rank = jnp.sum(hot * (both[:, :128] + run[...]), axis=0, keepdims=True)
        run[...] += both[:, 128:]
        ranki = rank.astype(jnp.int32)
        pos[pl.ds(x, 1), :] = rel * KREQ + ranki
        here = sub64 == ranki
        firsts, seconds = [], []
        for j in range(4):
            low = (idx[j] & 255).astype(F32)
            w = weight_ref[j, pl.ds(x, 1), :]
            whi = w.astype(BF16).astype(F32)
            firsts.append(jnp.where(here, low, 0.0))
            firsts.append(jnp.where(here, whi, 0.0))
            seconds.append(jnp.zeros((KREQ, 128), F32))
            seconds.append(jnp.where(here, w - whi, 0.0))
        table = jnp.concatenate(firsts + seconds, axis=0).astype(BF16)
        racc[...] += lax.dot_general(hotb, table, NT, preferred_element_type=F32)
        return jnp.maximum(top, rank)

    top = lax.fori_loop(0, NX, pack, jnp.zeros((1, 128), F32))
    flag = jnp.max(jnp.where(top >= KREQ, 1.0, 0.0), axis=1, keepdims=True)
    for j in range(4):
        req[:, j, :] = (
            racc[:, 128 * j : 128 * j + 128] + racc[:, 512 + 128 * j : 640 + 128 * j]
        )

    pl.semaphore_wait(barrier, 127)

    def ask(n, carry):
        tx, ty = chip(n, 1)
        for core in range(2):
            pltpu.make_async_remote_copy(
                src_ref=req.at[2 * n + core],
                dst_ref=reqin.at[2 * n + mc],
                send_sem=sem_req_s,
                recv_sem=sem_req_r,
                device_id=(tx, ty + core),
                device_id_type=MESH,
            ).start()
        return carry

    lax.fori_loop(1, 64, ask, 0)
    pltpu.make_async_remote_copy(
        src_ref=req.at[1 - mc],
        dst_ref=reqin.at[mc],
        send_sem=sem_req_s,
        recv_sem=sem_req_r,
        device_id=(gx, mx * 2 + 1 - mc),
        device_id_type=MESH,
    ).start()
    pltpu.make_async_copy(req.at[mc], reqin.at[mc], sem_req_r).start()

    lev = lax.broadcasted_iota(jnp.int32, (LEV, 128), 0)
    lane = lax.broadcasted_iota(jnp.int32, (LEV, 128), 1)

    def edge_copies(field, count, packed, landing, at):
        west = (gx > 0, field.at[1], field.at[count + 1], (gx - 1, gy))
        east = (gx < 15, field.at[count], field.at[0], (gx + 1, gy))
        south = (gy > 0, packed.at[0], landing.at[1], (gx, gy - 1))
        north = (gy < 7, packed.at[1], landing.at[0], (gx, gy + 1))
        made = []
        for k, (has, src, dst, target) in enumerate((west, east, south, north)):
            made.append(
                (
                    has,
                    pltpu.make_async_remote_copy(
                        src_ref=src,
                        dst_ref=dst,
                        send_sem=hs.at[at, k],
                        recv_sem=hr.at[at, k],
                        device_id=target,
                        device_id_type=MESH,
                    ),
                )
            )
        return made

    def edges_start(made):
        for has, copy in made:
            pl.when(has)(copy.start)

    def edges_wait(made):
        for k, other in ((0, 1), (1, 0), (2, 3), (3, 2)):
            pl.when(made[other][0])(made[k][1].wait_recv)

    def edges_sent(made):
        for has, copy in made:
            pl.when(has)(copy.wait_send)

    def clear_edges(field, count, landing):
        zero = jnp.zeros((LEV, 128), F32)

        @pl.when(gx == 0)
        def _():
            field[0] = zero

        @pl.when(gx == 15)
        def _():
            field[count + 1] = zero

        @pl.when(gy == 0)
        def _():
            landing[0] = zero

        @pl.when(gy == 7)
        def _():
            landing[1] = zero

    def pack_edges(field, count, packed):
        def one(x, carry):
            low, high = carry
            here = field[x + 1]
            low = jnp.where(lane == x, pltpu.roll(here, x, 1), low)
            high = jnp.where(lane == x, pltpu.roll(here, x + 1, 1), high)
            return low, high

        zero = jnp.zeros((LEV, 128), F32)
        low, high = lax.fori_loop(0, count, one, (zero, zero))
        packed[0] = low
        packed[1] = high

    def sides(field, x, landing):
        here = field[x + 1]
        south = jnp.where(
            lane == 0, pltpu.roll(landing[0], lax.rem(128 - x, 128), 1), pltpu.roll(here, 1, 1)
        )
        north = jnp.where(
            lane == 127, pltpu.roll(landing[1], 127 - x, 1), pltpu.roll(here, 127, 1)
        )
        return here, field[x], field[x + 2], south, north

    def across(field, x, landing, cx, cy):
        here, west, east, south, north = sides(field, x, landing)
        return here - cx * jnp.where(cx > 0, here - west, east - here) - cy * jnp.where(
            cy > 0, here - south, north - here
        )

    clear_edges(pq, PXN, pys)
    clear_edges(q0, NX, ybuf.at[0])
    clear_edges(q1, NX, ybuf.at[1])
    clear_edges(q2, NX, ybuf.at[2])

    def load_nest(x, carry):
        q0[x + 1] = jnp.where(lev >= terrain_ref[pl.ds(x, 1), :], nest_ref[:, x, :], 0.0)
        return carry

    for x in range(NX):
        load_nest(x, 0)
    pack_edges(q0, NX, ypack.at[0])
    q0_edges = edge_copies(q0, NX, ypack.at[0], ybuf.at[0], 0)
    edges_start(q0_edges)

    for x in range(PXN):
        value = parent_ref[:, x, :]
        pq[x + 1] = value
        shi[x], slo[x] = halves(value)
    shi[PXN] = jnp.zeros((LEV, 128), BF16)
    slo[PXN] = jnp.zeros((LEV, 128), BF16)
    pack_edges(pq, PXN, pyk)
    p_edges = edge_copies(pq, PXN, pyk, pys, 1)
    edges_start(p_edges)

    pltpu.make_async_copy(reqin, reqin, sem_req_r).wait()
    sub256 = lax.broadcasted_iota(jnp.int32, (256, 128), 0)
    left48 = lax.broadcasted_iota(jnp.int32, (48, 128), 1) < 64
    left4 = lax.broadcasted_iota(jnp.int32, (4, 128), 1) < 64

    def answer(n, tx, ty):
        a, b = reqin[2 * n], reqin[2 * n + 1]
        place = jnp.where(left4, a, pltpu.roll(b, 64, 1)).astype(jnp.int32)
        amount = jnp.where(left4, pltpu.roll(a, 64, 1), b)
        table = jnp.zeros((256, 128), F32)
        for j in range(4):
            table = jnp.where(sub256 == place[j : j + 1], amount[j : j + 1], table)
        right = jnp.concatenate(halves(table), axis=1)
        base = (tx * 8 + ty) * 2
        rows = []
        for core in range(2):
            first, second = slots_ref[base + 2 * core], slots_ref[base + 2 * core + 1]
            rows.append(jnp.concatenate([shi[first], shi[second]], axis=1))
            rows.append(jnp.concatenate([slo[first], slo[second]], axis=1))
        out = jnp.dot(jnp.concatenate(rows, axis=0), right, preferred_element_type=F32)
        v0 = out[0:96, :128] + out[0:96, 128:] + out[96:192, :128]
        v1 = out[192:288, :128] + out[192:288, 128:] + out[288:384, :128]
        ans[2 * n] = jnp.where(left48, v0[:48], pltpu.roll(v0[48:], 64, 1))
        ans[2 * n + 1] = jnp.where(left48, pltpu.roll(v1[:48], 64, 1), v1[48:])

    def reply(n, carry):
        tx, ty = chip(n, -1)
        answer(n, tx, ty)
        for core in range(2):
            pltpu.make_async_remote_copy(
                src_ref=ans.at[2 * n + core],
                dst_ref=ansin.at[2 * n + mc],
                send_sem=sem_ans_s,
                recv_sem=sem_ans_r.at[lax.div(n, 64 // GROUPS)],
                device_id=(tx, ty + core),
                device_id_type=MESH,
            ).start()
        return carry

    answer(0, gx, mx * 2)
    pltpu.make_async_remote_copy(
        src_ref=ans.at[1 - mc],
        dst_ref=ansin.at[mc],
        send_sem=sem_ans_s,
        recv_sem=sem_ans_r.at[0],
        device_id=(gx, mx * 2 + 1 - mc),
        device_id_type=MESH,
    ).start()
    pltpu.make_async_copy(ans.at[mc], ansin.at[mc], sem_ans_r.at[0]).start()
    lax.fori_loop(1, 64, reply, 0)

    edges_wait(q0_edges)

    for x in range(NX):
        here = q0[x + 1]
        terrain = terrain_ref[pl.ds(x, 1), :]
        cz = cz_ref[:, x, :]
        below = jnp.where(lev - 1 >= terrain, pltpu.roll(here, 1, 0), here)
        above = jnp.where(lev == LEV - 1, here, pltpu.roll(here, LEV - 1, 0))
        adv1[x] = across(q0, x, ybuf.at[0], cx_ref[:, x, :], cy_ref[:, x, :]) - cz * jnp.where(
            cz > 0, here - below, above - here
        )
        bound[x] = jnp.zeros((LEV, 128), F32)

    edges_wait(p_edges)
    sub512 = lax.broadcasted_iota(jnp.int32, (128, 512), 0)
    target = fbt_ref[...]
    for x in range(PXN):
        hot = jnp.where(sub512 == target - 128 * x, 1.0, 0.0).astype(BF16)
        tmat[x] = hot
        hits = lax.dot_general(jnp.ones((8, 512), BF16), hot, NT, preferred_element_type=F32)
        moved = across(pq, x, pys, pcx_ref[:, x, :], pcy_ref[:, x, :])
        keep[x] = moved * (1.0 - 0.5 * hits[0:1])

    sub16 = lax.broadcasted_iota(jnp.int32, (16, 128), 0)

    def count(r, carry):
        highs, lows = [], []
        for k in range(2):
            row = fbi_ref[pl.ds(2 * r + k, 1), :]
            high = jnp.where(sub16 == (row >> 7), 1.0, 0.0).astype(BF16)
            blank = jnp.zeros((16, 128), BF16)
            highs.append(jnp.concatenate([high, blank] if k == 0 else [blank, high], axis=1))
            lows.append(jnp.where(sub128 == (row & 127), 1.0, 0.0).astype(BF16))
        got = lax.dot_general(
            jnp.concatenate(highs, axis=0),
            jnp.concatenate(lows, axis=1),
            NT,
            preferred_element_type=F32,
        )
        counts[2 * r] = got[:16]
        counts[2 * r + 1] = got[16:]
        return carry

    lax.fori_loop(0, 128, count, 0)
    row256 = lax.broadcasted_iota(jnp.int32, (256, 512), 0)
    chosen = jnp.transpose(jnp.where(row256 == fbs_ref[...], 1.0, 0.0)).astype(BF16)
    for x in range(NX):
        cmat[:, 128 * x : 128 * x + 128] = jnp.dot(
            chosen, counts[:, x, :].astype(BF16), preferred_element_type=F32
        ).astype(BF16)
    qmat[...] = jnp.zeros_like(qmat)

    per = 64 // GROUPS
    wide = per * 128
    subw = lax.broadcasted_iota(jnp.int32, (wide, 128), 0)
    for g in range(GROUPS):
        part = ansin.at[pl.ds(2 * per * g, 2 * per)]
        pltpu.make_async_copy(part, part, sem_ans_r.at[g]).wait()
        for i in range(per):
            a, b = ansin[2 * (per * g + i)], ansin[2 * (per * g + i) + 1]
            upper = jnp.where(left48, a, pltpu.roll(b, 64, 1))
            lower = jnp.where(left48, pltpu.roll(a, 64, 1), b)
            high, low = halves(jnp.concatenate([upper, lower], axis=0))
            xmat[0:96, 128 * i : 128 * i + 128] = high
            xmat[96:192, 128 * i : 128 * i + 128] = low

        def pick(x, carry, g=g):
            hots = [
                jnp.where(subw == pos[pl.ds(2 * x + k, 1), :] - wide * g, 1.0, 0.0).astype(BF16)
                for k in range(2)
            ]
            got = jnp.dot(xmat[...], jnp.concatenate(hots, axis=1), preferred_element_type=F32)
            bound[2 * x] += got[:96, :128] + got[96:, :128]
            bound[2 * x + 1] += got[:96, 128:] + got[96:, 128:]
            return carry

        lax.fori_loop(0, NX // 2, pick, 0)

    def settle(x, adv):
        terrain = terrain_ref[pl.ds(x, 1), :]
        rel = relax_ref[pl.ds(x, 1), :]
        return jnp.where(lev >= terrain, adv + rel * (bound[x] - adv), 0.0)

    for x in range(NX):
        q1[x + 1] = settle(x, adv1[x])
    edges = [q0_edges, p_edges]
    for step, (now, later) in enumerate(((q1, q2), (q2, None))):
        pack_edges(now, NX, ypack.at[step + 1])
        made = edge_copies(now, NX, ypack.at[step + 1], ybuf.at[step + 1], step + 2)
        edges_start(made)
        edges.append(made)
        edges_wait(made)
        for x in range(NX):
            here = now[x + 1]
            terrain = terrain_ref[pl.ds(x, 1), :]
            cz = cz_ref[:, x, :]
            below = jnp.where(lev - 1 >= terrain, pltpu.roll(here, 1, 0), here)
            above = jnp.where(lev == LEV - 1, here, pltpu.roll(here, LEV - 1, 0))
            adv = across(
                now, x, ybuf.at[step + 1], cx_ref[:, x, :], cy_ref[:, x, :]
            ) - cz * jnp.where(cz > 0, here - below, above - here)
            value = settle(x, adv)
            if later is not None:
                later[x + 1] = value
            else:
                nest_out[:, x, :] = value
                high, low = halves(value)
                qmat[0:96, 128 * x : 128 * x + 128] = high
                qmat[128:224, 128 * x : 128 * x + 128] = low

    got = lax.dot_general(cmat[...], qmat[...], NT, preferred_element_type=F32)
    rows = (got[:, :128] + got[:, 128:]) * (1.0 / 81.0)
    lane512 = lax.broadcasted_iota(jnp.int32, (512, 128), 1)
    rows = jnp.where(lane512 == LEV, flag, rows)
    fbsend[...] = rows.reshape(128, 4, 128)

    def feed(n, carry):
        tx, ty = chip(n, 1)
        for core in range(2):
            pltpu.make_async_remote_copy(
                src_ref=fbsend.at[tx * 8 + ty + core],
                dst_ref=fbin.at[me],
                send_sem=sem_fb_s,
                recv_sem=sem_fb_r,
                device_id=(tx, ty + core),
                device_id_type=MESH,
            ).start()
        return carry

    lax.fori_loop(1, 64, feed, 0)
    other = mx * 2 + 1 - mc
    pltpu.make_async_remote_copy(
        src_ref=fbsend.at[gx * 8 + other],
        dst_ref=fbin.at[me],
        send_sem=sem_fb_s,
        recv_sem=sem_fb_r,
        device_id=(gx, other),
        device_id_type=MESH,
    ).start()
    pltpu.make_async_copy(fbsend.at[me], fbin.at[me], sem_fb_r).start()
    pltpu.make_async_copy(fbin, fbin, sem_fb_r).wait()

    values = fbin[...].reshape(512, 128)
    flag_out[...] = jnp.broadcast_to(jnp.max(values, axis=0, keepdims=True), (8, 128))
    high, low = halves(jnp.transpose(values)[:96])
    both = jnp.concatenate([high, low], axis=0)
    for x in range(PXN):
        got = lax.dot_general(both, tmat[x], NT, preferred_element_type=F32)
        parent_out[:, x, :] = keep[x] + 0.5 * (got[:96] + got[96:])

    for buffer, sem in ((req, sem_req_s), (ans, sem_ans_s), (fbsend, sem_fb_s)):
        part = buffer.at[pl.ds(0, 127)]
        pltpu.make_async_copy(part, part, sem).wait()
    for made in edges:
        edges_sent(made)


def fused_step(
    nest_field,
    courant_x,
    courant_y,
    courant_z,
    terrain,
    relax,
    interp_index,
    interp_weight,
    send_slots,
    parent_field,
    parent_cx,
    parent_cy,
    fb_index,
    fb_slot,
    fb_target,
):
    vmem = pl.BlockSpec(memory_space=pltpu.VMEM)
    smem = pl.BlockSpec(memory_space=pltpu.SMEM)
    padded = jnp.pad(fb_index[0], ((0, 0), (0, 128 - fb_index.shape[2])), constant_values=-1)
    slab = (LEV, 128)
    scratch = [
        pltpu.VMEM((NX + 2,) + slab, F32),
        pltpu.VMEM((NX + 2,) + slab, F32),
        pltpu.VMEM((NX + 2,) + slab, F32),
        pltpu.VMEM((3, 2) + slab, F32),
        pltpu.VMEM((3, 2) + slab, F32),
        pltpu.VMEM((NX,) + slab, F32),
        pltpu.VMEM((NX,) + slab, F32),
        pltpu.VMEM((PXN + 2,) + slab, F32),
        pltpu.VMEM((2,) + slab, F32),
        pltpu.VMEM((2,) + slab, F32),
        pltpu.VMEM((PXN,) + slab, F32),
        pltpu.VMEM((PXN + 1,) + slab, BF16),
        pltpu.VMEM((PXN + 1,) + slab, BF16),
        pltpu.VMEM((NX, 128), jnp.int32),
        pltpu.VMEM((128, 1024), F32),
        pltpu.VMEM((128, 4, 128), F32),
        pltpu.VMEM((128, 4, 128), F32),
        pltpu.VMEM((128, 48, 128), F32),
        pltpu.VMEM((128, 48, 128), F32),
        pltpu.VMEM((192, 64 // GROUPS * 128), BF16),
        pltpu.VMEM((256, NX, 128), F32),
        pltpu.VMEM((512, NX * 128), BF16),
        pltpu.VMEM((256, NX * 128), BF16),
        pltpu.VMEM((PXN, 128, 512), BF16),
        pltpu.VMEM((128, 4, 128), F32),
        pltpu.VMEM((128, 4, 128), F32),
        pltpu.VMEM((128, 128), F32),
        pltpu.SemaphoreType.DMA,
        pltpu.SemaphoreType.DMA,
        pltpu.SemaphoreType.DMA,
        pltpu.SemaphoreType.DMA((GROUPS,)),
        pltpu.SemaphoreType.DMA,
        pltpu.SemaphoreType.DMA,
        pltpu.SemaphoreType.DMA((4, 4)),
        pltpu.SemaphoreType.DMA((4, 4)),
    ]
    return pl.pallas_call(
        step_kernel,
        out_shape=(
            jax.ShapeDtypeStruct(nest_field.shape, F32),
            jax.ShapeDtypeStruct(parent_field.shape, F32),
            jax.ShapeDtypeStruct((8, 128), F32),
        ),
        in_specs=[smem] + [vmem] * 14,
        out_specs=(vmem, vmem, vmem),
        scratch_shapes=scratch,
        compiler_params=pltpu.CompilerParams(
            collective_id=0, has_side_effects=True, vmem_limit_bytes=56 * 2**20
        ),
        name="step",
    )(
        send_slots[0],
        nest_field,
        courant_x,
        courant_y,
        courant_z,
        terrain,
        relax,
        interp_index,
        interp_weight,
        parent_field,
        parent_cx,
        parent_cy,
        padded,
        fb_slot,
        fb_target,
    )


def on_device(*args):
    nest_out, parent_out, flags = fused_step(*args)
    return lax.cond(
        flags[0, LEV] > 0.5, lambda: dense_step(*args), lambda: (nest_out, parent_out)
    )


def solution(mesh):
    in_specs = (
        P(None, "gx", "gy"),
        P(None, "gx", "gy"),
        P(None, "gx", "gy"),
        P(None, "gx", "gy"),
        P("gx", "gy"),
        P("gx", "gy"),
        P(None, "gx", "gy"),
        P(None, "gx", "gy"),
        P(("gx", "gy"), None),
        P(None, "gx", "gy"),
        P(None, "gx", "gy"),
        P(None, "gx", "gy"),
        P(("gx", "gy"), None, None),
        P(("gx", "gy"), None),
        P(("gx", "gy"), None),
    )
    out_specs = (P(None, "gx", "gy"), P(None, "gx", "gy"))
    return jax.shard_map(
        on_device, mesh=mesh, in_specs=in_specs, out_specs=out_specs, check_vma=False
    )
```

```python
import functools

import jax
import jax.numpy as jnp
from jax import lax
from jax.experimental import pallas as pl
from jax.experimental.pallas import tpu as pltpu
from jax.sharding import PartitionSpec as P

TILE = 128
CAP = 2
FCAP = 4
SUBSTEPS = 3


blend_rate = 0.5


def extended(block, sides, width):
    for axis, dim in sides:
        count = lax.axis_size(axis)
        forward = [(i, i + 1) for i in range(count - 1)]
        backward = [(target, source) for source, target in forward]
        low = lax.ppermute(
            lax.slice_in_dim(block, block.shape[dim] - width, None, axis=dim), axis, forward
        )
        high = lax.ppermute(lax.slice_in_dim(block, 0, width, axis=dim), axis, backward)
        block = jnp.concatenate([low, block, high], axis=dim)
    return block


def upwind(padded, field, cx, cy):
    west = padded[:, :-2, 1:-1]
    east = padded[:, 2:, 1:-1]
    south = padded[:, 1:-1, :-2]
    north = padded[:, 1:-1, 2:]
    return cx * jnp.where(cx > 0, field - west, east - field) + cy * jnp.where(
        cy > 0, field - south, north - field
    )


def vertical(field, cz, mask):
    below = jnp.concatenate([field[:1], field[:-1]], axis=0)
    mask_below = jnp.concatenate([jnp.zeros_like(mask[:1]), mask[:-1]], axis=0)
    below = jnp.where(mask_below, below, field)
    above = jnp.concatenate([field[1:], field[-1:]], axis=0)
    return cz * jnp.where(cz > 0, field - below, above - field)


def dense_step(
    nest_field,
    courant_x,
    courant_y,
    courant_z,
    terrain,
    relax,
    interp_index,
    interp_weight,
    send_slots,
    parent_field,
    parent_cx,
    parent_cy,
    fb_index,
    fb_slot,
    fb_target,
):
    n_east = lax.axis_size("gx")
    n_north = lax.axis_size("gy")
    devices = n_east * n_north
    levels, nest_x, nest_y = nest_field.shape
    parent_x, parent_y = (parent_field.shape[1], parent_field.shape[2])
    parent_cols = parent_x * parent_y
    nest_cols = nest_x * nest_y
    slabs = parent_field
    slabs = jnp.concatenate([slabs, jnp.zeros((levels, 1, TILE), jnp.float32)], axis=1)
    picked = jnp.take(slabs, send_slots[0], axis=1)
    outgoing = picked.reshape(levels, devices, CAP, TILE)
    incoming = lax.all_to_all(outgoing, ("gx", "gy"), split_axis=1, concat_axis=1, tiled=True)
    received_cols = incoming.reshape(levels, -1).T
    padded_parent = extended(parent_field, (("gx", 1), ("gy", 2)), 1)
    advected = parent_field - upwind(padded_parent, parent_field, parent_cx, parent_cy)
    index_flat = interp_index.reshape(4, -1)
    weight_flat = interp_weight.reshape(4, -1)
    boundary_cols = weight_flat[0][:, None] * jnp.take(received_cols, index_flat[0], axis=0)
    for j in range(1, 4):
        boundary_cols = boundary_cols + weight_flat[j][:, None] * jnp.take(
            received_cols, index_flat[j], axis=0
        )
    boundary = boundary_cols.T.reshape(levels, nest_x, nest_y)
    level_ids = lax.broadcasted_iota(jnp.int32, (levels, 1, 1), 0)
    mask = level_ids >= terrain[None]
    field = jnp.where(mask, nest_field, 0.0)
    for step in range(SUBSTEPS):
        padded = extended(field, (("gx", 1), ("gy", 2)), 1)
        adv = field - upwind(padded, field, courant_x, courant_y) - vertical(field, courant_z, mask)
        field = jnp.where(mask, adv + relax[None] * (boundary - adv), 0.0)
    flat_nest = field.reshape(levels, nest_cols)
    row_count = fb_index.shape[1]
    averaged = fb_index.shape[2]
    row_ids = lax.broadcasted_iota(jnp.int32, (row_count, averaged), 0)
    averaging = jnp.zeros((row_count + 1, nest_cols), jnp.float32)
    averaging = averaging.at[row_ids, fb_index[0]].add(1.0 / averaged)
    slot_weights = jnp.take(averaging, fb_slot[0], axis=0)
    chosen_rows = lax.dot_general(
        slot_weights,
        flat_nest,
        (((1,), (1,)), ((), ())),
        precision=lax.Precision.HIGHEST,
        preferred_element_type=jnp.float32,
    )
    sending = chosen_rows.reshape(devices, FCAP * levels)
    arrived = lax.all_to_all(sending, ("gx", "gy"), split_axis=0, concat_axis=0, tiled=True)
    values = arrived.reshape(-1, levels)
    flat_parent = advected.reshape(levels, parent_cols)
    target = fb_target[0]
    current = jnp.take(flat_parent, jnp.minimum(target, parent_cols - 1), axis=1)
    delta = blend_rate * (values.T - current)
    updated = flat_parent.at[:, target].add(delta, mode="drop")
    return (field, updated.reshape(levels, parent_x, parent_y))


MESH = pl.DeviceIdType.MESH
LEV = 96
NX = 16
PXN = 32
KREQ = 64
GROUPS = 8
F32 = jnp.float32
BF16 = jnp.bfloat16
NT = (((1,), (1,)), ((), ()))


def halves(value):
    high = value.astype(BF16)
    return high, (value - high.astype(F32)).astype(BF16)


def step_kernel(
    slots_ref,
    nest_ref,
    cx_ref,
    cy_ref,
    cz_ref,
    terrain_ref,
    relax_ref,
    index_ref,
    weight_ref,
    parent_ref,
    pcx_ref,
    pcy_ref,
    fbi_ref,
    fbs_ref,
    fbt_ref,
    nest_out,
    parent_out,
    flag_out,
    q0,
    q1,
    q2,
    ybuf,
    ypack,
    adv1,
    bound,
    pq,
    pys,
    pyk,
    keep,
    shi,
    slo,
    req,
    reqin,
    ans,
    ansin,
    xmat,
    counts,
    cmat,
    qmat,
    tmat,
    fbsend,
    fbin,
    hotm,
    tabm,
    rankm,
    relm,
    nraw,
    cxs,
    cys,
    czs,
    pcxs,
    pcys,
    nres,
    fbt,
    fbn,
    sem_in,
    sem_out,
    sem_req_s,
    sem_req_r,
    sem_ans_s,
    sem_ans_r,
    sem_fb_s,
    sem_fb_r,
    hs,
    hr,
):
    gx = lax.axis_index("gx")
    gy = lax.axis_index("gy")
    mz, my, mx, mc = lax.div(gx, 4), lax.rem(gx, 4), lax.div(gy, 2), lax.rem(gy, 2)
    me = gx * 8 + gy

    def chip(n, sign):
        dx = lax.rem(n, 4)
        dy = lax.rem(lax.div(n, 4) + dx, 4)
        dz = lax.rem(lax.div(n, 16) + dy, 4)
        if sign < 0:
            dz, dy, dx = 4 - dz, 4 - dy, 4 - dx
        z, y, x = lax.rem(mz + dz, 4), lax.rem(my + dy, 4), lax.rem(mx + dx, 4)
        return z * 4 + y, x * 2

    barrier = pltpu.get_barrier_semaphore()

    def greet(n, carry):
        tx, ty = chip(n, 1)
        for core in range(2):
            pl.semaphore_signal(barrier, inc=1, device_id=(tx, ty + core), device_id_type=MESH)
        return carry

    lax.fori_loop(1, 64, greet, 0)
    pl.semaphore_signal(barrier, inc=1, device_id=(gx, mx * 2 + 1 - mc), device_id_type=MESH)

    def load(source, count, target, first, k):
        def one(x, carry):
            pltpu.make_async_copy(source.at[:, x], target.at[x + first], sem_in.at[k]).start()
            return carry

        lax.fori_loop(0, count, one, 0)

    def loaded(target, first, count, k):
        part = target.at[pl.ds(first, count)]
        pltpu.make_async_copy(part, part, sem_in.at[k]).wait()

    sub128 = lax.broadcasted_iota(jnp.int32, (128, 128), 0)
    lane128 = lax.broadcasted_iota(jnp.int32, (128, 128), 1)
    sub64 = lax.broadcasted_iota(jnp.int32, (KREQ, 128), 0)

    before = jnp.concatenate(
        [jnp.where(sub128 < lane128, 1.0, 0.0), jnp.ones((128, 128), F32)], axis=1
    ).astype(BF16)
    run = jnp.zeros((128, 128), F32)
    top = jnp.zeros((1, 128), F32)
    for x in range(NX):
        idx = [index_ref[j, x : x + 1, :] for j in range(4)]
        src = idx[0] >> 8
        dz, dy, dx = (src >> 5) - mz, ((src >> 3) & 3) - my, ((src >> 1) & 3) - mx
        rel = (((dz - dy) & 3) << 5) | (((dy - dx) & 3) << 3) | ((dx & 3) << 1) | (src & 1)
        relm[x : x + 1, :] = rel
        hot = jnp.where(sub128 == rel, 1.0, 0.0)
        hotb = hot.astype(BF16)
        both = jnp.dot(hotb, before, preferred_element_type=F32)
        rank = jnp.sum(hot * (both[:, :128] + run), axis=0, keepdims=True)
        run = run + both[:, 128:]
        top = jnp.maximum(top, rank)
        here = sub64 == rank.astype(jnp.int32)
        rankm[x] = jnp.where(here, 1.0, 0.0).astype(BF16)
        at = slice(128 * x, 128 * x + 128)
        hotm[:, at] = hotb
        for j in range(4):
            low = (idx[j] & 255).astype(F32)
            w = weight_ref[j, x : x + 1, :]
            whi = w.astype(BF16).astype(F32)
            tabm[128 * j : 128 * j + 64, at] = jnp.where(here, low, 0.0).astype(BF16)
            tabm[128 * j + 64 : 128 * j + 128, at] = jnp.where(here, whi, 0.0).astype(BF16)
            tabm[512 + 128 * j : 576 + 128 * j, at] = jnp.zeros((KREQ, 128), BF16)
            tabm[576 + 128 * j : 640 + 128 * j, at] = jnp.where(here, w - whi, 0.0).astype(BF16)
    flag = jnp.max(jnp.where(top >= KREQ, 1.0, 0.0), axis=1, keepdims=True)
    racc = lax.dot_general(hotm[...], tabm[...], NT, preferred_element_type=F32)
    for j in range(4):
        req[:, j, :] = (
            racc[:, 128 * j : 128 * j + 128] + racc[:, 512 + 128 * j : 640 + 128 * j]
        )

    load(parent_ref, PXN, pq, 1, 0)
    load(nest_ref, NX, nraw, 0, 1)
    pl.semaphore_wait(barrier, 127)

    def ask(n, carry):
        tx, ty = chip(n, 1)
        for core in range(2):
            pltpu.make_async_remote_copy(
                src_ref=req.at[2 * n + core],
                dst_ref=reqin.at[2 * n + mc],
                send_sem=sem_req_s,
                recv_sem=sem_req_r.at[lax.div(n, 64 // GROUPS)],
                device_id=(tx, ty + core),
                device_id_type=MESH,
            ).start()
        return carry

    lax.fori_loop(1, 64, ask, 0)
    pltpu.make_async_remote_copy(
        src_ref=req.at[1 - mc],
        dst_ref=reqin.at[mc],
        send_sem=sem_req_s,
        recv_sem=sem_req_r.at[0],
        device_id=(gx, mx * 2 + 1 - mc),
        device_id_type=MESH,
    ).start()
    pltpu.make_async_copy(req.at[mc], reqin.at[mc], sem_req_r.at[0]).start()

    load(cx_ref, NX, cxs, 0, 2)
    load(cy_ref, NX, cys, 0, 3)
    load(cz_ref, NX, czs, 0, 4)
    load(pcx_ref, PXN, pcxs, 0, 5)
    load(pcy_ref, PXN, pcys, 0, 6)

    lev = lax.broadcasted_iota(jnp.int32, (LEV, 128), 0)
    lane = lax.broadcasted_iota(jnp.int32, (LEV, 128), 1)

    def edge_copies(field, count, packed, landing, at):
        def face(x):
            return field.at[x, pl.ds(8, LEV)] if count == NX else field.at[x]

        west = (gx > 0, face(1), face(count + 1), (gx - 1, gy))
        east = (gx < 15, face(count), face(0), (gx + 1, gy))
        south = (gy > 0, packed.at[0], landing.at[1], (gx, gy - 1))
        north = (gy < 7, packed.at[1], landing.at[0], (gx, gy + 1))
        made = []
        for k, (has, src, dst, target) in enumerate((west, east, south, north)):
            made.append(
                (
                    has,
                    pltpu.make_async_remote_copy(
                        src_ref=src,
                        dst_ref=dst,
                        send_sem=hs.at[at, k],
                        recv_sem=hr.at[at, k],
                        device_id=target,
                        device_id_type=MESH,
                    ),
                )
            )
        return made

    def edges_start(made):
        for has, copy in made:
            pl.when(has)(copy.start)

    def edges_wait(made):
        for k, other in ((0, 1), (1, 0), (2, 3), (3, 2)):
            pl.when(made[other][0])(made[k][1].wait_recv)

    def edges_sent(made):
        for has, copy in made:
            pl.when(has)(copy.wait_send)

    def clear_edges(field, count, landing):
        zero = jnp.zeros((LEV, 128), F32)

        @pl.when(gx == 0)
        def _():
            field[0, pl.ds(8 if count == NX else 0, LEV), :] = zero

        @pl.when(gx == 15)
        def _():
            field[count + 1, pl.ds(8 if count == NX else 0, LEV), :] = zero

        @pl.when(gy == 0)
        def _():
            landing[0] = zero

        @pl.when(gy == 7)
        def _():
            landing[1] = zero

    def pack_edges(field, count, packed):
        base = 8 if count == NX else 0

        def one(x, carry):
            low, high = carry
            here = field[x + 1, pl.ds(base, LEV), :]
            low = jnp.where(lane == x, pltpu.roll(here, x, 1), low)
            high = jnp.where(lane == x, pltpu.roll(here, x + 1, 1), high)
            return low, high

        zero = jnp.zeros((LEV, 128), F32)
        low, high = lax.fori_loop(0, count, one, (zero, zero), unroll=4)
        packed[0] = low
        packed[1] = high

    deep = 32
    lanec = lax.broadcasted_iota(jnp.int32, (deep, 128), 1)
    levc = lax.broadcasted_iota(jnp.int32, (deep, 128), 0)

    def across(field, base, x, l0, landing, cx, cy):
        rows = pl.ds(base + l0, deep)
        here = field[x + 1, rows, :]
        west, east = field[x, rows, :], field[x + 2, rows, :]
        edge = pl.ds(l0, deep)
        south = jnp.where(
            lanec == 0,
            pltpu.roll(landing[0, edge, :], lax.rem(128 - x, 128), 1),
            pltpu.roll(here, 1, 1),
        )
        north = jnp.where(
            lanec == 127, pltpu.roll(landing[1, edge, :], 127 - x, 1), pltpu.roll(here, 127, 1)
        )
        return here, here - cx * jnp.where(cx > 0, here - west, east - here) - cy * jnp.where(
            cy > 0, here - south, north - here
        )

    def advance(field, x, l0, landing):
        edge = pl.ds(l0, deep)
        here, adv = across(field, 8, x, l0, landing, cxs[x, edge, :], cys[x, edge, :])
        cz = czs[x, edge, :]
        lower, upper = field[x + 1, pl.ds(7 + l0, deep), :], field[x + 1, pl.ds(9 + l0, deep), :]
        below = jnp.where(levc + (l0 - 1) >= terrain_ref[pl.ds(x, 1), :], lower, here)
        above = jnp.where(levc == LEV - 1 - l0, here, upper)
        return adv - cz * jnp.where(cz > 0, here - below, above - here)

    clear_edges(pq, PXN, pys)
    clear_edges(q0, NX, ybuf.at[0])
    clear_edges(q1, NX, ybuf.at[1])
    clear_edges(q2, NX, ybuf.at[2])

    blank8 = jnp.zeros((8, 128), F32)
    loaded(nraw, 0, NX, 1)

    def start_nest(x, carry):
        for field in (q0, q1, q2):
            field[x + 1, 0:8, :] = blank8
            field[x + 1, LEV + 8 : LEV + 16, :] = blank8
        q0[x + 1, 8 : LEV + 8, :] = jnp.where(lev >= terrain_ref[pl.ds(x, 1), :], nraw[x], 0.0)
        return carry

    lax.fori_loop(0, NX, start_nest, 0)
    pack_edges(q0, NX, ypack.at[0])
    q0_edges = edge_copies(q0, NX, ypack.at[0], ybuf.at[0], 0)
    edges_start(q0_edges)

    loaded(pq, 1, PXN, 0)

    def split(x, carry):
        shi[x], slo[x] = halves(pq[x + 1])
        return carry

    lax.fori_loop(0, PXN, split, 0, unroll=2)
    shi[PXN] = jnp.zeros((LEV, 128), BF16)
    slo[PXN] = jnp.zeros((LEV, 128), BF16)
    pack_edges(pq, PXN, pyk)
    p_edges = edge_copies(pq, PXN, pyk, pys, 1)
    edges_start(p_edges)


    def asked(g):
        part = reqin.at[pl.ds(g * (128 // GROUPS), 128 // GROUPS)]
        pltpu.make_async_copy(part, part, sem_req_r.at[g]).wait()

    sub256 = lax.broadcasted_iota(jnp.int32, (256, 128), 0)
    left48 = lax.broadcasted_iota(jnp.int32, (48, 128), 1) < 64
    left4 = lax.broadcasted_iota(jnp.int32, (4, 128), 1) < 64

    def answer(n, tx, ty):
        a, b = reqin[2 * n], reqin[2 * n + 1]
        place = jnp.where(left4, a, pltpu.roll(b, 64, 1)).astype(jnp.int32)
        amount = jnp.where(left4, pltpu.roll(a, 64, 1), b)
        table = jnp.zeros((256, 128), F32)
        for j in range(4):
            table = jnp.where(sub256 == place[j : j + 1], amount[j : j + 1], table)
        right = jnp.concatenate(halves(table), axis=1)
        base = (tx * 8 + ty) * 2
        rows = []
        for core in range(2):
            first, second = slots_ref[base + 2 * core], slots_ref[base + 2 * core + 1]
            rows.append(jnp.concatenate([shi[first], shi[second]], axis=1))
            rows.append(jnp.concatenate([slo[first], slo[second]], axis=1))
        out = jnp.dot(jnp.concatenate(rows, axis=0), right, preferred_element_type=F32)
        v0 = out[0:96, :128] + out[0:96, 128:] + out[96:192, :128]
        v1 = out[192:288, :128] + out[192:288, 128:] + out[288:384, :128]
        return (
            jnp.where(left48, v0[:48], pltpu.roll(v0[48:], 64, 1)),
            jnp.where(left48, pltpu.roll(v1[:48], 64, 1), v1[48:]),
        )

    def reply(base, count):
        places = [chip(base + u, -1) for u in range(count)]
        made = [answer(base + u, *places[u]) for u in range(count)]
        for u in range(count):
            ans[2 * (base + u)], ans[2 * (base + u) + 1] = made[u]
        for u in range(count):
            n = base + u
            tx, ty = places[u]
            for core in range(2):
                pltpu.make_async_remote_copy(
                    src_ref=ans.at[2 * n + core],
                    dst_ref=ansin.at[2 * n + mc],
                    send_sem=sem_ans_s,
                    recv_sem=sem_ans_r.at[lax.div(n, 64 // GROUPS)],
                    device_id=(tx, ty + core),
                    device_id_type=MESH,
                ).start()

    def replies(r, carry):
        asked(r)
        reply(8 * r, 4)
        reply(8 * r + 4, 4)
        return carry

    asked(0)
    ans[0], ans[1] = answer(0, gx, mx * 2)
    pltpu.make_async_remote_copy(
        src_ref=ans.at[1 - mc],
        dst_ref=ansin.at[mc],
        send_sem=sem_ans_s,
        recv_sem=sem_ans_r.at[0],
        device_id=(gx, mx * 2 + 1 - mc),
        device_id_type=MESH,
    ).start()
    pltpu.make_async_copy(ans.at[mc], ansin.at[mc], sem_ans_r.at[0]).start()
    reply(jnp.int32(1), 3)
    reply(jnp.int32(4), 4)
    lax.fori_loop(1, GROUPS, replies, 0)

    for k, (target, count) in enumerate(
        ((cxs, NX), (cys, NX), (czs, NX), (pcxs, PXN), (pcys, PXN))
    ):
        loaded(target, 0, count, k + 2)
    edges_wait(q0_edges)
    chunks = range(0, LEV, deep)

    def first_nest(x, carry):
        for l0 in chunks:
            adv1[x, pl.ds(l0, deep), :] = advance(q0, x, l0, ybuf.at[0])
        bound[x] = jnp.zeros((LEV, 128), F32)
        return carry

    lax.fori_loop(0, NX, first_nest, 0)

    edges_wait(p_edges)
    sub512 = lax.broadcasted_iota(jnp.int32, (256, 512), 0)
    ones8 = jnp.ones((8, 512), BF16)

    def parents(i, carry):
        hot = jnp.where(sub512 == fbt_ref[...] - 256 * i, 1.0, 0.0).astype(BF16)
        tmat[i] = hot
        left = 1.0 - 0.5 * lax.dot_general(ones8, hot, NT, preferred_element_type=F32)[0:1]
        for k in range(2):
            x = 2 * i + k
            for l0 in chunks:
                edge = pl.ds(l0, deep)
                moved = across(pq, 0, x, l0, pys, pcxs[x, edge, :], pcys[x, edge, :])[1]
                keep[x, edge, :] = moved * left[:, 128 * k : 128 * k + 128]
        return carry

    lax.fori_loop(0, PXN // 2, parents, 0)

    sub16 = lax.broadcasted_iota(jnp.int32, (16, 128), 0)

    fbt[...] = jnp.full((128, 256), -1.0, F32)

    def turn(i, carry):
        fbt[pl.ds(i, 1), :] = fbi_ref[i].astype(F32)
        return carry

    lax.fori_loop(0, 81, turn, 0)
    fbn[...] = jnp.transpose(fbt[...]).astype(jnp.int32)

    def count(r, carry):
        made = []
        for u in range(8):
            highs, lows = [], []
            for k in range(2):
                row = fbn[pl.ds(16 * r + 2 * u + k, 1), :]
                high = jnp.where(sub16 == (row >> 7), 1.0, 0.0).astype(BF16)
                blank = jnp.zeros((16, 128), BF16)
                highs.append(jnp.concatenate([high, blank] if k == 0 else [blank, high], axis=1))
                lows.append(jnp.where(sub128 == (row & 127), 1.0, 0.0).astype(BF16))
            made.append(
                lax.dot_general(
                    jnp.concatenate(highs, axis=0),
                    jnp.concatenate(lows, axis=1),
                    NT,
                    preferred_element_type=F32,
                )
            )
        for u in range(8):
            counts[16 * r + 2 * u] = made[u][:16]
            counts[16 * r + 2 * u + 1] = made[u][16:]
        return carry

    lax.fori_loop(0, 16, count, 0)
    row256 = lax.broadcasted_iota(jnp.int32, (256, 512), 0)
    chosen = jnp.transpose(jnp.where(row256 == fbs_ref[...], 1.0, 0.0)).astype(BF16)
    for x in range(NX):
        cmat[:, 128 * x : 128 * x + 128] = jnp.dot(
            chosen, counts[:, x, :].astype(BF16), preferred_element_type=F32
        ).astype(BF16)
    qmat[...] = jnp.zeros_like(qmat)


    per = 64 // GROUPS
    for g in range(GROUPS):
        part = ansin.at[pl.ds(2 * per * g, 2 * per)]
        pltpu.make_async_copy(part, part, sem_ans_r.at[g]).wait()
        for i in range(per):
            a, b = ansin[2 * (per * g + i)], ansin[2 * (per * g + i) + 1]
            upper = jnp.where(left48, a, pltpu.roll(b, 64, 1))
            lower = jnp.where(left48, pltpu.roll(a, 64, 1), b)
            high, low = halves(jnp.concatenate([upper, lower], axis=0))
            xmat[0:96, 128 * i : 128 * i + 128] = high
            xmat[96:192, 128 * i : 128 * i + 128] = low

        def pick(x, carry, g=g):
            hots = []
            for k in range(2):
                owner = jnp.broadcast_to(relm[pl.ds(2 * x + k, 1), :], (16, 128))
                ranks = rankm[2 * x + k]
                blocks = []
                for i in range(2 * per):
                    mine = jnp.where(owner == 2 * per * g + i, 1.0, 0.0).astype(BF16)
                    blocks.append(ranks * jnp.concatenate([mine] * (KREQ // 16), axis=0))
                hots.append(jnp.concatenate(blocks, axis=0))
            got = jnp.dot(xmat[...], jnp.concatenate(hots, axis=1), preferred_element_type=F32)
            bound[2 * x] += got[:96, :128] + got[96:, :128]
            bound[2 * x + 1] += got[:96, 128:] + got[96:, 128:]
            return carry

        lax.fori_loop(0, NX // 2, pick, 0)

    def settle(x, l0, adv):
        terrain = terrain_ref[pl.ds(x, 1), :]
        rel = relax_ref[pl.ds(x, 1), :]
        pull = bound[x, pl.ds(l0, deep), :] - adv
        return jnp.where(levc + l0 >= terrain, adv + rel * pull, 0.0)

    def first_settle(x, carry):
        for l0 in chunks:
            q1[x + 1, pl.ds(8 + l0, deep), :] = settle(x, l0, adv1[x, pl.ds(l0, deep), :])
        return carry

    lax.fori_loop(0, NX, first_settle, 0)
    edges = [q0_edges, p_edges]

    def exchange(now, step):
        pack_edges(now, NX, ypack.at[step])
        made = edge_copies(now, NX, ypack.at[step], ybuf.at[step], step + 1)
        edges_start(made)
        edges_wait(made)
        edges.append(made)

    exchange(q1, 1)

    def second(x, carry):
        for l0 in chunks:
            q2[x + 1, pl.ds(8 + l0, deep), :] = settle(x, l0, advance(q1, x, l0, ybuf.at[1]))
        return carry

    lax.fori_loop(0, NX, second, 0)
    exchange(q2, 2)

    def third(x, carry):
        at = pl.ds(pl.multiple_of(128 * x, 128), 128)
        for l0 in chunks:
            value = settle(x, l0, advance(q2, x, l0, ybuf.at[2]))
            nres[x, pl.ds(l0, deep), :] = value
            high, low = halves(value)
            qmat[pl.ds(l0, deep), at] = high
            qmat[pl.ds(128 + l0, deep), at] = low
        return carry

    lax.fori_loop(0, NX, third, 0)

    got = lax.dot_general(cmat[...], qmat[...], NT, preferred_element_type=F32)
    rows = (got[:, :128] + got[:, 128:]) * (1.0 / 81.0)
    lane512 = lax.broadcasted_iota(jnp.int32, (512, 128), 1)
    rows = jnp.where(lane512 == LEV, flag, rows)
    fbsend[...] = rows.reshape(128, 4, 128)

    def feed(n, carry):
        tx, ty = chip(n, 1)
        for core in range(2):
            pltpu.make_async_remote_copy(
                src_ref=fbsend.at[tx * 8 + ty + core],
                dst_ref=fbin.at[me],
                send_sem=sem_fb_s,
                recv_sem=sem_fb_r,
                device_id=(tx, ty + core),
                device_id_type=MESH,
            ).start()
        return carry

    lax.fori_loop(1, 64, feed, 0)
    other = mx * 2 + 1 - mc
    pltpu.make_async_remote_copy(
        src_ref=fbsend.at[gx * 8 + other],
        dst_ref=fbin.at[me],
        send_sem=sem_fb_s,
        recv_sem=sem_fb_r,
        device_id=(gx, other),
        device_id_type=MESH,
    ).start()
    pltpu.make_async_copy(fbsend.at[me], fbin.at[me], sem_fb_r).start()

    def store_nest(x, carry):
        pltpu.make_async_copy(nres.at[x], nest_out.at[:, x], sem_out.at[0]).start()
        return carry

    lax.fori_loop(0, NX, store_nest, 0)
    pltpu.make_async_copy(fbin, fbin, sem_fb_r).wait()


    values = fbin[...].reshape(512, 128)
    high, low = halves(jnp.transpose(values)[:96])
    both = jnp.concatenate([high, low], axis=0)
    for i in range(PXN // 2):
        got = lax.dot_general(both, tmat[i], NT, preferred_element_type=F32)
        for k in range(2):
            x, at = 2 * i + k, slice(128 * k, 128 * k + 128)
            keep[x] += 0.5 * (got[:96, at] + got[96:, at])
            pltpu.make_async_copy(keep.at[x], parent_out.at[:, x], sem_out.at[1]).start()
    worst = jnp.max(jnp.where(lane512 == LEV, values, 0.0))
    flag_out[0] = jnp.where(worst > 0.5, 1, 0)
    pltpu.make_async_copy(nres, nres, sem_out.at[0]).wait()
    pltpu.make_async_copy(keep, keep, sem_out.at[1]).wait()

    for buffer, sem in ((req, sem_req_s), (ans, sem_ans_s), (fbsend, sem_fb_s)):
        part = buffer.at[pl.ds(0, 127)]
        pltpu.make_async_copy(part, part, sem).wait()
    for made in edges:
        edges_sent(made)


def fused_step(
    nest_field,
    courant_x,
    courant_y,
    courant_z,
    terrain,
    relax,
    interp_index,
    interp_weight,
    send_slots,
    parent_field,
    parent_cx,
    parent_cy,
    fb_index,
    fb_slot,
    fb_target,
):
    vmem = pl.BlockSpec(memory_space=pltpu.VMEM)
    smem = pl.BlockSpec(memory_space=pltpu.SMEM)
    hbm = pl.BlockSpec(memory_space=pl.ANY)
    slab = (LEV, 128)
    scratch = [
        pltpu.VMEM((NX + 2, LEV + 16, 128), F32),
        pltpu.VMEM((NX + 2, LEV + 16, 128), F32),
        pltpu.VMEM((NX + 2, LEV + 16, 128), F32),
        pltpu.VMEM((3, 2) + slab, F32),
        pltpu.VMEM((3, 2) + slab, F32),
        pltpu.VMEM((NX,) + slab, F32),
        pltpu.VMEM((NX,) + slab, F32),
        pltpu.VMEM((PXN + 2,) + slab, F32),
        pltpu.VMEM((2,) + slab, F32),
        pltpu.VMEM((2,) + slab, F32),
        pltpu.VMEM((PXN,) + slab, F32),
        pltpu.VMEM((PXN + 1,) + slab, BF16),
        pltpu.VMEM((PXN + 1,) + slab, BF16),
        pltpu.VMEM((128, 4, 128), F32),
        pltpu.VMEM((128, 4, 128), F32),
        pltpu.VMEM((128, 48, 128), F32),
        pltpu.VMEM((128, 48, 128), F32),
        pltpu.VMEM((192, 64 // GROUPS * 128), BF16),
        pltpu.VMEM((256, NX, 128), F32),
        pltpu.VMEM((512, NX * 128), BF16),
        pltpu.VMEM((256, NX * 128), BF16),
        pltpu.VMEM((PXN // 2, 256, 512), BF16),
        pltpu.VMEM((128, 4, 128), F32),
        pltpu.VMEM((128, 4, 128), F32),
        pltpu.VMEM((128, NX * 128), BF16),
        pltpu.VMEM((1024, NX * 128), BF16),
        pltpu.VMEM((NX, KREQ, 128), BF16),
        pltpu.VMEM((NX, 128), jnp.int32),
        pltpu.VMEM((NX,) + slab, F32),
        pltpu.VMEM((NX,) + slab, F32),
        pltpu.VMEM((NX,) + slab, F32),
        pltpu.VMEM((NX,) + slab, F32),
        pltpu.VMEM((PXN,) + slab, F32),
        pltpu.VMEM((PXN,) + slab, F32),
        pltpu.VMEM((NX,) + slab, F32),
        pltpu.VMEM((128, 256), F32),
        pltpu.VMEM((256, 128), jnp.int32),
        pltpu.SemaphoreType.DMA((7,)),
        pltpu.SemaphoreType.DMA((2,)),
        pltpu.SemaphoreType.DMA,
        pltpu.SemaphoreType.DMA((GROUPS,)),
        pltpu.SemaphoreType.DMA,
        pltpu.SemaphoreType.DMA((GROUPS,)),
        pltpu.SemaphoreType.DMA,
        pltpu.SemaphoreType.DMA,
        pltpu.SemaphoreType.DMA((4, 4)),
        pltpu.SemaphoreType.DMA((4, 4)),
    ]
    return pl.pallas_call(
        step_kernel,
        out_shape=(
            jax.ShapeDtypeStruct(nest_field.shape, F32),
            jax.ShapeDtypeStruct(parent_field.shape, F32),
            jax.ShapeDtypeStruct((1,), jnp.int32),
        ),
        in_specs=[smem] + [hbm] * 4 + [vmem] * 4 + [hbm] * 3 + [vmem] * 3,
        out_specs=(hbm, hbm, smem),
        scratch_shapes=scratch,
        compiler_params=pltpu.CompilerParams(
            collective_id=0, has_side_effects=True, vmem_limit_bytes=56 * 2**20
        ),
        name="step",
    )(
        send_slots[0],
        nest_field,
        courant_x,
        courant_y,
        courant_z,
        terrain,
        relax,
        interp_index,
        interp_weight,
        parent_field,
        parent_cx,
        parent_cy,
        jnp.transpose(fb_index, (2, 0, 1)),
        fb_slot,
        fb_target,
    )


def on_device(*args):
    nest_out, parent_out, flags = fused_step(*args)
    return lax.cond(
        flags[0] > 0, lambda: dense_step(*args), lambda: (nest_out, parent_out)
    )


def solution(mesh):
    in_specs = (
        P(None, "gx", "gy"),
        P(None, "gx", "gy"),
        P(None, "gx", "gy"),
        P(None, "gx", "gy"),
        P("gx", "gy"),
        P("gx", "gy"),
        P(None, "gx", "gy"),
        P(None, "gx", "gy"),
        P(("gx", "gy"), None),
        P(None, "gx", "gy"),
        P(None, "gx", "gy"),
        P(None, "gx", "gy"),
        P(("gx", "gy"), None, None),
        P(("gx", "gy"), None),
        P(("gx", "gy"), None),
    )
    out_specs = (P(None, "gx", "gy"), P(None, "gx", "gy"))
    return jax.shard_map(
        on_device, mesh=mesh, in_specs=in_specs, out_specs=out_specs, check_vma=False
    )
```

```python
import functools

import jax
import jax.numpy as jnp
from jax import lax
from jax.experimental import pallas as pl
from jax.experimental.pallas import tpu as pltpu
from jax.sharding import PartitionSpec as P

TILE = 128
CAP = 2
FCAP = 4
SUBSTEPS = 3


blend_rate = 0.5


def extended(block, sides, width):
    for axis, dim in sides:
        count = lax.axis_size(axis)
        forward = [(i, i + 1) for i in range(count - 1)]
        backward = [(target, source) for source, target in forward]
        low = lax.ppermute(
            lax.slice_in_dim(block, block.shape[dim] - width, None, axis=dim), axis, forward
        )
        high = lax.ppermute(lax.slice_in_dim(block, 0, width, axis=dim), axis, backward)
        block = jnp.concatenate([low, block, high], axis=dim)
    return block


def upwind(padded, field, cx, cy):
    west = padded[:, :-2, 1:-1]
    east = padded[:, 2:, 1:-1]
    south = padded[:, 1:-1, :-2]
    north = padded[:, 1:-1, 2:]
    return cx * jnp.where(cx > 0, field - west, east - field) + cy * jnp.where(
        cy > 0, field - south, north - field
    )


def vertical(field, cz, mask):
    below = jnp.concatenate([field[:1], field[:-1]], axis=0)
    mask_below = jnp.concatenate([jnp.zeros_like(mask[:1]), mask[:-1]], axis=0)
    below = jnp.where(mask_below, below, field)
    above = jnp.concatenate([field[1:], field[-1:]], axis=0)
    return cz * jnp.where(cz > 0, field - below, above - field)


def dense_step(
    nest_field,
    courant_x,
    courant_y,
    courant_z,
    terrain,
    relax,
    interp_index,
    interp_weight,
    send_slots,
    parent_field,
    parent_cx,
    parent_cy,
    fb_index,
    fb_slot,
    fb_target,
):
    n_east = lax.axis_size("gx")
    n_north = lax.axis_size("gy")
    devices = n_east * n_north
    levels, nest_x, nest_y = nest_field.shape
    parent_x, parent_y = (parent_field.shape[1], parent_field.shape[2])
    parent_cols = parent_x * parent_y
    nest_cols = nest_x * nest_y
    slabs = parent_field
    slabs = jnp.concatenate([slabs, jnp.zeros((levels, 1, TILE), jnp.float32)], axis=1)
    picked = jnp.take(slabs, send_slots[0], axis=1)
    outgoing = picked.reshape(levels, devices, CAP, TILE)
    incoming = lax.all_to_all(outgoing, ("gx", "gy"), split_axis=1, concat_axis=1, tiled=True)
    received_cols = incoming.reshape(levels, -1).T
    padded_parent = extended(parent_field, (("gx", 1), ("gy", 2)), 1)
    advected = parent_field - upwind(padded_parent, parent_field, parent_cx, parent_cy)
    index_flat = interp_index.reshape(4, -1)
    weight_flat = interp_weight.reshape(4, -1)
    boundary_cols = weight_flat[0][:, None] * jnp.take(received_cols, index_flat[0], axis=0)
    for j in range(1, 4):
        boundary_cols = boundary_cols + weight_flat[j][:, None] * jnp.take(
            received_cols, index_flat[j], axis=0
        )
    boundary = boundary_cols.T.reshape(levels, nest_x, nest_y)
    level_ids = lax.broadcasted_iota(jnp.int32, (levels, 1, 1), 0)
    mask = level_ids >= terrain[None]
    field = jnp.where(mask, nest_field, 0.0)
    for step in range(SUBSTEPS):
        padded = extended(field, (("gx", 1), ("gy", 2)), 1)
        adv = field - upwind(padded, field, courant_x, courant_y) - vertical(field, courant_z, mask)
        field = jnp.where(mask, adv + relax[None] * (boundary - adv), 0.0)
    flat_nest = field.reshape(levels, nest_cols)
    row_count = fb_index.shape[1]
    averaged = fb_index.shape[2]
    row_ids = lax.broadcasted_iota(jnp.int32, (row_count, averaged), 0)
    averaging = jnp.zeros((row_count + 1, nest_cols), jnp.float32)
    averaging = averaging.at[row_ids, fb_index[0]].add(1.0 / averaged)
    slot_weights = jnp.take(averaging, fb_slot[0], axis=0)
    chosen_rows = lax.dot_general(
        slot_weights,
        flat_nest,
        (((1,), (1,)), ((), ())),
        precision=lax.Precision.HIGHEST,
        preferred_element_type=jnp.float32,
    )
    sending = chosen_rows.reshape(devices, FCAP * levels)
    arrived = lax.all_to_all(sending, ("gx", "gy"), split_axis=0, concat_axis=0, tiled=True)
    values = arrived.reshape(-1, levels)
    flat_parent = advected.reshape(levels, parent_cols)
    target = fb_target[0]
    current = jnp.take(flat_parent, jnp.minimum(target, parent_cols - 1), axis=1)
    delta = blend_rate * (values.T - current)
    updated = flat_parent.at[:, target].add(delta, mode="drop")
    return (field, updated.reshape(levels, parent_x, parent_y))


MESH = pl.DeviceIdType.MESH
LEV = 96
NX = 16
PXN = 32
KREQ = 64
GROUPS = 8
F32 = jnp.float32
BF16 = jnp.bfloat16
NT = (((1,), (1,)), ((), ()))


def halves(value):
    high = value.astype(BF16)
    return high, (value - high.astype(F32)).astype(BF16)


def step_kernel(
    slots_ref,
    nest_ref,
    cx_ref,
    cy_ref,
    cz_ref,
    terrain_ref,
    relax_ref,
    index_ref,
    weight_ref,
    parent_ref,
    pcx_ref,
    pcy_ref,
    fbi_ref,
    fbs_ref,
    fbt_ref,
    nest_out,
    parent_out,
    flag_out,
    q0,
    q1,
    q2,
    ybuf,
    ypack,
    adv1,
    bound,
    pq,
    pys,
    pyk,
    keep,
    shi,
    slo,
    req,
    reqin,
    ans,
    ansin,
    xmat,
    counts,
    cmat,
    qmat,
    tmat,
    fbsend,
    fbin,
    hotm,
    tabm,
    rankm,
    relm,
    nraw,
    cxs,
    cys,
    czs,
    pcxs,
    pcys,
    nres,
    fbt,
    fbn,
    sem_in,
    sem_out,
    sem_req_s,
    sem_req_r,
    sem_ans_s,
    sem_ans_r,
    sem_fb_s,
    sem_fb_r,
    hs,
    hr,
):
    gx = lax.axis_index("gx")
    gy = lax.axis_index("gy")
    mz, my, mx, mc = lax.div(gx, 4), lax.rem(gx, 4), lax.div(gy, 2), lax.rem(gy, 2)
    me = gx * 8 + gy

    def chip(n, sign):
        dx = lax.rem(n, 4)
        dy = lax.rem(lax.div(n, 4) + dx, 4)
        dz = lax.rem(lax.div(n, 16) + dy, 4)
        if sign < 0:
            dz, dy, dx = 4 - dz, 4 - dy, 4 - dx
        z, y, x = lax.rem(mz + dz, 4), lax.rem(my + dy, 4), lax.rem(mx + dx, 4)
        return z * 4 + y, x * 2

    barrier = pltpu.get_barrier_semaphore()

    def greet(n, carry):
        tx, ty = chip(n, 1)
        for core in range(2):
            pl.semaphore_signal(barrier, inc=1, device_id=(tx, ty + core), device_id_type=MESH)
        return carry

    lax.fori_loop(1, 64, greet, 0)
    pl.semaphore_signal(barrier, inc=1, device_id=(gx, mx * 2 + 1 - mc), device_id_type=MESH)

    def load(source, count, target, first, k):
        def one(x, carry):
            pltpu.make_async_copy(source.at[:, x], target.at[x + first], sem_in.at[k]).start()
            return carry

        lax.fori_loop(0, count, one, 0)

    def loaded(target, first, count, k):
        part = target.at[pl.ds(first, count)]
        pltpu.make_async_copy(part, part, sem_in.at[k]).wait()

    sub128 = lax.broadcasted_iota(jnp.int32, (128, 128), 0)
    lane128 = lax.broadcasted_iota(jnp.int32, (128, 128), 1)
    sub64 = lax.broadcasted_iota(jnp.int32, (KREQ, 128), 0)

    before = jnp.concatenate(
        [jnp.where(sub128 < lane128, 1.0, 0.0), jnp.ones((128, 128), F32)], axis=1
    ).astype(BF16)
    run = jnp.zeros((128, 128), F32)
    top = jnp.zeros((1, 128), F32)
    for x in range(NX):
        idx = [index_ref[j, x : x + 1, :] for j in range(4)]
        src = idx[0] >> 8
        dz, dy, dx = (src >> 5) - mz, ((src >> 3) & 3) - my, ((src >> 1) & 3) - mx
        rel = (((dz - dy) & 3) << 5) | (((dy - dx) & 3) << 3) | ((dx & 3) << 1) | (src & 1)
        relm[x : x + 1, :] = rel
        hot = jnp.where(sub128 == rel, 1.0, 0.0)
        hotb = hot.astype(BF16)
        both = jnp.dot(hotb, before, preferred_element_type=F32)
        rank = jnp.sum(hot * (both[:, :128] + run), axis=0, keepdims=True)
        run = run + both[:, 128:]
        top = jnp.maximum(top, rank)
        here = sub64 == rank.astype(jnp.int32)
        rankm[x] = jnp.where(here, 1.0, 0.0).astype(BF16)
        at = slice(128 * x, 128 * x + 128)
        hotm[:, at] = hotb
        for j in range(4):
            low = (idx[j] & 255).astype(F32)
            w = weight_ref[j, x : x + 1, :]
            whi = w.astype(BF16).astype(F32)
            tabm[128 * j : 128 * j + 64, at] = jnp.where(here, low, 0.0).astype(BF16)
            tabm[128 * j + 64 : 128 * j + 128, at] = jnp.where(here, whi, 0.0).astype(BF16)
            tabm[512 + 128 * j : 576 + 128 * j, at] = jnp.zeros((KREQ, 128), BF16)
            tabm[576 + 128 * j : 640 + 128 * j, at] = jnp.where(here, w - whi, 0.0).astype(BF16)
    flag = jnp.max(jnp.where(top >= KREQ, 1.0, 0.0), axis=1, keepdims=True)
    racc = lax.dot_general(hotm[...], tabm[...], NT, preferred_element_type=F32)
    for j in range(4):
        req[:, j, :] = (
            racc[:, 128 * j : 128 * j + 128] + racc[:, 512 + 128 * j : 640 + 128 * j]
        )

    load(parent_ref, PXN, pq, 1, 0)
    load(nest_ref, NX, nraw, 0, 1)
    pl.semaphore_wait(barrier, 127)

    def ask(n, carry):
        tx, ty = chip(n, 1)
        for core in range(2):
            pltpu.make_async_remote_copy(
                src_ref=req.at[2 * n + core],
                dst_ref=reqin.at[2 * n + mc],
                send_sem=sem_req_s,
                recv_sem=sem_req_r.at[lax.div(n, 64 // GROUPS)],
                device_id=(tx, ty + core),
                device_id_type=MESH,
            ).start()
        return carry

    lax.fori_loop(1, 64, ask, 0)
    pltpu.make_async_remote_copy(
        src_ref=req.at[1 - mc],
        dst_ref=reqin.at[mc],
        send_sem=sem_req_s,
        recv_sem=sem_req_r.at[0],
        device_id=(gx, mx * 2 + 1 - mc),
        device_id_type=MESH,
    ).start()
    pltpu.make_async_copy(req.at[mc], reqin.at[mc], sem_req_r.at[0]).start()

    load(cx_ref, NX, cxs, 0, 2)
    load(cy_ref, NX, cys, 0, 3)
    load(cz_ref, NX, czs, 0, 4)
    load(pcx_ref, PXN, pcxs, 0, 5)
    load(pcy_ref, PXN, pcys, 0, 6)

    lev = lax.broadcasted_iota(jnp.int32, (LEV, 128), 0)
    lane = lax.broadcasted_iota(jnp.int32, (LEV, 128), 1)

    def edge_copies(field, count, packed, landing, at):
        def face(x):
            return field.at[x, pl.ds(8, LEV)] if count == NX else field.at[x]

        west = (gx > 0, face(1), face(count + 1), (gx - 1, gy))
        east = (gx < 15, face(count), face(0), (gx + 1, gy))
        south = (gy > 0, packed.at[0], landing.at[1], (gx, gy - 1))
        north = (gy < 7, packed.at[1], landing.at[0], (gx, gy + 1))
        made = []
        for k, (has, src, dst, target) in enumerate((west, east, south, north)):
            made.append(
                (
                    has,
                    pltpu.make_async_remote_copy(
                        src_ref=src,
                        dst_ref=dst,
                        send_sem=hs.at[at, k],
                        recv_sem=hr.at[at, k],
                        device_id=target,
                        device_id_type=MESH,
                    ),
                )
            )
        return made

    def edges_start(made):
        for has, copy in made:
            pl.when(has)(copy.start)

    def edges_wait(made):
        for k, other in ((0, 1), (1, 0), (2, 3), (3, 2)):
            pl.when(made[other][0])(made[k][1].wait_recv)

    def edges_sent(made):
        for has, copy in made:
            pl.when(has)(copy.wait_send)

    def clear_edges(field, count, landing):
        zero = jnp.zeros((LEV, 128), F32)

        @pl.when(gx == 0)
        def _():
            field[0, pl.ds(8 if count == NX else 0, LEV), :] = zero

        @pl.when(gx == 15)
        def _():
            field[count + 1, pl.ds(8 if count == NX else 0, LEV), :] = zero

        @pl.when(gy == 0)
        def _():
            landing[0] = zero

        @pl.when(gy == 7)
        def _():
            landing[1] = zero

    def pack_edges(field, count, packed):
        base = 8 if count == NX else 0

        def one(x, carry):
            low, high = carry
            here = field[x + 1, pl.ds(base, LEV), :]
            low = jnp.where(lane == x, pltpu.roll(here, x, 1), low)
            high = jnp.where(lane == x, pltpu.roll(here, x + 1, 1), high)
            return low, high

        zero = jnp.zeros((LEV, 128), F32)
        low, high = lax.fori_loop(0, count, one, (zero, zero), unroll=16)
        packed[0] = low
        packed[1] = high

    deep = 32
    lanec = lax.broadcasted_iota(jnp.int32, (deep, 128), 1)
    levc = lax.broadcasted_iota(jnp.int32, (deep, 128), 0)

    def across(field, base, x, l0, landing, cx, cy):
        rows = pl.ds(base + l0, deep)
        here = field[x + 1, rows, :]
        west, east = field[x, rows, :], field[x + 2, rows, :]
        edge = pl.ds(l0, deep)
        south = jnp.where(
            lanec == 0,
            pltpu.roll(landing[0, edge, :], lax.rem(128 - x, 128), 1),
            pltpu.roll(here, 1, 1),
        )
        north = jnp.where(
            lanec == 127, pltpu.roll(landing[1, edge, :], 127 - x, 1), pltpu.roll(here, 127, 1)
        )
        return here, here - cx * jnp.where(cx > 0, here - west, east - here) - cy * jnp.where(
            cy > 0, here - south, north - here
        )

    def advance(field, x, l0, landing):
        edge = pl.ds(l0, deep)
        here, adv = across(field, 8, x, l0, landing, cxs[x, edge, :], cys[x, edge, :])
        cz = czs[x, edge, :]
        lower, upper = field[x + 1, pl.ds(7 + l0, deep), :], field[x + 1, pl.ds(9 + l0, deep), :]
        below = jnp.where(levc + (l0 - 1) >= terrain_ref[pl.ds(x, 1), :], lower, here)
        above = jnp.where(levc == LEV - 1 - l0, here, upper)
        return adv - cz * jnp.where(cz > 0, here - below, above - here)

    clear_edges(pq, PXN, pys)
    clear_edges(q0, NX, ybuf.at[0])
    clear_edges(q1, NX, ybuf.at[1])
    clear_edges(q2, NX, ybuf.at[2])

    blank8 = jnp.zeros((8, 128), F32)
    loaded(nraw, 0, NX, 1)

    def start_nest(x, carry):
        for field in (q0, q1, q2):
            field[x + 1, 0:8, :] = blank8
            field[x + 1, LEV + 8 : LEV + 16, :] = blank8
        q0[x + 1, 8 : LEV + 8, :] = jnp.where(lev >= terrain_ref[pl.ds(x, 1), :], nraw[x], 0.0)
        return carry

    lax.fori_loop(0, NX, start_nest, 0)
    pack_edges(q0, NX, ypack.at[0])
    q0_edges = edge_copies(q0, NX, ypack.at[0], ybuf.at[0], 0)
    edges_start(q0_edges)

    loaded(pq, 1, PXN, 0)

    def split(x, carry):
        shi[x], slo[x] = halves(pq[x + 1])
        return carry

    lax.fori_loop(0, PXN, split, 0, unroll=2)
    shi[PXN] = jnp.zeros((LEV, 128), BF16)
    slo[PXN] = jnp.zeros((LEV, 128), BF16)
    pack_edges(pq, PXN, pyk)
    p_edges = edge_copies(pq, PXN, pyk, pys, 1)
    edges_start(p_edges)


    def asked(g):
        part = reqin.at[pl.ds(g * (128 // GROUPS), 128 // GROUPS)]
        pltpu.make_async_copy(part, part, sem_req_r.at[g]).wait()

    sub256 = lax.broadcasted_iota(jnp.int32, (256, 128), 0)
    left48 = lax.broadcasted_iota(jnp.int32, (48, 128), 1) < 64
    left4 = lax.broadcasted_iota(jnp.int32, (4, 128), 1) < 64

    def answer(n, tx, ty):
        a, b = reqin[2 * n], reqin[2 * n + 1]
        place = jnp.where(left4, a, pltpu.roll(b, 64, 1)).astype(jnp.int32)
        amount = jnp.where(left4, pltpu.roll(a, 64, 1), b)
        table = jnp.zeros((256, 128), F32)
        for j in range(4):
            table = jnp.where(sub256 == place[j : j + 1], amount[j : j + 1], table)
        right = jnp.concatenate(halves(table), axis=1)
        base = (tx * 8 + ty) * 2
        rows = []
        for core in range(2):
            first, second = slots_ref[base + 2 * core], slots_ref[base + 2 * core + 1]
            rows.append(jnp.concatenate([shi[first], shi[second]], axis=1))
            rows.append(jnp.concatenate([slo[first], slo[second]], axis=1))
        out = jnp.dot(jnp.concatenate(rows, axis=0), right, preferred_element_type=F32)
        v0 = out[0:96, :128] + out[0:96, 128:] + out[96:192, :128]
        v1 = out[192:288, :128] + out[192:288, 128:] + out[288:384, :128]
        return (
            jnp.where(left48, v0[:48], pltpu.roll(v0[48:], 64, 1)),
            jnp.where(left48, pltpu.roll(v1[:48], 64, 1), v1[48:]),
        )

    def reply(base, count):
        places = [chip(base + u, -1) for u in range(count)]
        made = [answer(base + u, *places[u]) for u in range(count)]
        for u in range(count):
            ans[2 * (base + u)], ans[2 * (base + u) + 1] = made[u]
        for u in range(count):
            n = base + u
            tx, ty = places[u]
            for core in range(2):
                pltpu.make_async_remote_copy(
                    src_ref=ans.at[2 * n + core],
                    dst_ref=ansin.at[2 * n + mc],
                    send_sem=sem_ans_s,
                    recv_sem=sem_ans_r.at[lax.div(n, 64 // GROUPS)],
                    device_id=(tx, ty + core),
                    device_id_type=MESH,
                ).start()

    def replies(r, carry):
        asked(r)
        reply(8 * r, 4)
        reply(8 * r + 4, 4)
        return carry

    asked(0)
    ans[0], ans[1] = answer(0, gx, mx * 2)
    pltpu.make_async_remote_copy(
        src_ref=ans.at[1 - mc],
        dst_ref=ansin.at[mc],
        send_sem=sem_ans_s,
        recv_sem=sem_ans_r.at[0],
        device_id=(gx, mx * 2 + 1 - mc),
        device_id_type=MESH,
    ).start()
    pltpu.make_async_copy(ans.at[mc], ansin.at[mc], sem_ans_r.at[0]).start()
    reply(jnp.int32(1), 3)
    reply(jnp.int32(4), 4)
    lax.fori_loop(1, GROUPS, replies, 0)

    for k, (target, count) in enumerate(
        ((cxs, NX), (cys, NX), (czs, NX), (pcxs, PXN), (pcys, PXN))
    ):
        loaded(target, 0, count, k + 2)
    edges_wait(q0_edges)
    chunks = range(0, LEV, deep)

    def first_nest(x, carry):
        for l0 in chunks:
            adv1[x, pl.ds(l0, deep), :] = advance(q0, x, l0, ybuf.at[0])
        bound[x] = jnp.zeros((LEV, 128), F32)
        return carry

    lax.fori_loop(0, NX, first_nest, 0)

    edges_wait(p_edges)
    sub512 = lax.broadcasted_iota(jnp.int32, (256, 512), 0)
    ones8 = jnp.ones((8, 512), BF16)

    def parents(i, carry):
        hot = jnp.where(sub512 == fbt_ref[...] - 256 * i, 1.0, 0.0).astype(BF16)
        tmat[i] = hot
        left = 1.0 - 0.5 * lax.dot_general(ones8, hot, NT, preferred_element_type=F32)[0:1]
        for k in range(2):
            x = 2 * i + k
            for l0 in chunks:
                edge = pl.ds(l0, deep)
                moved = across(pq, 0, x, l0, pys, pcxs[x, edge, :], pcys[x, edge, :])[1]
                keep[x, edge, :] = moved * left[:, 128 * k : 128 * k + 128]
        return carry

    lax.fori_loop(0, PXN // 2, parents, 0)

    sub16 = lax.broadcasted_iota(jnp.int32, (16, 128), 0)

    fbt[...] = jnp.full((128, 256), -1.0, F32)

    def turn(i, carry):
        fbt[pl.ds(i, 1), :] = fbi_ref[i].astype(F32)
        return carry

    lax.fori_loop(0, 81, turn, 0)
    fbn[...] = jnp.transpose(fbt[...]).astype(jnp.int32)

    def count(r, carry):
        made = []
        for u in range(8):
            highs, lows = [], []
            for k in range(2):
                row = fbn[pl.ds(16 * r + 2 * u + k, 1), :]
                high = jnp.where(sub16 == (row >> 7), 1.0, 0.0).astype(BF16)
                blank = jnp.zeros((16, 128), BF16)
                highs.append(jnp.concatenate([high, blank] if k == 0 else [blank, high], axis=1))
                lows.append(jnp.where(sub128 == (row & 127), 1.0, 0.0).astype(BF16))
            made.append(
                lax.dot_general(
                    jnp.concatenate(highs, axis=0),
                    jnp.concatenate(lows, axis=1),
                    NT,
                    preferred_element_type=F32,
                )
            )
        for u in range(8):
            counts[16 * r + 2 * u] = made[u][:16]
            counts[16 * r + 2 * u + 1] = made[u][16:]
        return carry

    lax.fori_loop(0, 16, count, 0)
    row256 = lax.broadcasted_iota(jnp.int32, (256, 512), 0)
    chosen = jnp.transpose(jnp.where(row256 == fbs_ref[...], 1.0, 0.0)).astype(BF16)
    for x in range(NX):
        cmat[:, 128 * x : 128 * x + 128] = jnp.dot(
            chosen, counts[:, x, :].astype(BF16), preferred_element_type=F32
        ).astype(BF16)
    qmat[...] = jnp.zeros_like(qmat)


    per = 64 // GROUPS
    for g in range(GROUPS):
        part = ansin.at[pl.ds(2 * per * g, 2 * per)]
        pltpu.make_async_copy(part, part, sem_ans_r.at[g]).wait()
        for i in range(per):
            a, b = ansin[2 * (per * g + i)], ansin[2 * (per * g + i) + 1]
            upper = jnp.where(left48, a, pltpu.roll(b, 64, 1))
            lower = jnp.where(left48, pltpu.roll(a, 64, 1), b)
            high, low = halves(jnp.concatenate([upper, lower], axis=0))
            xmat[0:96, 128 * i : 128 * i + 128] = high
            xmat[96:192, 128 * i : 128 * i + 128] = low

        def pick(x, carry, g=g):
            hots = []
            for k in range(2):
                owner = jnp.broadcast_to(relm[pl.ds(2 * x + k, 1), :], (16, 128))
                ranks = rankm[2 * x + k]
                blocks = []
                for i in range(2 * per):
                    mine = jnp.where(owner == 2 * per * g + i, 1.0, 0.0).astype(BF16)
                    blocks.append(ranks * jnp.concatenate([mine] * (KREQ // 16), axis=0))
                hots.append(jnp.concatenate(blocks, axis=0))
            got = jnp.dot(xmat[...], jnp.concatenate(hots, axis=1), preferred_element_type=F32)
            bound[2 * x] += got[:96, :128] + got[96:, :128]
            bound[2 * x + 1] += got[:96, 128:] + got[96:, 128:]
            return carry

        lax.fori_loop(0, NX // 2, pick, 0, unroll=2)

    def settle(x, l0, adv):
        terrain = terrain_ref[pl.ds(x, 1), :]
        rel = relax_ref[pl.ds(x, 1), :]
        pull = bound[x, pl.ds(l0, deep), :] - adv
        return jnp.where(levc + l0 >= terrain, adv + rel * pull, 0.0)

    def first_settle(x, carry):
        for l0 in chunks:
            q1[x + 1, pl.ds(8 + l0, deep), :] = settle(x, l0, adv1[x, pl.ds(l0, deep), :])
        return carry

    lax.fori_loop(0, NX, first_settle, 0)
    edges = [q0_edges, p_edges]

    def exchange(now, step):
        pack_edges(now, NX, ypack.at[step])
        made = edge_copies(now, NX, ypack.at[step], ybuf.at[step], step + 1)
        edges_start(made)
        edges_wait(made)
        edges.append(made)

    exchange(q1, 1)

    def second(x, carry):
        for l0 in chunks:
            q2[x + 1, pl.ds(8 + l0, deep), :] = settle(x, l0, advance(q1, x, l0, ybuf.at[1]))
        return carry

    lax.fori_loop(0, NX, second, 0, unroll=4)
    exchange(q2, 2)

    def third(x, carry):
        at = pl.ds(pl.multiple_of(128 * x, 128), 128)
        for l0 in chunks:
            value = settle(x, l0, advance(q2, x, l0, ybuf.at[2]))
            nres[x, pl.ds(l0, deep), :] = value
            high, low = halves(value)
            qmat[pl.ds(l0, deep), at] = high
            qmat[pl.ds(128 + l0, deep), at] = low
        return carry

    lax.fori_loop(0, NX, third, 0, unroll=4)

    got = lax.dot_general(cmat[...], qmat[...], NT, preferred_element_type=F32)
    rows = (got[:, :128] + got[:, 128:]) * (1.0 / 81.0)
    lane512 = lax.broadcasted_iota(jnp.int32, (512, 128), 1)
    rows = jnp.where(lane512 == LEV, flag, rows)
    fbsend[...] = rows.reshape(128, 4, 128)

    def feed(n, carry):
        tx, ty = chip(n, 1)
        for core in range(2):
            pltpu.make_async_remote_copy(
                src_ref=fbsend.at[tx * 8 + ty + core],
                dst_ref=fbin.at[me],
                send_sem=sem_fb_s,
                recv_sem=sem_fb_r,
                device_id=(tx, ty + core),
                device_id_type=MESH,
            ).start()
        return carry

    lax.fori_loop(1, 64, feed, 0)
    other = mx * 2 + 1 - mc
    pltpu.make_async_remote_copy(
        src_ref=fbsend.at[gx * 8 + other],
        dst_ref=fbin.at[me],
        send_sem=sem_fb_s,
        recv_sem=sem_fb_r,
        device_id=(gx, other),
        device_id_type=MESH,
    ).start()
    pltpu.make_async_copy(fbsend.at[me], fbin.at[me], sem_fb_r).start()

    def store_nest(x, carry):
        pltpu.make_async_copy(nres.at[x], nest_out.at[:, x], sem_out.at[0]).start()
        return carry

    lax.fori_loop(0, NX, store_nest, 0)
    pltpu.make_async_copy(fbin, fbin, sem_fb_r).wait()


    values = fbin[...].reshape(512, 128)
    high, low = halves(jnp.transpose(values)[:96])
    both = jnp.concatenate([high, low], axis=0)
    for i in range(PXN // 2):
        got = lax.dot_general(both, tmat[i], NT, preferred_element_type=F32)
        for k in range(2):
            x, at = 2 * i + k, slice(128 * k, 128 * k + 128)
            keep[x] += 0.5 * (got[:96, at] + got[96:, at])
            pltpu.make_async_copy(keep.at[x], parent_out.at[:, x], sem_out.at[1]).start()
    worst = jnp.max(jnp.where(lane512 == LEV, values, 0.0))
    flag_out[0] = jnp.where(worst > 0.5, 1, 0)
    pltpu.make_async_copy(nres, nres, sem_out.at[0]).wait()
    pltpu.make_async_copy(keep, keep, sem_out.at[1]).wait()

    for buffer, sem in ((req, sem_req_s), (ans, sem_ans_s), (fbsend, sem_fb_s)):
        part = buffer.at[pl.ds(0, 127)]
        pltpu.make_async_copy(part, part, sem).wait()
    for made in edges:
        edges_sent(made)


def fused_step(
    nest_field,
    courant_x,
    courant_y,
    courant_z,
    terrain,
    relax,
    interp_index,
    interp_weight,
    send_slots,
    parent_field,
    parent_cx,
    parent_cy,
    fb_index,
    fb_slot,
    fb_target,
):
    vmem = pl.BlockSpec(memory_space=pltpu.VMEM)
    smem = pl.BlockSpec(memory_space=pltpu.SMEM)
    hbm = pl.BlockSpec(memory_space=pl.ANY)
    slab = (LEV, 128)
    scratch = [
        pltpu.VMEM((NX + 2, LEV + 16, 128), F32),
        pltpu.VMEM((NX + 2, LEV + 16, 128), F32),
        pltpu.VMEM((NX + 2, LEV + 16, 128), F32),
        pltpu.VMEM((3, 2) + slab, F32),
        pltpu.VMEM((3, 2) + slab, F32),
        pltpu.VMEM((NX,) + slab, F32),
        pltpu.VMEM((NX,) + slab, F32),
        pltpu.VMEM((PXN + 2,) + slab, F32),
        pltpu.VMEM((2,) + slab, F32),
        pltpu.VMEM((2,) + slab, F32),
        pltpu.VMEM((PXN,) + slab, F32),
        pltpu.VMEM((PXN + 1,) + slab, BF16),
        pltpu.VMEM((PXN + 1,) + slab, BF16),
        pltpu.VMEM((128, 4, 128), F32),
        pltpu.VMEM((128, 4, 128), F32),
        pltpu.VMEM((128, 48, 128), F32),
        pltpu.VMEM((128, 48, 128), F32),
        pltpu.VMEM((192, 64 // GROUPS * 128), BF16),
        pltpu.VMEM((256, NX, 128), F32),
        pltpu.VMEM((512, NX * 128), BF16),
        pltpu.VMEM((256, NX * 128), BF16),
        pltpu.VMEM((PXN // 2, 256, 512), BF16),
        pltpu.VMEM((128, 4, 128), F32),
        pltpu.VMEM((128, 4, 128), F32),
        pltpu.VMEM((128, NX * 128), BF16),
        pltpu.VMEM((1024, NX * 128), BF16),
        pltpu.VMEM((NX, KREQ, 128), BF16),
        pltpu.VMEM((NX, 128), jnp.int32),
        pltpu.VMEM((NX,) + slab, F32),
        pltpu.VMEM((NX,) + slab, F32),
        pltpu.VMEM((NX,) + slab, F32),
        pltpu.VMEM((NX,) + slab, F32),
        pltpu.VMEM((PXN,) + slab, F32),
        pltpu.VMEM((PXN,) + slab, F32),
        pltpu.VMEM((NX,) + slab, F32),
        pltpu.VMEM((128, 256), F32),
        pltpu.VMEM((256, 128), jnp.int32),
        pltpu.SemaphoreType.DMA((7,)),
        pltpu.SemaphoreType.DMA((2,)),
        pltpu.SemaphoreType.DMA,
        pltpu.SemaphoreType.DMA((GROUPS,)),
        pltpu.SemaphoreType.DMA,
        pltpu.SemaphoreType.DMA((GROUPS,)),
        pltpu.SemaphoreType.DMA,
        pltpu.SemaphoreType.DMA,
        pltpu.SemaphoreType.DMA((4, 4)),
        pltpu.SemaphoreType.DMA((4, 4)),
    ]
    return pl.pallas_call(
        step_kernel,
        out_shape=(
            jax.ShapeDtypeStruct(nest_field.shape, F32),
            jax.ShapeDtypeStruct(parent_field.shape, F32),
            jax.ShapeDtypeStruct((1,), jnp.int32),
        ),
        in_specs=[smem] + [hbm] * 4 + [vmem] * 4 + [hbm] * 3 + [vmem] * 3,
        out_specs=(hbm, hbm, smem),
        scratch_shapes=scratch,
        compiler_params=pltpu.CompilerParams(
            collective_id=0, has_side_effects=True, vmem_limit_bytes=56 * 2**20
        ),
        name="step",
    )(
        send_slots[0],
        nest_field,
        courant_x,
        courant_y,
        courant_z,
        terrain,
        relax,
        interp_index,
        interp_weight,
        parent_field,
        parent_cx,
        parent_cy,
        jnp.transpose(fb_index, (2, 0, 1)),
        fb_slot,
        fb_target,
    )


def hand_over(nest_ref, parent_ref, nest_out, parent_out, sem):
    copies = []
    for k, (source, target) in enumerate(((nest_ref, nest_out), (parent_ref, parent_out))):
        for part in range(8):
            rows = pl.ds(12 * part, 12)
            copies.append(
                pltpu.make_async_copy(source.at[rows], target.at[rows], sem.at[k, part])
            )
    for copy in copies:
        copy.start()
    for copy in copies:
        copy.wait()


def handed(nest_out, parent_out):
    hbm = pl.BlockSpec(memory_space=pl.ANY)
    return pl.pallas_call(
        hand_over,
        out_shape=(
            jax.ShapeDtypeStruct(nest_out.shape, F32),
            jax.ShapeDtypeStruct(parent_out.shape, F32),
        ),
        in_specs=[hbm, hbm],
        out_specs=(hbm, hbm),
        scratch_shapes=[pltpu.SemaphoreType.DMA((2, 8))],
        name="hand_over",
    )(nest_out, parent_out)


def on_device(*args):
    nest_out, parent_out, flags = fused_step(*args)
    return lax.cond(
        flags[0] > 0, lambda: dense_step(*args), lambda: handed(nest_out, parent_out)
    )


def solution(mesh):
    in_specs = (
        P(None, "gx", "gy"),
        P(None, "gx", "gy"),
        P(None, "gx", "gy"),
        P(None, "gx", "gy"),
        P("gx", "gy"),
        P("gx", "gy"),
        P(None, "gx", "gy"),
        P(None, "gx", "gy"),
        P(("gx", "gy"), None),
        P(None, "gx", "gy"),
        P(None, "gx", "gy"),
        P(None, "gx", "gy"),
        P(("gx", "gy"), None, None),
        P(("gx", "gy"), None),
        P(("gx", "gy"), None),
    )
    out_specs = (P(None, "gx", "gy"), P(None, "gx", "gy"))
    return jax.shard_map(
        on_device, mesh=mesh, in_specs=in_specs, out_specs=out_specs, check_vma=False
    )
```

```python
import functools

import jax
import jax.numpy as jnp
from jax import lax
from jax.experimental import pallas as pl
from jax.experimental.pallas import tpu as pltpu
from jax.sharding import PartitionSpec as P

TILE = 128
CAP = 2
FCAP = 4
SUBSTEPS = 3


blend_rate = 0.5


def extended(block, sides, width):
    for axis, dim in sides:
        count = lax.axis_size(axis)
        forward = [(i, i + 1) for i in range(count - 1)]
        backward = [(target, source) for source, target in forward]
        low = lax.ppermute(
            lax.slice_in_dim(block, block.shape[dim] - width, None, axis=dim), axis, forward
        )
        high = lax.ppermute(lax.slice_in_dim(block, 0, width, axis=dim), axis, backward)
        block = jnp.concatenate([low, block, high], axis=dim)
    return block


def upwind(padded, field, cx, cy):
    west = padded[:, :-2, 1:-1]
    east = padded[:, 2:, 1:-1]
    south = padded[:, 1:-1, :-2]
    north = padded[:, 1:-1, 2:]
    return cx * jnp.where(cx > 0, field - west, east - field) + cy * jnp.where(
        cy > 0, field - south, north - field
    )


def vertical(field, cz, mask):
    below = jnp.concatenate([field[:1], field[:-1]], axis=0)
    mask_below = jnp.concatenate([jnp.zeros_like(mask[:1]), mask[:-1]], axis=0)
    below = jnp.where(mask_below, below, field)
    above = jnp.concatenate([field[1:], field[-1:]], axis=0)
    return cz * jnp.where(cz > 0, field - below, above - field)


def dense_step(
    nest_field,
    courant_x,
    courant_y,
    courant_z,
    terrain,
    relax,
    interp_index,
    interp_weight,
    send_slots,
    parent_field,
    parent_cx,
    parent_cy,
    fb_index,
    fb_slot,
    fb_target,
):
    n_east = lax.axis_size("gx")
    n_north = lax.axis_size("gy")
    devices = n_east * n_north
    levels, nest_x, nest_y = nest_field.shape
    parent_x, parent_y = (parent_field.shape[1], parent_field.shape[2])
    parent_cols = parent_x * parent_y
    nest_cols = nest_x * nest_y
    slabs = parent_field
    slabs = jnp.concatenate([slabs, jnp.zeros((levels, 1, TILE), jnp.float32)], axis=1)
    picked = jnp.take(slabs, send_slots[0], axis=1)
    outgoing = picked.reshape(levels, devices, CAP, TILE)
    incoming = lax.all_to_all(outgoing, ("gx", "gy"), split_axis=1, concat_axis=1, tiled=True)
    received_cols = incoming.reshape(levels, -1).T
    padded_parent = extended(parent_field, (("gx", 1), ("gy", 2)), 1)
    advected = parent_field - upwind(padded_parent, parent_field, parent_cx, parent_cy)
    index_flat = interp_index.reshape(4, -1)
    weight_flat = interp_weight.reshape(4, -1)
    boundary_cols = weight_flat[0][:, None] * jnp.take(received_cols, index_flat[0], axis=0)
    for j in range(1, 4):
        boundary_cols = boundary_cols + weight_flat[j][:, None] * jnp.take(
            received_cols, index_flat[j], axis=0
        )
    boundary = boundary_cols.T.reshape(levels, nest_x, nest_y)
    level_ids = lax.broadcasted_iota(jnp.int32, (levels, 1, 1), 0)
    mask = level_ids >= terrain[None]
    field = jnp.where(mask, nest_field, 0.0)
    for step in range(SUBSTEPS):
        padded = extended(field, (("gx", 1), ("gy", 2)), 1)
        adv = field - upwind(padded, field, courant_x, courant_y) - vertical(field, courant_z, mask)
        field = jnp.where(mask, adv + relax[None] * (boundary - adv), 0.0)
    flat_nest = field.reshape(levels, nest_cols)
    row_count = fb_index.shape[1]
    averaged = fb_index.shape[2]
    row_ids = lax.broadcasted_iota(jnp.int32, (row_count, averaged), 0)
    averaging = jnp.zeros((row_count + 1, nest_cols), jnp.float32)
    averaging = averaging.at[row_ids, fb_index[0]].add(1.0 / averaged)
    slot_weights = jnp.take(averaging, fb_slot[0], axis=0)
    chosen_rows = lax.dot_general(
        slot_weights,
        flat_nest,
        (((1,), (1,)), ((), ())),
        precision=lax.Precision.HIGHEST,
        preferred_element_type=jnp.float32,
    )
    sending = chosen_rows.reshape(devices, FCAP * levels)
    arrived = lax.all_to_all(sending, ("gx", "gy"), split_axis=0, concat_axis=0, tiled=True)
    values = arrived.reshape(-1, levels)
    flat_parent = advected.reshape(levels, parent_cols)
    target = fb_target[0]
    current = jnp.take(flat_parent, jnp.minimum(target, parent_cols - 1), axis=1)
    delta = blend_rate * (values.T - current)
    updated = flat_parent.at[:, target].add(delta, mode="drop")
    return (field, updated.reshape(levels, parent_x, parent_y))


MESH = pl.DeviceIdType.MESH
LEV = 96
NX = 16
PXN = 32
KREQ = 64
GROUPS = 8
F32 = jnp.float32
BF16 = jnp.bfloat16
NT = (((1,), (1,)), ((), ()))


def halves(value):
    high = value.astype(BF16)
    return high, (value - high.astype(F32)).astype(BF16)


def step_kernel(
    slots_ref,
    nest_ref,
    cx_ref,
    cy_ref,
    cz_ref,
    terrain_ref,
    relax_ref,
    index_ref,
    weight_ref,
    parent_ref,
    pcx_ref,
    pcy_ref,
    fbi_ref,
    fbs_ref,
    fbt_ref,
    nest_out,
    parent_out,
    flag_out,
    q0,
    q1,
    q2,
    ybuf,
    ypack,
    adv1,
    bound,
    pq,
    pys,
    pyk,
    keep,
    shi,
    slo,
    req,
    reqin,
    ans,
    ansin,
    xmat,
    counts,
    cmat,
    qmat,
    tmat,
    fbsend,
    fbin,
    hotm,
    tabm,
    rankm,
    relm,
    nraw,
    cxs,
    cys,
    czs,
    pcxs,
    pcys,
    nres,
    fbt,
    fbn,
    sem_in,
    sem_out,
    sem_req_s,
    sem_req_r,
    sem_ans_s,
    sem_ans_r,
    sem_fb_s,
    sem_fb_r,
    hs,
    hr,
):
    gx = lax.axis_index("gx")
    gy = lax.axis_index("gy")
    mz, my, mx, mc = lax.div(gx, 4), lax.rem(gx, 4), lax.div(gy, 2), lax.rem(gy, 2)
    me = gx * 8 + gy

    def chip(n, sign):
        dx = lax.rem(n, 4)
        dy = lax.rem(lax.div(n, 4) + dx, 4)
        dz = lax.rem(lax.div(n, 16) + dy, 4)
        if sign < 0:
            dz, dy, dx = 4 - dz, 4 - dy, 4 - dx
        z, y, x = lax.rem(mz + dz, 4), lax.rem(my + dy, 4), lax.rem(mx + dx, 4)
        return z * 4 + y, x * 2

    barrier = pltpu.get_barrier_semaphore()

    def greet(n, carry):
        tx, ty = chip(n, 1)
        for core in range(2):
            pl.semaphore_signal(barrier, inc=1, device_id=(tx, ty + core), device_id_type=MESH)
        return carry

    lax.fori_loop(1, 64, greet, 0)
    pl.semaphore_signal(barrier, inc=1, device_id=(gx, mx * 2 + 1 - mc), device_id_type=MESH)

    def load(source, count, target, first, k):
        def one(x, carry):
            pltpu.make_async_copy(source.at[:, x], target.at[x + first], sem_in.at[k]).start()
            return carry

        lax.fori_loop(0, count, one, 0)

    def loaded(target, first, count, k):
        part = target.at[pl.ds(first, count)]
        pltpu.make_async_copy(part, part, sem_in.at[k]).wait()

    sub128 = lax.broadcasted_iota(jnp.int32, (128, 128), 0)
    lane128 = lax.broadcasted_iota(jnp.int32, (128, 128), 1)
    sub64 = lax.broadcasted_iota(jnp.int32, (KREQ, 128), 0)

    before = jnp.concatenate(
        [jnp.where(sub128 < lane128, 1.0, 0.0), jnp.ones((128, 128), F32)], axis=1
    ).astype(BF16)
    run = jnp.zeros((128, 128), F32)
    top = jnp.zeros((1, 128), F32)
    for x in range(NX):
        idx = [index_ref[j, x : x + 1, :] for j in range(4)]
        src = idx[0] >> 8
        dz, dy, dx = (src >> 5) - mz, ((src >> 3) & 3) - my, ((src >> 1) & 3) - mx
        rel = (((dz - dy) & 3) << 5) | (((dy - dx) & 3) << 3) | ((dx & 3) << 1) | (src & 1)
        relm[x : x + 1, :] = rel
        hot = jnp.where(sub128 == rel, 1.0, 0.0)
        hotb = hot.astype(BF16)
        both = jnp.dot(hotb, before, preferred_element_type=F32)
        rank = jnp.sum(hot * (both[:, :128] + run), axis=0, keepdims=True)
        run = run + both[:, 128:]
        top = jnp.maximum(top, rank)
        here = sub64 == rank.astype(jnp.int32)
        rankm[x] = jnp.where(here, 1.0, 0.0).astype(BF16)
        at = slice(128 * x, 128 * x + 128)
        hotm[:, at] = hotb
        for j in range(4):
            low = (idx[j] & 255).astype(F32)
            w = weight_ref[j, x : x + 1, :]
            whi = w.astype(BF16).astype(F32)
            tabm[128 * j : 128 * j + 64, at] = jnp.where(here, low, 0.0).astype(BF16)
            tabm[128 * j + 64 : 128 * j + 128, at] = jnp.where(here, whi, 0.0).astype(BF16)
            tabm[512 + 128 * j : 576 + 128 * j, at] = jnp.zeros((KREQ, 128), BF16)
            tabm[576 + 128 * j : 640 + 128 * j, at] = jnp.where(here, w - whi, 0.0).astype(BF16)
    flag = jnp.max(jnp.where(top >= KREQ, 1.0, 0.0), axis=1, keepdims=True)
    racc = lax.dot_general(hotm[...], tabm[...], NT, preferred_element_type=F32)
    for j in range(4):
        req[:, j, :] = (
            racc[:, 128 * j : 128 * j + 128] + racc[:, 512 + 128 * j : 640 + 128 * j]
        )

    load(parent_ref, PXN, pq, 1, 0)
    load(nest_ref, NX, nraw, 0, 1)
    pl.semaphore_wait(barrier, 127)

    def ask(n, carry):
        tx, ty = chip(n, 1)
        for core in range(2):
            pltpu.make_async_remote_copy(
                src_ref=req.at[2 * n + core],
                dst_ref=reqin.at[2 * n + mc],
                send_sem=sem_req_s,
                recv_sem=sem_req_r.at[lax.div(n, 64 // GROUPS)],
                device_id=(tx, ty + core),
                device_id_type=MESH,
            ).start()
        return carry

    lax.fori_loop(1, 64, ask, 0)
    pltpu.make_async_remote_copy(
        src_ref=req.at[1 - mc],
        dst_ref=reqin.at[mc],
        send_sem=sem_req_s,
        recv_sem=sem_req_r.at[0],
        device_id=(gx, mx * 2 + 1 - mc),
        device_id_type=MESH,
    ).start()
    pltpu.make_async_copy(req.at[mc], reqin.at[mc], sem_req_r.at[0]).start()


    lev = lax.broadcasted_iota(jnp.int32, (LEV, 128), 0)
    lane = lax.broadcasted_iota(jnp.int32, (LEV, 128), 1)

    def edge_copies(field, count, packed, landing, at):
        def face(x):
            return field.at[x, pl.ds(8, LEV)] if count == NX else field.at[x]

        west = (gx > 0, face(1), face(count + 1), (gx - 1, gy))
        east = (gx < 15, face(count), face(0), (gx + 1, gy))
        south = (gy > 0, packed.at[0], landing.at[1], (gx, gy - 1))
        north = (gy < 7, packed.at[1], landing.at[0], (gx, gy + 1))
        made = []
        for k, (has, src, dst, target) in enumerate((west, east, south, north)):
            made.append(
                (
                    has,
                    pltpu.make_async_remote_copy(
                        src_ref=src,
                        dst_ref=dst,
                        send_sem=hs.at[at, k],
                        recv_sem=hr.at[at, k],
                        device_id=target,
                        device_id_type=MESH,
                    ),
                )
            )
        return made

    def edges_start(made):
        for has, copy in made:
            pl.when(has)(copy.start)

    def edges_wait(made):
        for k, other in ((0, 1), (1, 0), (2, 3), (3, 2)):
            pl.when(made[other][0])(made[k][1].wait_recv)

    def edges_sent(made):
        for has, copy in made:
            pl.when(has)(copy.wait_send)

    def clear_edges(field, count, landing):
        zero = jnp.zeros((LEV, 128), F32)

        @pl.when(gx == 0)
        def _():
            field[0, pl.ds(8 if count == NX else 0, LEV), :] = zero

        @pl.when(gx == 15)
        def _():
            field[count + 1, pl.ds(8 if count == NX else 0, LEV), :] = zero

        @pl.when(gy == 0)
        def _():
            landing[0] = zero

        @pl.when(gy == 7)
        def _():
            landing[1] = zero

    def pack_edges(field, count, packed):
        base = 8 if count == NX else 0

        def one(x, carry):
            low, high = carry
            here = field[x + 1, pl.ds(base, LEV), :]
            low = jnp.where(lane == x, pltpu.roll(here, x, 1), low)
            high = jnp.where(lane == x, pltpu.roll(here, x + 1, 1), high)
            return low, high

        zero = jnp.zeros((LEV, 128), F32)
        low, high = lax.fori_loop(0, count, one, (zero, zero), unroll=16)
        packed[0] = low
        packed[1] = high

    deep = 32
    lanec = lax.broadcasted_iota(jnp.int32, (deep, 128), 1)
    levc = lax.broadcasted_iota(jnp.int32, (deep, 128), 0)

    def across(field, base, x, l0, landing, cx, cy):
        rows = pl.ds(base + l0, deep)
        here = field[x + 1, rows, :]
        west, east = field[x, rows, :], field[x + 2, rows, :]
        edge = pl.ds(l0, deep)
        south = jnp.where(
            lanec == 0,
            pltpu.roll(landing[0, edge, :], lax.rem(128 - x, 128), 1),
            pltpu.roll(here, 1, 1),
        )
        north = jnp.where(
            lanec == 127, pltpu.roll(landing[1, edge, :], 127 - x, 1), pltpu.roll(here, 127, 1)
        )
        return here, here - cx * jnp.where(cx > 0, here - west, east - here) - cy * jnp.where(
            cy > 0, here - south, north - here
        )

    def advance(field, x, l0, landing):
        edge = pl.ds(l0, deep)
        here, adv = across(field, 8, x, l0, landing, cxs[x, edge, :], cys[x, edge, :])
        cz = czs[x, edge, :]
        lower, upper = field[x + 1, pl.ds(7 + l0, deep), :], field[x + 1, pl.ds(9 + l0, deep), :]
        below = jnp.where(levc + (l0 - 1) >= terrain_ref[pl.ds(x, 1), :], lower, here)
        above = jnp.where(levc == LEV - 1 - l0, here, upper)
        return adv - cz * jnp.where(cz > 0, here - below, above - here)

    clear_edges(pq, PXN, pys)
    clear_edges(q0, NX, ybuf.at[0])
    clear_edges(q1, NX, ybuf.at[1])
    clear_edges(q2, NX, ybuf.at[2])

    blank8 = jnp.zeros((8, 128), F32)
    loaded(nraw, 0, NX, 1)

    def start_nest(x, carry):
        for field in (q0, q1, q2):
            field[x + 1, 0:8, :] = blank8
            field[x + 1, LEV + 8 : LEV + 16, :] = blank8
        q0[x + 1, 8 : LEV + 8, :] = jnp.where(lev >= terrain_ref[pl.ds(x, 1), :], nraw[x], 0.0)
        return carry

    lax.fori_loop(0, NX, start_nest, 0)
    pack_edges(q0, NX, ypack.at[0])
    q0_edges = edge_copies(q0, NX, ypack.at[0], ybuf.at[0], 0)
    edges_start(q0_edges)

    loaded(pq, 1, PXN, 0)

    def split(x, carry):
        shi[x], slo[x] = halves(pq[x + 1])
        return carry

    lax.fori_loop(0, PXN, split, 0, unroll=2)
    shi[PXN] = jnp.zeros((LEV, 128), BF16)
    slo[PXN] = jnp.zeros((LEV, 128), BF16)
    pack_edges(pq, PXN, pyk)
    p_edges = edge_copies(pq, PXN, pyk, pys, 1)
    edges_start(p_edges)


    def asked(g):
        part = reqin.at[pl.ds(g * (128 // GROUPS), 128 // GROUPS)]
        pltpu.make_async_copy(part, part, sem_req_r.at[g]).wait()

    sub256 = lax.broadcasted_iota(jnp.int32, (256, 128), 0)
    left48 = lax.broadcasted_iota(jnp.int32, (48, 128), 1) < 64
    left4 = lax.broadcasted_iota(jnp.int32, (4, 128), 1) < 64

    def answer(n, tx, ty):
        a, b = reqin[2 * n], reqin[2 * n + 1]
        place = jnp.where(left4, a, pltpu.roll(b, 64, 1)).astype(jnp.int32)
        amount = jnp.where(left4, pltpu.roll(a, 64, 1), b)
        table = jnp.zeros((256, 128), F32)
        for j in range(4):
            table = jnp.where(sub256 == place[j : j + 1], amount[j : j + 1], table)
        right = jnp.concatenate(halves(table), axis=1)
        base = (tx * 8 + ty) * 2
        rows = []
        for core in range(2):
            first, second = slots_ref[base + 2 * core], slots_ref[base + 2 * core + 1]
            rows.append(jnp.concatenate([shi[first], shi[second]], axis=1))
            rows.append(jnp.concatenate([slo[first], slo[second]], axis=1))
        out = jnp.dot(jnp.concatenate(rows, axis=0), right, preferred_element_type=F32)
        v0 = out[0:96, :128] + out[0:96, 128:] + out[96:192, :128]
        v1 = out[192:288, :128] + out[192:288, 128:] + out[288:384, :128]
        return (
            jnp.where(left48, v0[:48], pltpu.roll(v0[48:], 64, 1)),
            jnp.where(left48, pltpu.roll(v1[:48], 64, 1), v1[48:]),
        )

    def reply(base, count):
        places = [chip(base + u, -1) for u in range(count)]
        made = [answer(base + u, *places[u]) for u in range(count)]
        for u in range(count):
            ans[2 * (base + u)], ans[2 * (base + u) + 1] = made[u]
        for u in range(count):
            n = base + u
            tx, ty = places[u]
            for core in range(2):
                pltpu.make_async_remote_copy(
                    src_ref=ans.at[2 * n + core],
                    dst_ref=ansin.at[2 * n + mc],
                    send_sem=sem_ans_s,
                    recv_sem=sem_ans_r.at[lax.div(n, 64 // GROUPS)],
                    device_id=(tx, ty + core),
                    device_id_type=MESH,
                ).start()

    def replies(r, carry):
        asked(r)
        reply(8 * r, 4)
        reply(8 * r + 4, 4)
        return carry

    asked(0)
    ans[0], ans[1] = answer(0, gx, mx * 2)
    pltpu.make_async_remote_copy(
        src_ref=ans.at[1 - mc],
        dst_ref=ansin.at[mc],
        send_sem=sem_ans_s,
        recv_sem=sem_ans_r.at[0],
        device_id=(gx, mx * 2 + 1 - mc),
        device_id_type=MESH,
    ).start()
    pltpu.make_async_copy(ans.at[mc], ansin.at[mc], sem_ans_r.at[0]).start()
    reply(jnp.int32(1), 3)
    reply(jnp.int32(4), 4)
    lax.fori_loop(1, GROUPS, replies, 0)
    load(cx_ref, NX, cxs, 0, 2)
    load(cy_ref, NX, cys, 0, 3)
    load(cz_ref, NX, czs, 0, 4)
    load(pcx_ref, PXN, pcxs, 0, 5)
    load(pcy_ref, PXN, pcys, 0, 6)

    for k, (target, count) in enumerate(
        ((cxs, NX), (cys, NX), (czs, NX), (pcxs, PXN), (pcys, PXN))
    ):
        loaded(target, 0, count, k + 2)
    edges_wait(q0_edges)
    chunks = range(0, LEV, deep)

    def first_nest(x, carry):
        for l0 in chunks:
            adv1[x, pl.ds(l0, deep), :] = advance(q0, x, l0, ybuf.at[0])
        bound[x] = jnp.zeros((LEV, 128), F32)
        return carry

    lax.fori_loop(0, NX, first_nest, 0)

    edges_wait(p_edges)
    sub512 = lax.broadcasted_iota(jnp.int32, (256, 512), 0)
    ones8 = jnp.ones((8, 512), BF16)

    def parents(i, carry):
        hot = jnp.where(sub512 == fbt_ref[...] - 256 * i, 1.0, 0.0).astype(BF16)
        tmat[i] = hot
        left = 1.0 - 0.5 * lax.dot_general(ones8, hot, NT, preferred_element_type=F32)[0:1]
        for k in range(2):
            x = 2 * i + k
            for l0 in chunks:
                edge = pl.ds(l0, deep)
                moved = across(pq, 0, x, l0, pys, pcxs[x, edge, :], pcys[x, edge, :])[1]
                keep[x, edge, :] = moved * left[:, 128 * k : 128 * k + 128]
        return carry

    lax.fori_loop(0, PXN // 2, parents, 0)

    sub16 = lax.broadcasted_iota(jnp.int32, (16, 128), 0)

    fbt[...] = jnp.full((128, 256), -1.0, F32)

    def turn(i, carry):
        fbt[pl.ds(i, 1), :] = fbi_ref[i].astype(F32)
        return carry

    lax.fori_loop(0, 81, turn, 0)
    fbn[...] = jnp.transpose(fbt[...]).astype(jnp.int32)

    def count(r, carry):
        made = []
        for u in range(8):
            highs, lows = [], []
            for k in range(2):
                row = fbn[pl.ds(16 * r + 2 * u + k, 1), :]
                high = jnp.where(sub16 == (row >> 7), 1.0, 0.0).astype(BF16)
                blank = jnp.zeros((16, 128), BF16)
                highs.append(jnp.concatenate([high, blank] if k == 0 else [blank, high], axis=1))
                lows.append(jnp.where(sub128 == (row & 127), 1.0, 0.0).astype(BF16))
            made.append(
                lax.dot_general(
                    jnp.concatenate(highs, axis=0),
                    jnp.concatenate(lows, axis=1),
                    NT,
                    preferred_element_type=F32,
                )
            )
        for u in range(8):
            counts[16 * r + 2 * u] = made[u][:16]
            counts[16 * r + 2 * u + 1] = made[u][16:]
        return carry

    lax.fori_loop(0, 16, count, 0)
    row256 = lax.broadcasted_iota(jnp.int32, (256, 512), 0)
    chosen = jnp.transpose(jnp.where(row256 == fbs_ref[...], 1.0, 0.0)).astype(BF16)
    for x in range(NX):
        cmat[:, 128 * x : 128 * x + 128] = jnp.dot(
            chosen, counts[:, x, :].astype(BF16), preferred_element_type=F32
        ).astype(BF16)
    qmat[...] = jnp.zeros_like(qmat)


    per = 64 // GROUPS
    for g in range(GROUPS):
        part = ansin.at[pl.ds(2 * per * g, 2 * per)]
        pltpu.make_async_copy(part, part, sem_ans_r.at[g]).wait()
        for i in range(per):
            a, b = ansin[2 * (per * g + i)], ansin[2 * (per * g + i) + 1]
            upper = jnp.where(left48, a, pltpu.roll(b, 64, 1))
            lower = jnp.where(left48, pltpu.roll(a, 64, 1), b)
            high, low = halves(jnp.concatenate([upper, lower], axis=0))
            xmat[0:96, 128 * i : 128 * i + 128] = high
            xmat[96:192, 128 * i : 128 * i + 128] = low

        def pick(x, carry, g=g):
            hots = []
            for k in range(2):
                owner = jnp.broadcast_to(relm[pl.ds(2 * x + k, 1), :], (16, 128))
                ranks = rankm[2 * x + k]
                blocks = []
                for i in range(2 * per):
                    mine = jnp.where(owner == 2 * per * g + i, 1.0, 0.0).astype(BF16)
                    blocks.append(ranks * jnp.concatenate([mine] * (KREQ // 16), axis=0))
                hots.append(jnp.concatenate(blocks, axis=0))
            got = jnp.dot(xmat[...], jnp.concatenate(hots, axis=1), preferred_element_type=F32)
            bound[2 * x] += got[:96, :128] + got[96:, :128]
            bound[2 * x + 1] += got[:96, 128:] + got[96:, 128:]
            return carry

        lax.fori_loop(0, NX // 2, pick, 0, unroll=4)

    def settle(x, l0, adv):
        terrain = terrain_ref[pl.ds(x, 1), :]
        rel = relax_ref[pl.ds(x, 1), :]
        pull = bound[x, pl.ds(l0, deep), :] - adv
        return jnp.where(levc + l0 >= terrain, adv + rel * pull, 0.0)

    def first_settle(x, carry):
        for l0 in chunks:
            q1[x + 1, pl.ds(8 + l0, deep), :] = settle(x, l0, adv1[x, pl.ds(l0, deep), :])
        return carry

    lax.fori_loop(0, NX, first_settle, 0)
    edges = [q0_edges, p_edges]

    def exchange(now, step):
        pack_edges(now, NX, ypack.at[step])
        made = edge_copies(now, NX, ypack.at[step], ybuf.at[step], step + 1)
        edges_start(made)
        edges_wait(made)
        edges.append(made)

    exchange(q1, 1)

    def second(x, carry):
        for l0 in chunks:
            q2[x + 1, pl.ds(8 + l0, deep), :] = settle(x, l0, advance(q1, x, l0, ybuf.at[1]))
        return carry

    lax.fori_loop(0, NX, second, 0, unroll=4)
    exchange(q2, 2)

    def third(x, carry):
        at = pl.ds(pl.multiple_of(128 * x, 128), 128)
        for l0 in chunks:
            value = settle(x, l0, advance(q2, x, l0, ybuf.at[2]))
            nres[x, pl.ds(l0, deep), :] = value
            high, low = halves(value)
            qmat[pl.ds(l0, deep), at] = high
            qmat[pl.ds(128 + l0, deep), at] = low
        return carry

    lax.fori_loop(0, NX, third, 0, unroll=4)

    got = lax.dot_general(cmat[...], qmat[...], NT, preferred_element_type=F32)
    rows = (got[:, :128] + got[:, 128:]) * (1.0 / 81.0)
    lane512 = lax.broadcasted_iota(jnp.int32, (512, 128), 1)
    rows = jnp.where(lane512 == LEV, flag, rows)
    fbsend[...] = rows.reshape(128, 4, 128)

    def feed(n, carry):
        tx, ty = chip(n, 1)
        for core in range(2):
            pltpu.make_async_remote_copy(
                src_ref=fbsend.at[tx * 8 + ty + core],
                dst_ref=fbin.at[me],
                send_sem=sem_fb_s,
                recv_sem=sem_fb_r,
                device_id=(tx, ty + core),
                device_id_type=MESH,
            ).start()
        return carry

    lax.fori_loop(1, 64, feed, 0)
    other = mx * 2 + 1 - mc
    pltpu.make_async_remote_copy(
        src_ref=fbsend.at[gx * 8 + other],
        dst_ref=fbin.at[me],
        send_sem=sem_fb_s,
        recv_sem=sem_fb_r,
        device_id=(gx, other),
        device_id_type=MESH,
    ).start()
    pltpu.make_async_copy(fbsend.at[me], fbin.at[me], sem_fb_r).start()

    def store_nest(x, carry):
        pltpu.make_async_copy(nres.at[x], nest_out.at[:, x], sem_out.at[0]).start()
        return carry

    lax.fori_loop(0, NX, store_nest, 0)
    pltpu.make_async_copy(fbin, fbin, sem_fb_r).wait()


    values = fbin[...].reshape(512, 128)
    high, low = halves(jnp.transpose(values)[:96])
    both = jnp.concatenate([high, low], axis=0)
    for i in range(PXN // 2):
        got = lax.dot_general(both, tmat[i], NT, preferred_element_type=F32)
        for k in range(2):
            x, at = 2 * i + k, slice(128 * k, 128 * k + 128)
            keep[x] += 0.5 * (got[:96, at] + got[96:, at])
            pltpu.make_async_copy(keep.at[x], parent_out.at[:, x], sem_out.at[1]).start()
    worst = jnp.max(jnp.where(lane512 == LEV, values, 0.0))
    flag_out[0] = jnp.where(worst > 0.5, 1, 0)
    pltpu.make_async_copy(nres, nres, sem_out.at[0]).wait()
    pltpu.make_async_copy(keep, keep, sem_out.at[1]).wait()

    for buffer, sem in ((req, sem_req_s), (ans, sem_ans_s), (fbsend, sem_fb_s)):
        part = buffer.at[pl.ds(0, 127)]
        pltpu.make_async_copy(part, part, sem).wait()
    for made in edges:
        edges_sent(made)


def fused_step(
    nest_field,
    courant_x,
    courant_y,
    courant_z,
    terrain,
    relax,
    interp_index,
    interp_weight,
    send_slots,
    parent_field,
    parent_cx,
    parent_cy,
    fb_index,
    fb_slot,
    fb_target,
):
    vmem = pl.BlockSpec(memory_space=pltpu.VMEM)
    smem = pl.BlockSpec(memory_space=pltpu.SMEM)
    hbm = pl.BlockSpec(memory_space=pl.ANY)
    slab = (LEV, 128)
    scratch = [
        pltpu.VMEM((NX + 2, LEV + 16, 128), F32),
        pltpu.VMEM((NX + 2, LEV + 16, 128), F32),
        pltpu.VMEM((NX + 2, LEV + 16, 128), F32),
        pltpu.VMEM((3, 2) + slab, F32),
        pltpu.VMEM((3, 2) + slab, F32),
        pltpu.VMEM((NX,) + slab, F32),
        pltpu.VMEM((NX,) + slab, F32),
        pltpu.VMEM((PXN + 2,) + slab, F32),
        pltpu.VMEM((2,) + slab, F32),
        pltpu.VMEM((2,) + slab, F32),
        pltpu.VMEM((PXN,) + slab, F32),
        pltpu.VMEM((PXN + 1,) + slab, BF16),
        pltpu.VMEM((PXN + 1,) + slab, BF16),
        pltpu.VMEM((128, 4, 128), F32),
        pltpu.VMEM((128, 4, 128), F32),
        pltpu.VMEM((128, 48, 128), F32),
        pltpu.VMEM((128, 48, 128), F32),
        pltpu.VMEM((192, 64 // GROUPS * 128), BF16),
        pltpu.VMEM((256, NX, 128), F32),
        pltpu.VMEM((512, NX * 128), BF16),
        pltpu.VMEM((256, NX * 128), BF16),
        pltpu.VMEM((PXN // 2, 256, 512), BF16),
        pltpu.VMEM((128, 4, 128), F32),
        pltpu.VMEM((128, 4, 128), F32),
        pltpu.VMEM((128, NX * 128), BF16),
        pltpu.VMEM((1024, NX * 128), BF16),
        pltpu.VMEM((NX, KREQ, 128), BF16),
        pltpu.VMEM((NX, 128), jnp.int32),
        pltpu.VMEM((NX,) + slab, F32),
        pltpu.VMEM((NX,) + slab, F32),
        pltpu.VMEM((NX,) + slab, F32),
        pltpu.VMEM((NX,) + slab, F32),
        pltpu.VMEM((PXN,) + slab, F32),
        pltpu.VMEM((PXN,) + slab, F32),
        pltpu.VMEM((NX,) + slab, F32),
        pltpu.VMEM((128, 256), F32),
        pltpu.VMEM((256, 128), jnp.int32),
        pltpu.SemaphoreType.DMA((7,)),
        pltpu.SemaphoreType.DMA((2,)),
        pltpu.SemaphoreType.DMA,
        pltpu.SemaphoreType.DMA((GROUPS,)),
        pltpu.SemaphoreType.DMA,
        pltpu.SemaphoreType.DMA((GROUPS,)),
        pltpu.SemaphoreType.DMA,
        pltpu.SemaphoreType.DMA,
        pltpu.SemaphoreType.DMA((4, 4)),
        pltpu.SemaphoreType.DMA((4, 4)),
    ]
    return pl.pallas_call(
        step_kernel,
        out_shape=(
            jax.ShapeDtypeStruct(nest_field.shape, F32),
            jax.ShapeDtypeStruct(parent_field.shape, F32),
            jax.ShapeDtypeStruct((1,), jnp.int32),
        ),
        in_specs=[smem] + [hbm] * 4 + [vmem] * 4 + [hbm] * 3 + [vmem] * 3,
        out_specs=(hbm, hbm, smem),
        scratch_shapes=scratch,
        compiler_params=pltpu.CompilerParams(
            collective_id=0, has_side_effects=True, vmem_limit_bytes=56 * 2**20
        ),
        name="step",
    )(
        send_slots[0],
        nest_field,
        courant_x,
        courant_y,
        courant_z,
        terrain,
        relax,
        interp_index,
        interp_weight,
        parent_field,
        parent_cx,
        parent_cy,
        jnp.transpose(fb_index, (2, 0, 1)),
        fb_slot,
        fb_target,
    )


def hand_over(nest_ref, parent_ref, nest_out, parent_out, nest_buf, parent_buf, come, go):
    arriving, leaving = [], []
    for part in range(4):
        rows = pl.ds(24 * part, 24)
        for k, (source, held, target) in enumerate(
            ((nest_ref, nest_buf, nest_out), (parent_ref, parent_buf, parent_out))
        ):
            arriving.append(
                pltpu.make_async_copy(source.at[rows], held.at[rows], come.at[k, part])
            )
            leaving.append(pltpu.make_async_copy(held.at[rows], target.at[rows], go.at[k, part]))
    for copy in arriving:
        copy.start()
    for first, second in zip(arriving, leaving):
        first.wait()
        second.start()
    for copy in leaving:
        copy.wait()


def handed(nest_out, parent_out):
    hbm = pl.BlockSpec(memory_space=pl.ANY)
    return pl.pallas_call(
        hand_over,
        out_shape=(
            jax.ShapeDtypeStruct(nest_out.shape, F32),
            jax.ShapeDtypeStruct(parent_out.shape, F32),
        ),
        in_specs=[hbm, hbm],
        out_specs=(hbm, hbm),
        scratch_shapes=[
            pltpu.VMEM(nest_out.shape, F32),
            pltpu.VMEM(parent_out.shape, F32),
            pltpu.SemaphoreType.DMA((2, 4)),
            pltpu.SemaphoreType.DMA((2, 4)),
        ],
        compiler_params=pltpu.CompilerParams(vmem_limit_bytes=16 * 2**20),
        name="hand_over",
    )(nest_out, parent_out)


def on_device(*args):
    nest_out, parent_out, flags = fused_step(*args)
    return lax.cond(
        flags[0] > 0, lambda: dense_step(*args), lambda: handed(nest_out, parent_out)
    )


def solution(mesh):
    in_specs = (
        P(None, "gx", "gy"),
        P(None, "gx", "gy"),
        P(None, "gx", "gy"),
        P(None, "gx", "gy"),
        P("gx", "gy"),
        P("gx", "gy"),
        P(None, "gx", "gy"),
        P(None, "gx", "gy"),
        P(("gx", "gy"), None),
        P(None, "gx", "gy"),
        P(None, "gx", "gy"),
        P(None, "gx", "gy"),
        P(("gx", "gy"), None, None),
        P(("gx", "gy"), None),
        P(("gx", "gy"), None),
    )
    out_specs = (P(None, "gx", "gy"), P(None, "gx", "gy"))
    return jax.shard_map(
        on_device, mesh=mesh, in_specs=in_specs, out_specs=out_specs, check_vma=False
    )
```

```python
import functools

import jax
import jax.numpy as jnp
from jax import lax
from jax.experimental import pallas as pl
from jax.experimental.pallas import tpu as pltpu
from jax.sharding import PartitionSpec as P

TILE = 128
CAP = 2
FCAP = 4
SUBSTEPS = 3


blend_rate = 0.5


def extended(block, sides, width):
    for axis, dim in sides:
        count = lax.axis_size(axis)
        forward = [(i, i + 1) for i in range(count - 1)]
        backward = [(target, source) for source, target in forward]
        low = lax.ppermute(
            lax.slice_in_dim(block, block.shape[dim] - width, None, axis=dim), axis, forward
        )
        high = lax.ppermute(lax.slice_in_dim(block, 0, width, axis=dim), axis, backward)
        block = jnp.concatenate([low, block, high], axis=dim)
    return block


def upwind(padded, field, cx, cy):
    west = padded[:, :-2, 1:-1]
    east = padded[:, 2:, 1:-1]
    south = padded[:, 1:-1, :-2]
    north = padded[:, 1:-1, 2:]
    return cx * jnp.where(cx > 0, field - west, east - field) + cy * jnp.where(
        cy > 0, field - south, north - field
    )


def vertical(field, cz, mask):
    below = jnp.concatenate([field[:1], field[:-1]], axis=0)
    mask_below = jnp.concatenate([jnp.zeros_like(mask[:1]), mask[:-1]], axis=0)
    below = jnp.where(mask_below, below, field)
    above = jnp.concatenate([field[1:], field[-1:]], axis=0)
    return cz * jnp.where(cz > 0, field - below, above - field)


def dense_step(
    nest_field,
    courant_x,
    courant_y,
    courant_z,
    terrain,
    relax,
    interp_index,
    interp_weight,
    send_slots,
    parent_field,
    parent_cx,
    parent_cy,
    fb_index,
    fb_slot,
    fb_target,
):
    n_east = lax.axis_size("gx")
    n_north = lax.axis_size("gy")
    devices = n_east * n_north
    levels, nest_x, nest_y = nest_field.shape
    parent_x, parent_y = (parent_field.shape[1], parent_field.shape[2])
    parent_cols = parent_x * parent_y
    nest_cols = nest_x * nest_y
    slabs = parent_field
    slabs = jnp.concatenate([slabs, jnp.zeros((levels, 1, TILE), jnp.float32)], axis=1)
    picked = jnp.take(slabs, send_slots[0], axis=1)
    outgoing = picked.reshape(levels, devices, CAP, TILE)
    incoming = lax.all_to_all(outgoing, ("gx", "gy"), split_axis=1, concat_axis=1, tiled=True)
    received_cols = incoming.reshape(levels, -1).T
    padded_parent = extended(parent_field, (("gx", 1), ("gy", 2)), 1)
    advected = parent_field - upwind(padded_parent, parent_field, parent_cx, parent_cy)
    index_flat = interp_index.reshape(4, -1)
    weight_flat = interp_weight.reshape(4, -1)
    boundary_cols = weight_flat[0][:, None] * jnp.take(received_cols, index_flat[0], axis=0)
    for j in range(1, 4):
        boundary_cols = boundary_cols + weight_flat[j][:, None] * jnp.take(
            received_cols, index_flat[j], axis=0
        )
    boundary = boundary_cols.T.reshape(levels, nest_x, nest_y)
    level_ids = lax.broadcasted_iota(jnp.int32, (levels, 1, 1), 0)
    mask = level_ids >= terrain[None]
    field = jnp.where(mask, nest_field, 0.0)
    for step in range(SUBSTEPS):
        padded = extended(field, (("gx", 1), ("gy", 2)), 1)
        adv = field - upwind(padded, field, courant_x, courant_y) - vertical(field, courant_z, mask)
        field = jnp.where(mask, adv + relax[None] * (boundary - adv), 0.0)
    flat_nest = field.reshape(levels, nest_cols)
    row_count = fb_index.shape[1]
    averaged = fb_index.shape[2]
    row_ids = lax.broadcasted_iota(jnp.int32, (row_count, averaged), 0)
    averaging = jnp.zeros((row_count + 1, nest_cols), jnp.float32)
    averaging = averaging.at[row_ids, fb_index[0]].add(1.0 / averaged)
    slot_weights = jnp.take(averaging, fb_slot[0], axis=0)
    chosen_rows = lax.dot_general(
        slot_weights,
        flat_nest,
        (((1,), (1,)), ((), ())),
        precision=lax.Precision.HIGHEST,
        preferred_element_type=jnp.float32,
    )
    sending = chosen_rows.reshape(devices, FCAP * levels)
    arrived = lax.all_to_all(sending, ("gx", "gy"), split_axis=0, concat_axis=0, tiled=True)
    values = arrived.reshape(-1, levels)
    flat_parent = advected.reshape(levels, parent_cols)
    target = fb_target[0]
    current = jnp.take(flat_parent, jnp.minimum(target, parent_cols - 1), axis=1)
    delta = blend_rate * (values.T - current)
    updated = flat_parent.at[:, target].add(delta, mode="drop")
    return (field, updated.reshape(levels, parent_x, parent_y))


MESH = pl.DeviceIdType.MESH
LEV = 96
NX = 16
PXN = 32
KREQ = 64
GROUPS = 8
F32 = jnp.float32
BF16 = jnp.bfloat16
NT = (((1,), (1,)), ((), ()))


def halves(value):
    high = value.astype(BF16)
    return high, (value - high.astype(F32)).astype(BF16)


def step_kernel(
    slots_ref,
    nest_ref,
    cx_ref,
    cy_ref,
    cz_ref,
    terrain_ref,
    relax_ref,
    index_ref,
    weight_ref,
    parent_ref,
    pcx_ref,
    pcy_ref,
    fbi_ref,
    fbs_ref,
    fbt_ref,
    nest_out,
    parent_out,
    flag_out,
    q0,
    q1,
    q2,
    ybuf,
    ypack,
    adv1,
    bound,
    pq,
    pys,
    pyk,
    keep,
    shi,
    slo,
    req,
    reqin,
    ans,
    ansin,
    xmat,
    counts,
    cmat,
    qmat,
    tmat,
    fbsend,
    fbin,
    hotm,
    tabm,
    rankm,
    relm,
    nraw,
    cxs,
    cys,
    czs,
    pcxs,
    pcys,
    nres,
    fbt,
    fbn,
    sem_in,
    sem_out,
    sem_req_s,
    sem_req_r,
    sem_ans_s,
    sem_ans_r,
    sem_fb_s,
    sem_fb_r,
    hs,
    hr,
):
    gx = lax.axis_index("gx")
    gy = lax.axis_index("gy")
    mz, my, mx, mc = lax.div(gx, 4), lax.rem(gx, 4), lax.div(gy, 2), lax.rem(gy, 2)
    me = gx * 8 + gy

    def chip(n, sign):
        dx = lax.rem(n, 4)
        dy = lax.rem(lax.div(n, 4) + dx, 4)
        dz = lax.rem(lax.div(n, 16) + dy, 4)
        if sign < 0:
            dz, dy, dx = 4 - dz, 4 - dy, 4 - dx
        z, y, x = lax.rem(mz + dz, 4), lax.rem(my + dy, 4), lax.rem(mx + dx, 4)
        return z * 4 + y, x * 2

    barrier = pltpu.get_barrier_semaphore()

    zs = [lax.rem(mz + k, 4) * 4 for k in range(4)]
    ys = [lax.rem(my + k, 4) for k in range(4)]
    xs = [lax.rem(mx + k, 4) * 2 for k in range(4)]

    def ahead(n):
        dx = n % 4
        dy = (n // 4 + dx) % 4
        dz = (n // 16 + dy) % 4
        return zs[dz] + ys[dy], xs[dx]

    for n in range(1, 64):
        tx, ty = ahead(n)
        for core in range(2):
            pl.semaphore_signal(barrier, inc=1, device_id=(tx, ty + core), device_id_type=MESH)
    pl.semaphore_signal(barrier, inc=1, device_id=(gx, mx * 2 + 1 - mc), device_id_type=MESH)

    def load(source, count, target, first, k):
        def one(x, carry):
            pltpu.make_async_copy(source.at[:, x], target.at[x + first], sem_in.at[k]).start()
            return carry

        lax.fori_loop(0, count, one, 0)

    def loaded(target, first, count, k):
        part = target.at[pl.ds(first, count)]
        pltpu.make_async_copy(part, part, sem_in.at[k]).wait()

    sub128 = lax.broadcasted_iota(jnp.int32, (128, 128), 0)
    lane128 = lax.broadcasted_iota(jnp.int32, (128, 128), 1)
    sub64 = lax.broadcasted_iota(jnp.int32, (KREQ, 128), 0)

    before = jnp.concatenate(
        [jnp.where(sub128 < lane128, 1.0, 0.0), jnp.ones((128, 128), F32)], axis=1
    ).astype(BF16)
    run = jnp.zeros((128, 128), F32)
    top = jnp.zeros((1, 128), F32)
    for x in range(NX):
        idx = [index_ref[j, x : x + 1, :] for j in range(4)]
        src = idx[0] >> 8
        dz, dy, dx = (src >> 5) - mz, ((src >> 3) & 3) - my, ((src >> 1) & 3) - mx
        rel = (((dz - dy) & 3) << 5) | (((dy - dx) & 3) << 3) | ((dx & 3) << 1) | (src & 1)
        relm[x : x + 1, :] = rel
        hot = jnp.where(sub128 == rel, 1.0, 0.0)
        hotb = hot.astype(BF16)
        both = jnp.dot(hotb, before, preferred_element_type=F32)
        rank = jnp.sum(hot * (both[:, :128] + run), axis=0, keepdims=True)
        run = run + both[:, 128:]
        top = jnp.maximum(top, rank)
        here = sub64 == rank.astype(jnp.int32)
        rankm[x] = jnp.where(here, 1.0, 0.0).astype(BF16)
        at = slice(128 * x, 128 * x + 128)
        hotm[:, at] = hotb
        for j in range(4):
            low = (idx[j] & 255).astype(F32)
            w = weight_ref[j, x : x + 1, :]
            whi = w.astype(BF16).astype(F32)
            tabm[128 * j : 128 * j + 64, at] = jnp.where(here, low, 0.0).astype(BF16)
            tabm[128 * j + 64 : 128 * j + 128, at] = jnp.where(here, whi, 0.0).astype(BF16)
            tabm[512 + 128 * j : 576 + 128 * j, at] = jnp.zeros((KREQ, 128), BF16)
            tabm[576 + 128 * j : 640 + 128 * j, at] = jnp.where(here, w - whi, 0.0).astype(BF16)
    flag = jnp.max(jnp.where(top >= KREQ, 1.0, 0.0), axis=1, keepdims=True)
    racc = lax.dot_general(hotm[...], tabm[...], NT, preferred_element_type=F32)
    for j in range(4):
        req[:, j, :] = (
            racc[:, 128 * j : 128 * j + 128] + racc[:, 512 + 128 * j : 640 + 128 * j]
        )

    load(parent_ref, PXN, pq, 1, 0)
    load(nest_ref, NX, nraw, 0, 1)
    pl.semaphore_wait(barrier, 127)

    for n in range(1, 64):
        tx, ty = ahead(n)
        for core in range(2):
            pltpu.make_async_remote_copy(
                src_ref=req.at[2 * n + core],
                dst_ref=reqin.at[2 * n + mc],
                send_sem=sem_req_s,
                recv_sem=sem_req_r.at[n // (64 // GROUPS)],
                device_id=(tx, ty + core),
                device_id_type=MESH,
            ).start()
    pltpu.make_async_remote_copy(
        src_ref=req.at[1 - mc],
        dst_ref=reqin.at[mc],
        send_sem=sem_req_s,
        recv_sem=sem_req_r.at[0],
        device_id=(gx, mx * 2 + 1 - mc),
        device_id_type=MESH,
    ).start()
    pltpu.make_async_copy(req.at[mc], reqin.at[mc], sem_req_r.at[0]).start()

    load(cx_ref, NX, cxs, 0, 2)
    load(cy_ref, NX, cys, 0, 3)
    load(cz_ref, NX, czs, 0, 4)
    load(pcx_ref, PXN, pcxs, 0, 5)
    load(pcy_ref, PXN, pcys, 0, 6)

    lev = lax.broadcasted_iota(jnp.int32, (LEV, 128), 0)
    lane = lax.broadcasted_iota(jnp.int32, (LEV, 128), 1)

    def edge_copies(field, count, packed, landing, at):
        def face(x):
            return field.at[x, pl.ds(8, LEV)] if count == NX else field.at[x]

        west = (gx > 0, face(1), face(count + 1), (gx - 1, gy))
        east = (gx < 15, face(count), face(0), (gx + 1, gy))
        south = (gy > 0, packed.at[0], landing.at[1], (gx, gy - 1))
        north = (gy < 7, packed.at[1], landing.at[0], (gx, gy + 1))
        made = []
        for k, (has, src, dst, target) in enumerate((west, east, south, north)):
            made.append(
                (
                    has,
                    pltpu.make_async_remote_copy(
                        src_ref=src,
                        dst_ref=dst,
                        send_sem=hs.at[at, k],
                        recv_sem=hr.at[at, k],
                        device_id=target,
                        device_id_type=MESH,
                    ),
                )
            )
        return made

    def edges_start(made):
        for has, copy in made:
            pl.when(has)(copy.start)

    def edges_wait(made):
        for k, other in ((0, 1), (1, 0), (2, 3), (3, 2)):
            pl.when(made[other][0])(made[k][1].wait_recv)

    def edges_sent(made):
        for has, copy in made:
            pl.when(has)(copy.wait_send)

    def clear_edges(field, count, landing):
        zero = jnp.zeros((LEV, 128), F32)

        @pl.when(gx == 0)
        def _():
            field[0, pl.ds(8 if count == NX else 0, LEV), :] = zero

        @pl.when(gx == 15)
        def _():
            field[count + 1, pl.ds(8 if count == NX else 0, LEV), :] = zero

        @pl.when(gy == 0)
        def _():
            landing[0] = zero

        @pl.when(gy == 7)
        def _():
            landing[1] = zero

    def pack_edges(field, count, packed):
        base = 8 if count == NX else 0

        def one(x, carry):
            low, high = carry
            here = field[x + 1, pl.ds(base, LEV), :]
            low = jnp.where(lane == x, pltpu.roll(here, x, 1), low)
            high = jnp.where(lane == x, pltpu.roll(here, x + 1, 1), high)
            return low, high

        zero = jnp.zeros((LEV, 128), F32)
        low, high = lax.fori_loop(0, count, one, (zero, zero), unroll=16)
        packed[0] = low
        packed[1] = high

    deep = 32
    lanec = lax.broadcasted_iota(jnp.int32, (deep, 128), 1)
    levc = lax.broadcasted_iota(jnp.int32, (deep, 128), 0)

    def across(field, base, x, l0, landing, cx, cy):
        rows = pl.ds(base + l0, deep)
        here = field[x + 1, rows, :]
        west, east = field[x, rows, :], field[x + 2, rows, :]
        edge = pl.ds(l0, deep)
        south = jnp.where(
            lanec == 0,
            pltpu.roll(landing[0, edge, :], lax.rem(128 - x, 128), 1),
            pltpu.roll(here, 1, 1),
        )
        north = jnp.where(
            lanec == 127, pltpu.roll(landing[1, edge, :], 127 - x, 1), pltpu.roll(here, 127, 1)
        )
        return here, here - cx * jnp.where(cx > 0, here - west, east - here) - cy * jnp.where(
            cy > 0, here - south, north - here
        )

    def advance(field, x, l0, landing):
        edge = pl.ds(l0, deep)
        here, adv = across(field, 8, x, l0, landing, cxs[x, edge, :], cys[x, edge, :])
        cz = czs[x, edge, :]
        lower, upper = field[x + 1, pl.ds(7 + l0, deep), :], field[x + 1, pl.ds(9 + l0, deep), :]
        below = jnp.where(levc + (l0 - 1) >= terrain_ref[pl.ds(x, 1), :], lower, here)
        above = jnp.where(levc == LEV - 1 - l0, here, upper)
        return adv - cz * jnp.where(cz > 0, here - below, above - here)

    clear_edges(pq, PXN, pys)
    clear_edges(q0, NX, ybuf.at[0])
    clear_edges(q1, NX, ybuf.at[1])
    clear_edges(q2, NX, ybuf.at[2])

    blank8 = jnp.zeros((8, 128), F32)
    loaded(nraw, 0, NX, 1)

    def start_nest(x, carry):
        for field in (q0, q1, q2):
            field[x + 1, 0:8, :] = blank8
            field[x + 1, LEV + 8 : LEV + 16, :] = blank8
        q0[x + 1, 8 : LEV + 8, :] = jnp.where(lev >= terrain_ref[pl.ds(x, 1), :], nraw[x], 0.0)
        return carry

    lax.fori_loop(0, NX, start_nest, 0)
    pack_edges(q0, NX, ypack.at[0])
    q0_edges = edge_copies(q0, NX, ypack.at[0], ybuf.at[0], 0)
    edges_start(q0_edges)

    loaded(pq, 1, PXN, 0)

    def split(x, carry):
        shi[x], slo[x] = halves(pq[x + 1])
        return carry

    lax.fori_loop(0, PXN, split, 0, unroll=2)
    shi[PXN] = jnp.zeros((LEV, 128), BF16)
    slo[PXN] = jnp.zeros((LEV, 128), BF16)
    pack_edges(pq, PXN, pyk)
    p_edges = edge_copies(pq, PXN, pyk, pys, 1)
    edges_start(p_edges)


    def asked(g):
        part = reqin.at[pl.ds(g * (128 // GROUPS), 128 // GROUPS)]
        pltpu.make_async_copy(part, part, sem_req_r.at[g]).wait()

    sub256 = lax.broadcasted_iota(jnp.int32, (256, 128), 0)
    left48 = lax.broadcasted_iota(jnp.int32, (48, 128), 1) < 64
    left4 = lax.broadcasted_iota(jnp.int32, (4, 128), 1) < 64

    def answer(n, tx, ty):
        a, b = reqin[2 * n], reqin[2 * n + 1]
        place = jnp.where(left4, a, pltpu.roll(b, 64, 1)).astype(jnp.int32)
        amount = jnp.where(left4, pltpu.roll(a, 64, 1), b)
        table = jnp.zeros((256, 128), F32)
        for j in range(4):
            table = jnp.where(sub256 == place[j : j + 1], amount[j : j + 1], table)
        right = jnp.concatenate(halves(table), axis=1)
        base = (tx * 8 + ty) * 2
        rows = []
        for core in range(2):
            first, second = slots_ref[base + 2 * core], slots_ref[base + 2 * core + 1]
            rows.append(jnp.concatenate([shi[first], shi[second]], axis=1))
            rows.append(jnp.concatenate([slo[first], slo[second]], axis=1))
        out = jnp.dot(jnp.concatenate(rows, axis=0), right, preferred_element_type=F32)
        v0 = out[0:96, :128] + out[0:96, 128:] + out[96:192, :128]
        v1 = out[192:288, :128] + out[192:288, 128:] + out[288:384, :128]
        return (
            jnp.where(left48, v0[:48], pltpu.roll(v0[48:], 64, 1)),
            jnp.where(left48, pltpu.roll(v1[:48], 64, 1), v1[48:]),
        )

    def reply(base, count):
        places = [chip(base + u, -1) for u in range(count)]
        made = [answer(base + u, *places[u]) for u in range(count)]
        for u in range(count):
            ans[2 * (base + u)], ans[2 * (base + u) + 1] = made[u]
        for u in range(count):
            n = base + u
            tx, ty = places[u]
            for core in range(2):
                pltpu.make_async_remote_copy(
                    src_ref=ans.at[2 * n + core],
                    dst_ref=ansin.at[2 * n + mc],
                    send_sem=sem_ans_s,
                    recv_sem=sem_ans_r.at[lax.div(n, 64 // GROUPS)],
                    device_id=(tx, ty + core),
                    device_id_type=MESH,
                ).start()

    def replies(r, carry):
        asked(r)
        reply(8 * r, 4)
        reply(8 * r + 4, 4)
        return carry

    asked(0)
    ans[0], ans[1] = answer(0, gx, mx * 2)
    pltpu.make_async_remote_copy(
        src_ref=ans.at[1 - mc],
        dst_ref=ansin.at[mc],
        send_sem=sem_ans_s,
        recv_sem=sem_ans_r.at[0],
        device_id=(gx, mx * 2 + 1 - mc),
        device_id_type=MESH,
    ).start()
    pltpu.make_async_copy(ans.at[mc], ansin.at[mc], sem_ans_r.at[0]).start()
    reply(jnp.int32(1), 3)
    reply(jnp.int32(4), 4)
    lax.fori_loop(1, GROUPS, replies, 0)

    for k, (target, count) in enumerate(
        ((cxs, NX), (cys, NX), (czs, NX), (pcxs, PXN), (pcys, PXN))
    ):
        loaded(target, 0, count, k + 2)
    edges_wait(q0_edges)
    chunks = range(0, LEV, deep)

    def first_nest(x, carry):
        for l0 in chunks:
            adv1[x, pl.ds(l0, deep), :] = advance(q0, x, l0, ybuf.at[0])
        bound[x] = jnp.zeros((LEV, 128), F32)
        return carry

    lax.fori_loop(0, NX, first_nest, 0)

    edges_wait(p_edges)
    sub512 = lax.broadcasted_iota(jnp.int32, (256, 512), 0)
    ones8 = jnp.ones((8, 512), BF16)

    def parents(i, carry):
        hot = jnp.where(sub512 == fbt_ref[...] - 256 * i, 1.0, 0.0).astype(BF16)
        tmat[i] = hot
        left = 1.0 - 0.5 * lax.dot_general(ones8, hot, NT, preferred_element_type=F32)[0:1]
        for k in range(2):
            x = 2 * i + k
            for l0 in chunks:
                edge = pl.ds(l0, deep)
                moved = across(pq, 0, x, l0, pys, pcxs[x, edge, :], pcys[x, edge, :])[1]
                keep[x, edge, :] = moved * left[:, 128 * k : 128 * k + 128]
        return carry

    lax.fori_loop(0, PXN // 2, parents, 0)

    sub16 = lax.broadcasted_iota(jnp.int32, (16, 128), 0)

    fbt[...] = jnp.full((128, 256), -1.0, F32)

    def turn(i, carry):
        fbt[pl.ds(i, 1), :] = fbi_ref[i].astype(F32)
        return carry

    lax.fori_loop(0, 81, turn, 0)
    fbn[...] = jnp.transpose(fbt[...]).astype(jnp.int32)

    def count(r, carry):
        made = []
        for u in range(8):
            highs, lows = [], []
            for k in range(2):
                row = fbn[pl.ds(16 * r + 2 * u + k, 1), :]
                high = jnp.where(sub16 == (row >> 7), 1.0, 0.0).astype(BF16)
                blank = jnp.zeros((16, 128), BF16)
                highs.append(jnp.concatenate([high, blank] if k == 0 else [blank, high], axis=1))
                lows.append(jnp.where(sub128 == (row & 127), 1.0, 0.0).astype(BF16))
            made.append(
                lax.dot_general(
                    jnp.concatenate(highs, axis=0),
                    jnp.concatenate(lows, axis=1),
                    NT,
                    preferred_element_type=F32,
                )
            )
        for u in range(8):
            counts[16 * r + 2 * u] = made[u][:16]
            counts[16 * r + 2 * u + 1] = made[u][16:]
        return carry

    lax.fori_loop(0, 16, count, 0)
    row256 = lax.broadcasted_iota(jnp.int32, (256, 512), 0)
    chosen = jnp.transpose(jnp.where(row256 == fbs_ref[...], 1.0, 0.0)).astype(BF16)
    for x in range(NX):
        cmat[:, 128 * x : 128 * x + 128] = jnp.dot(
            chosen, counts[:, x, :].astype(BF16), preferred_element_type=F32
        ).astype(BF16)
    qmat[...] = jnp.zeros_like(qmat)


    per = 64 // GROUPS
    for g in range(GROUPS):
        part = ansin.at[pl.ds(2 * per * g, 2 * per)]
        pltpu.make_async_copy(part, part, sem_ans_r.at[g]).wait()
        for i in range(per):
            a, b = ansin[2 * (per * g + i)], ansin[2 * (per * g + i) + 1]
            upper = jnp.where(left48, a, pltpu.roll(b, 64, 1))
            lower = jnp.where(left48, pltpu.roll(a, 64, 1), b)
            high, low = halves(jnp.concatenate([upper, lower], axis=0))
            xmat[0:96, 128 * i : 128 * i + 128] = high
            xmat[96:192, 128 * i : 128 * i + 128] = low

        def pick(x, carry, g=g):
            hots = []
            for k in range(2):
                owner = jnp.broadcast_to(relm[pl.ds(2 * x + k, 1), :], (16, 128))
                ranks = rankm[2 * x + k]
                blocks = []
                for i in range(2 * per):
                    mine = jnp.where(owner == 2 * per * g + i, 1.0, 0.0).astype(BF16)
                    blocks.append(ranks * jnp.concatenate([mine] * (KREQ // 16), axis=0))
                hots.append(jnp.concatenate(blocks, axis=0))
            got = jnp.dot(xmat[...], jnp.concatenate(hots, axis=1), preferred_element_type=F32)
            bound[2 * x] += got[:96, :128] + got[96:, :128]
            bound[2 * x + 1] += got[:96, 128:] + got[96:, 128:]
            return carry

        lax.fori_loop(0, NX // 2, pick, 0, unroll=4)

    def settle(x, l0, adv):
        terrain = terrain_ref[pl.ds(x, 1), :]
        rel = relax_ref[pl.ds(x, 1), :]
        pull = bound[x, pl.ds(l0, deep), :] - adv
        return jnp.where(levc + l0 >= terrain, adv + rel * pull, 0.0)

    def first_settle(x, carry):
        for l0 in chunks:
            q1[x + 1, pl.ds(8 + l0, deep), :] = settle(x, l0, adv1[x, pl.ds(l0, deep), :])
        return carry

    lax.fori_loop(0, NX, first_settle, 0)
    edges = [q0_edges, p_edges]

    def exchange(now, step):
        pack_edges(now, NX, ypack.at[step])
        made = edge_copies(now, NX, ypack.at[step], ybuf.at[step], step + 1)
        edges_start(made)
        edges_wait(made)
        edges.append(made)

    exchange(q1, 1)

    def second(x, carry):
        for l0 in chunks:
            q2[x + 1, pl.ds(8 + l0, deep), :] = settle(x, l0, advance(q1, x, l0, ybuf.at[1]))
        return carry

    lax.fori_loop(0, NX, second, 0, unroll=4)
    exchange(q2, 2)

    def third(x, carry):
        at = pl.ds(pl.multiple_of(128 * x, 128), 128)
        for l0 in chunks:
            value = settle(x, l0, advance(q2, x, l0, ybuf.at[2]))
            nres[x, pl.ds(l0, deep), :] = value
            high, low = halves(value)
            qmat[pl.ds(l0, deep), at] = high
            qmat[pl.ds(128 + l0, deep), at] = low
        return carry

    lax.fori_loop(0, NX, third, 0, unroll=4)

    got = lax.dot_general(cmat[...], qmat[...], NT, preferred_element_type=F32)
    rows = (got[:, :128] + got[:, 128:]) * (1.0 / 81.0)
    lane512 = lax.broadcasted_iota(jnp.int32, (512, 128), 1)
    rows = jnp.where(lane512 == LEV, flag, rows)
    fbsend[...] = rows.reshape(128, 4, 128)

    for n in range(1, 64):
        tx, ty = ahead(n)
        for core in range(2):
            pltpu.make_async_remote_copy(
                src_ref=fbsend.at[tx * 8 + ty + core],
                dst_ref=fbin.at[me],
                send_sem=sem_fb_s,
                recv_sem=sem_fb_r,
                device_id=(tx, ty + core),
                device_id_type=MESH,
            ).start()
    other = mx * 2 + 1 - mc
    pltpu.make_async_remote_copy(
        src_ref=fbsend.at[gx * 8 + other],
        dst_ref=fbin.at[me],
        send_sem=sem_fb_s,
        recv_sem=sem_fb_r,
        device_id=(gx, other),
        device_id_type=MESH,
    ).start()
    pltpu.make_async_copy(fbsend.at[me], fbin.at[me], sem_fb_r).start()

    def store_nest(x, carry):
        pltpu.make_async_copy(nres.at[x], nest_out.at[:, x], sem_out.at[0]).start()
        return carry

    lax.fori_loop(0, NX, store_nest, 0)
    pltpu.make_async_copy(fbin, fbin, sem_fb_r).wait()


    values = fbin[...].reshape(512, 128)
    high, low = halves(jnp.transpose(values)[:96])
    both = jnp.concatenate([high, low], axis=0)
    for i in range(PXN // 2):
        got = lax.dot_general(both, tmat[i], NT, preferred_element_type=F32)
        for k in range(2):
            x, at = 2 * i + k, slice(128 * k, 128 * k + 128)
            keep[x] += 0.5 * (got[:96, at] + got[96:, at])
            pltpu.make_async_copy(keep.at[x], parent_out.at[:, x], sem_out.at[1]).start()
    worst = jnp.max(jnp.where(lane512 == LEV, values, 0.0))
    flag_out[0] = jnp.where(worst > 0.5, 1, 0)
    pltpu.make_async_copy(nres, nres, sem_out.at[0]).wait()
    pltpu.make_async_copy(keep, keep, sem_out.at[1]).wait()

    for buffer, sem in ((req, sem_req_s), (ans, sem_ans_s), (fbsend, sem_fb_s)):
        part = buffer.at[pl.ds(0, 127)]
        pltpu.make_async_copy(part, part, sem).wait()
    for made in edges:
        edges_sent(made)


def fused_step(
    nest_field,
    courant_x,
    courant_y,
    courant_z,
    terrain,
    relax,
    interp_index,
    interp_weight,
    send_slots,
    parent_field,
    parent_cx,
    parent_cy,
    fb_index,
    fb_slot,
    fb_target,
):
    vmem = pl.BlockSpec(memory_space=pltpu.VMEM)
    smem = pl.BlockSpec(memory_space=pltpu.SMEM)
    hbm = pl.BlockSpec(memory_space=pl.ANY)
    slab = (LEV, 128)
    scratch = [
        pltpu.VMEM((NX + 2, LEV + 16, 128), F32),
        pltpu.VMEM((NX + 2, LEV + 16, 128), F32),
        pltpu.VMEM((NX + 2, LEV + 16, 128), F32),
        pltpu.VMEM((3, 2) + slab, F32),
        pltpu.VMEM((3, 2) + slab, F32),
        pltpu.VMEM((NX,) + slab, F32),
        pltpu.VMEM((NX,) + slab, F32),
        pltpu.VMEM((PXN + 2,) + slab, F32),
        pltpu.VMEM((2,) + slab, F32),
        pltpu.VMEM((2,) + slab, F32),
        pltpu.VMEM((PXN,) + slab, F32),
        pltpu.VMEM((PXN + 1,) + slab, BF16),
        pltpu.VMEM((PXN + 1,) + slab, BF16),
        pltpu.VMEM((128, 4, 128), F32),
        pltpu.VMEM((128, 4, 128), F32),
        pltpu.VMEM((128, 48, 128), F32),
        pltpu.VMEM((128, 48, 128), F32),
        pltpu.VMEM((192, 64 // GROUPS * 128), BF16),
        pltpu.VMEM((256, NX, 128), F32),
        pltpu.VMEM((512, NX * 128), BF16),
        pltpu.VMEM((256, NX * 128), BF16),
        pltpu.VMEM((PXN // 2, 256, 512), BF16),
        pltpu.VMEM((128, 4, 128), F32),
        pltpu.VMEM((128, 4, 128), F32),
        pltpu.VMEM((128, NX * 128), BF16),
        pltpu.VMEM((1024, NX * 128), BF16),
        pltpu.VMEM((NX, KREQ, 128), BF16),
        pltpu.VMEM((NX, 128), jnp.int32),
        pltpu.VMEM((NX,) + slab, F32),
        pltpu.VMEM((NX,) + slab, F32),
        pltpu.VMEM((NX,) + slab, F32),
        pltpu.VMEM((NX,) + slab, F32),
        pltpu.VMEM((PXN,) + slab, F32),
        pltpu.VMEM((PXN,) + slab, F32),
        pltpu.VMEM((NX,) + slab, F32),
        pltpu.VMEM((128, 256), F32),
        pltpu.VMEM((256, 128), jnp.int32),
        pltpu.SemaphoreType.DMA((7,)),
        pltpu.SemaphoreType.DMA((2,)),
        pltpu.SemaphoreType.DMA,
        pltpu.SemaphoreType.DMA((GROUPS,)),
        pltpu.SemaphoreType.DMA,
        pltpu.SemaphoreType.DMA((GROUPS,)),
        pltpu.SemaphoreType.DMA,
        pltpu.SemaphoreType.DMA,
        pltpu.SemaphoreType.DMA((4, 4)),
        pltpu.SemaphoreType.DMA((4, 4)),
    ]
    return pl.pallas_call(
        step_kernel,
        out_shape=(
            jax.ShapeDtypeStruct(nest_field.shape, F32),
            jax.ShapeDtypeStruct(parent_field.shape, F32),
            jax.ShapeDtypeStruct((1,), jnp.int32),
        ),
        in_specs=[smem] + [hbm] * 4 + [vmem] * 4 + [hbm] * 3 + [vmem] * 3,
        out_specs=(hbm, hbm, smem),
        scratch_shapes=scratch,
        compiler_params=pltpu.CompilerParams(
            collective_id=0, has_side_effects=True, vmem_limit_bytes=56 * 2**20
        ),
        name="step",
    )(
        send_slots[0],
        nest_field,
        courant_x,
        courant_y,
        courant_z,
        terrain,
        relax,
        interp_index,
        interp_weight,
        parent_field,
        parent_cx,
        parent_cy,
        jnp.transpose(fb_index, (2, 0, 1)),
        fb_slot,
        fb_target,
    )


def hand_over(nest_ref, parent_ref, nest_out, parent_out, nest_buf, parent_buf, come, go):
    arriving, leaving = [], []
    for part in range(4):
        rows = pl.ds(24 * part, 24)
        for k, (source, held, target) in enumerate(
            ((nest_ref, nest_buf, nest_out), (parent_ref, parent_buf, parent_out))
        ):
            arriving.append(
                pltpu.make_async_copy(source.at[rows], held.at[rows], come.at[k, part])
            )
            leaving.append(pltpu.make_async_copy(held.at[rows], target.at[rows], go.at[k, part]))
    for copy in arriving:
        copy.start()
    for first, second in zip(arriving, leaving):
        first.wait()
        second.start()
    for copy in leaving:
        copy.wait()


def handed(nest_out, parent_out):
    hbm = pl.BlockSpec(memory_space=pl.ANY)
    return pl.pallas_call(
        hand_over,
        out_shape=(
            jax.ShapeDtypeStruct(nest_out.shape, F32),
            jax.ShapeDtypeStruct(parent_out.shape, F32),
        ),
        in_specs=[hbm, hbm],
        out_specs=(hbm, hbm),
        scratch_shapes=[
            pltpu.VMEM(nest_out.shape, F32),
            pltpu.VMEM(parent_out.shape, F32),
            pltpu.SemaphoreType.DMA((2, 4)),
            pltpu.SemaphoreType.DMA((2, 4)),
        ],
        compiler_params=pltpu.CompilerParams(vmem_limit_bytes=16 * 2**20),
        name="hand_over",
    )(nest_out, parent_out)


def on_device(*args):
    nest_out, parent_out, flags = fused_step(*args)
    return lax.cond(
        flags[0] > 0, lambda: dense_step(*args), lambda: handed(nest_out, parent_out)
    )


def solution(mesh):
    in_specs = (
        P(None, "gx", "gy"),
        P(None, "gx", "gy"),
        P(None, "gx", "gy"),
        P(None, "gx", "gy"),
        P("gx", "gy"),
        P("gx", "gy"),
        P(None, "gx", "gy"),
        P(None, "gx", "gy"),
        P(("gx", "gy"), None),
        P(None, "gx", "gy"),
        P(None, "gx", "gy"),
        P(None, "gx", "gy"),
        P(("gx", "gy"), None, None),
        P(("gx", "gy"), None),
        P(("gx", "gy"), None),
    )
    out_specs = (P(None, "gx", "gy"), P(None, "gx", "gy"))
    return jax.shard_map(
        on_device, mesh=mesh, in_specs=in_specs, out_specs=out_specs, check_vma=False
    )
```

```python
import functools

import jax
import jax.numpy as jnp
from jax import lax
from jax.experimental import pallas as pl
from jax.experimental.pallas import tpu as pltpu
from jax.sharding import PartitionSpec as P

TILE = 128
CAP = 2
FCAP = 4
SUBSTEPS = 3


blend_rate = 0.5


def extended(block, sides, width):
    for axis, dim in sides:
        count = lax.axis_size(axis)
        forward = [(i, i + 1) for i in range(count - 1)]
        backward = [(target, source) for source, target in forward]
        low = lax.ppermute(
            lax.slice_in_dim(block, block.shape[dim] - width, None, axis=dim), axis, forward
        )
        high = lax.ppermute(lax.slice_in_dim(block, 0, width, axis=dim), axis, backward)
        block = jnp.concatenate([low, block, high], axis=dim)
    return block


def upwind(padded, field, cx, cy):
    west = padded[:, :-2, 1:-1]
    east = padded[:, 2:, 1:-1]
    south = padded[:, 1:-1, :-2]
    north = padded[:, 1:-1, 2:]
    return cx * jnp.where(cx > 0, field - west, east - field) + cy * jnp.where(
        cy > 0, field - south, north - field
    )


def vertical(field, cz, mask):
    below = jnp.concatenate([field[:1], field[:-1]], axis=0)
    mask_below = jnp.concatenate([jnp.zeros_like(mask[:1]), mask[:-1]], axis=0)
    below = jnp.where(mask_below, below, field)
    above = jnp.concatenate([field[1:], field[-1:]], axis=0)
    return cz * jnp.where(cz > 0, field - below, above - field)


def dense_step(
    nest_field,
    courant_x,
    courant_y,
    courant_z,
    terrain,
    relax,
    interp_index,
    interp_weight,
    send_slots,
    parent_field,
    parent_cx,
    parent_cy,
    fb_index,
    fb_slot,
    fb_target,
):
    n_east = lax.axis_size("gx")
    n_north = lax.axis_size("gy")
    devices = n_east * n_north
    levels, nest_x, nest_y = nest_field.shape
    parent_x, parent_y = (parent_field.shape[1], parent_field.shape[2])
    parent_cols = parent_x * parent_y
    nest_cols = nest_x * nest_y
    slabs = parent_field
    slabs = jnp.concatenate([slabs, jnp.zeros((levels, 1, TILE), jnp.float32)], axis=1)
    picked = jnp.take(slabs, send_slots[0], axis=1)
    outgoing = picked.reshape(levels, devices, CAP, TILE)
    incoming = lax.all_to_all(outgoing, ("gx", "gy"), split_axis=1, concat_axis=1, tiled=True)
    received_cols = incoming.reshape(levels, -1).T
    padded_parent = extended(parent_field, (("gx", 1), ("gy", 2)), 1)
    advected = parent_field - upwind(padded_parent, parent_field, parent_cx, parent_cy)
    index_flat = interp_index.reshape(4, -1)
    weight_flat = interp_weight.reshape(4, -1)
    boundary_cols = weight_flat[0][:, None] * jnp.take(received_cols, index_flat[0], axis=0)
    for j in range(1, 4):
        boundary_cols = boundary_cols + weight_flat[j][:, None] * jnp.take(
            received_cols, index_flat[j], axis=0
        )
    boundary = boundary_cols.T.reshape(levels, nest_x, nest_y)
    level_ids = lax.broadcasted_iota(jnp.int32, (levels, 1, 1), 0)
    mask = level_ids >= terrain[None]
    field = jnp.where(mask, nest_field, 0.0)
    for step in range(SUBSTEPS):
        padded = extended(field, (("gx", 1), ("gy", 2)), 1)
        adv = field - upwind(padded, field, courant_x, courant_y) - vertical(field, courant_z, mask)
        field = jnp.where(mask, adv + relax[None] * (boundary - adv), 0.0)
    flat_nest = field.reshape(levels, nest_cols)
    row_count = fb_index.shape[1]
    averaged = fb_index.shape[2]
    row_ids = lax.broadcasted_iota(jnp.int32, (row_count, averaged), 0)
    averaging = jnp.zeros((row_count + 1, nest_cols), jnp.float32)
    averaging = averaging.at[row_ids, fb_index[0]].add(1.0 / averaged)
    slot_weights = jnp.take(averaging, fb_slot[0], axis=0)
    chosen_rows = lax.dot_general(
        slot_weights,
        flat_nest,
        (((1,), (1,)), ((), ())),
        precision=lax.Precision.HIGHEST,
        preferred_element_type=jnp.float32,
    )
    sending = chosen_rows.reshape(devices, FCAP * levels)
    arrived = lax.all_to_all(sending, ("gx", "gy"), split_axis=0, concat_axis=0, tiled=True)
    values = arrived.reshape(-1, levels)
    flat_parent = advected.reshape(levels, parent_cols)
    target = fb_target[0]
    current = jnp.take(flat_parent, jnp.minimum(target, parent_cols - 1), axis=1)
    delta = blend_rate * (values.T - current)
    updated = flat_parent.at[:, target].add(delta, mode="drop")
    return (field, updated.reshape(levels, parent_x, parent_y))


MESH = pl.DeviceIdType.MESH
LEV = 96
NX = 16
PXN = 32
KREQ = 64
GROUPS = 8
F32 = jnp.float32
BF16 = jnp.bfloat16
NT = (((1,), (1,)), ((), ()))


def halves(value):
    high = value.astype(BF16)
    return high, (value - high.astype(F32)).astype(BF16)


def step_kernel(
    slots_ref,
    nest_ref,
    cx_ref,
    cy_ref,
    cz_ref,
    terrain_ref,
    relax_ref,
    index_ref,
    weight_ref,
    parent_ref,
    pcx_ref,
    pcy_ref,
    fbi_ref,
    fbs_ref,
    fbt_ref,
    nest_out,
    keep_out,
    rows_out,
    flag_out,
    q0,
    q1,
    q2,
    ybuf,
    ypack,
    adv1,
    bound,
    pq,
    pys,
    pyk,
    keep,
    shi,
    slo,
    req,
    reqin,
    ans,
    ansin,
    xmat,
    counts,
    cmat,
    qmat,
    fbsend,
    fbin,
    hotm,
    tabm,
    rankm,
    relm,
    nraw,
    cxs,
    cys,
    czs,
    pcxs,
    pcys,
    nres,
    fbt,
    fbn,
    sem_in,
    sem_out,
    sem_req_s,
    sem_req_r,
    sem_ans_s,
    sem_ans_r,
    sem_fb_s,
    sem_fb_r,
    hs,
    hr,
):
    gx = lax.axis_index("gx")
    gy = lax.axis_index("gy")
    mz, my, mx, mc = lax.div(gx, 4), lax.rem(gx, 4), lax.div(gy, 2), lax.rem(gy, 2)
    me = gx * 8 + gy

    def chip(n, sign):
        dx = lax.rem(n, 4)
        dy = lax.rem(lax.div(n, 4) + dx, 4)
        dz = lax.rem(lax.div(n, 16) + dy, 4)
        if sign < 0:
            dz, dy, dx = 4 - dz, 4 - dy, 4 - dx
        z, y, x = lax.rem(mz + dz, 4), lax.rem(my + dy, 4), lax.rem(mx + dx, 4)
        return z * 4 + y, x * 2

    barrier = pltpu.get_barrier_semaphore()

    zs = [lax.rem(mz + k, 4) * 4 for k in range(4)]
    ys = [lax.rem(my + k, 4) for k in range(4)]
    xs = [lax.rem(mx + k, 4) * 2 for k in range(4)]

    def ahead(n):
        dx = n % 4
        dy = (n // 4 + dx) % 4
        dz = (n // 16 + dy) % 4
        return zs[dz] + ys[dy], xs[dx]

    for n in range(1, 64):
        tx, ty = ahead(n)
        for core in range(2):
            pl.semaphore_signal(barrier, inc=1, device_id=(tx, ty + core), device_id_type=MESH)
    pl.semaphore_signal(barrier, inc=1, device_id=(gx, mx * 2 + 1 - mc), device_id_type=MESH)

    def load(source, count, target, first, k):
        def one(x, carry):
            pltpu.make_async_copy(source.at[:, x], target.at[x + first], sem_in.at[k]).start()
            return carry

        lax.fori_loop(0, count, one, 0)

    def loaded(target, first, count, k):
        part = target.at[pl.ds(first, count)]
        pltpu.make_async_copy(part, part, sem_in.at[k]).wait()

    sub128 = lax.broadcasted_iota(jnp.int32, (128, 128), 0)
    lane128 = lax.broadcasted_iota(jnp.int32, (128, 128), 1)
    sub64 = lax.broadcasted_iota(jnp.int32, (KREQ, 128), 0)

    before = jnp.concatenate(
        [jnp.where(sub128 < lane128, 1.0, 0.0), jnp.ones((128, 128), F32)], axis=1
    ).astype(BF16)
    run = jnp.zeros((128, 128), F32)
    top = jnp.zeros((1, 128), F32)
    for x in range(NX):
        idx = [index_ref[j, x : x + 1, :] for j in range(4)]
        src = idx[0] >> 8
        dz, dy, dx = (src >> 5) - mz, ((src >> 3) & 3) - my, ((src >> 1) & 3) - mx
        rel = (((dz - dy) & 3) << 5) | (((dy - dx) & 3) << 3) | ((dx & 3) << 1) | (src & 1)
        relm[x : x + 1, :] = rel
        hot = jnp.where(sub128 == rel, 1.0, 0.0)
        hotb = hot.astype(BF16)
        both = jnp.dot(hotb, before, preferred_element_type=F32)
        rank = jnp.sum(hot * (both[:, :128] + run), axis=0, keepdims=True)
        run = run + both[:, 128:]
        top = jnp.maximum(top, rank)
        here = sub64 == rank.astype(jnp.int32)
        rankm[x] = jnp.where(here, 1.0, 0.0).astype(BF16)
        at = slice(128 * x, 128 * x + 128)
        hotm[:, at] = hotb
        for j in range(4):
            low = (idx[j] & 255).astype(F32)
            w = weight_ref[j, x : x + 1, :]
            whi = w.astype(BF16).astype(F32)
            tabm[128 * j : 128 * j + 64, at] = jnp.where(here, low, 0.0).astype(BF16)
            tabm[128 * j + 64 : 128 * j + 128, at] = jnp.where(here, whi, 0.0).astype(BF16)
            tabm[512 + 128 * j : 576 + 128 * j, at] = jnp.zeros((KREQ, 128), BF16)
            tabm[576 + 128 * j : 640 + 128 * j, at] = jnp.where(here, w - whi, 0.0).astype(BF16)
    flag = jnp.max(jnp.where(top >= KREQ, 1.0, 0.0), axis=1, keepdims=True)
    racc = lax.dot_general(hotm[...], tabm[...], NT, preferred_element_type=F32)
    for j in range(4):
        req[:, j, :] = (
            racc[:, 128 * j : 128 * j + 128] + racc[:, 512 + 128 * j : 640 + 128 * j]
        )

    load(parent_ref, PXN, pq, 1, 0)
    load(nest_ref, NX, nraw, 0, 1)
    pl.semaphore_wait(barrier, 127)

    for n in range(1, 64):
        tx, ty = ahead(n)
        for core in range(2):
            pltpu.make_async_remote_copy(
                src_ref=req.at[2 * n + core],
                dst_ref=reqin.at[2 * n + mc],
                send_sem=sem_req_s,
                recv_sem=sem_req_r.at[n // (64 // GROUPS)],
                device_id=(tx, ty + core),
                device_id_type=MESH,
            ).start()
    pltpu.make_async_remote_copy(
        src_ref=req.at[1 - mc],
        dst_ref=reqin.at[mc],
        send_sem=sem_req_s,
        recv_sem=sem_req_r.at[0],
        device_id=(gx, mx * 2 + 1 - mc),
        device_id_type=MESH,
    ).start()
    pltpu.make_async_copy(req.at[mc], reqin.at[mc], sem_req_r.at[0]).start()

    load(cx_ref, NX, cxs, 0, 2)
    load(cy_ref, NX, cys, 0, 3)
    load(cz_ref, NX, czs, 0, 4)
    load(pcx_ref, PXN, pcxs, 0, 5)
    load(pcy_ref, PXN, pcys, 0, 6)

    lev = lax.broadcasted_iota(jnp.int32, (LEV, 128), 0)
    lane = lax.broadcasted_iota(jnp.int32, (LEV, 128), 1)

    def edge_copies(field, count, packed, landing, at):
        def face(x):
            return field.at[x, pl.ds(8, LEV)] if count == NX else field.at[x]

        west = (gx > 0, face(1), face(count + 1), (gx - 1, gy))
        east = (gx < 15, face(count), face(0), (gx + 1, gy))
        south = (gy > 0, packed.at[0], landing.at[1], (gx, gy - 1))
        north = (gy < 7, packed.at[1], landing.at[0], (gx, gy + 1))
        made = []
        for k, (has, src, dst, target) in enumerate((west, east, south, north)):
            made.append(
                (
                    has,
                    pltpu.make_async_remote_copy(
                        src_ref=src,
                        dst_ref=dst,
                        send_sem=hs.at[at, k],
                        recv_sem=hr.at[at, k],
                        device_id=target,
                        device_id_type=MESH,
                    ),
                )
            )
        return made

    def edges_start(made):
        for has, copy in made:
            pl.when(has)(copy.start)

    def edges_wait(made):
        for k, other in ((0, 1), (1, 0), (2, 3), (3, 2)):
            pl.when(made[other][0])(made[k][1].wait_recv)

    def edges_sent(made):
        for has, copy in made:
            pl.when(has)(copy.wait_send)

    def clear_edges(field, count, landing):
        zero = jnp.zeros((LEV, 128), F32)

        @pl.when(gx == 0)
        def _():
            field[0, pl.ds(8 if count == NX else 0, LEV), :] = zero

        @pl.when(gx == 15)
        def _():
            field[count + 1, pl.ds(8 if count == NX else 0, LEV), :] = zero

        @pl.when(gy == 0)
        def _():
            landing[0] = zero

        @pl.when(gy == 7)
        def _():
            landing[1] = zero

    def pack_edges(field, count, packed):
        base = 8 if count == NX else 0

        def one(x, carry):
            low, high = carry
            here = field[x + 1, pl.ds(base, LEV), :]
            low = jnp.where(lane == x, pltpu.roll(here, x, 1), low)
            high = jnp.where(lane == x, pltpu.roll(here, x + 1, 1), high)
            return low, high

        zero = jnp.zeros((LEV, 128), F32)
        low, high = lax.fori_loop(0, count, one, (zero, zero), unroll=16)
        packed[0] = low
        packed[1] = high

    deep = 32
    lanec = lax.broadcasted_iota(jnp.int32, (deep, 128), 1)
    levc = lax.broadcasted_iota(jnp.int32, (deep, 128), 0)

    def across(field, base, x, l0, landing, cx, cy):
        rows = pl.ds(base + l0, deep)
        here = field[x + 1, rows, :]
        west, east = field[x, rows, :], field[x + 2, rows, :]
        edge = pl.ds(l0, deep)
        south = jnp.where(
            lanec == 0,
            pltpu.roll(landing[0, edge, :], lax.rem(128 - x, 128), 1),
            pltpu.roll(here, 1, 1),
        )
        north = jnp.where(
            lanec == 127, pltpu.roll(landing[1, edge, :], 127 - x, 1), pltpu.roll(here, 127, 1)
        )
        return here, here - cx * jnp.where(cx > 0, here - west, east - here) - cy * jnp.where(
            cy > 0, here - south, north - here
        )

    def advance(field, x, l0, landing):
        edge = pl.ds(l0, deep)
        here, adv = across(field, 8, x, l0, landing, cxs[x, edge, :], cys[x, edge, :])
        cz = czs[x, edge, :]
        lower, upper = field[x + 1, pl.ds(7 + l0, deep), :], field[x + 1, pl.ds(9 + l0, deep), :]
        below = jnp.where(levc + (l0 - 1) >= terrain_ref[pl.ds(x, 1), :], lower, here)
        above = jnp.where(levc == LEV - 1 - l0, here, upper)
        return adv - cz * jnp.where(cz > 0, here - below, above - here)

    clear_edges(pq, PXN, pys)
    clear_edges(q0, NX, ybuf.at[0])
    clear_edges(q1, NX, ybuf.at[1])
    clear_edges(q2, NX, ybuf.at[2])

    blank8 = jnp.zeros((8, 128), F32)
    loaded(nraw, 0, NX, 1)

    def start_nest(x, carry):
        for field in (q0, q1, q2):
            field[x + 1, 0:8, :] = blank8
            field[x + 1, LEV + 8 : LEV + 16, :] = blank8
        q0[x + 1, 8 : LEV + 8, :] = jnp.where(lev >= terrain_ref[pl.ds(x, 1), :], nraw[x], 0.0)
        return carry

    lax.fori_loop(0, NX, start_nest, 0)
    pack_edges(q0, NX, ypack.at[0])
    q0_edges = edge_copies(q0, NX, ypack.at[0], ybuf.at[0], 0)
    edges_start(q0_edges)

    loaded(pq, 1, PXN, 0)

    def split(x, carry):
        shi[x], slo[x] = halves(pq[x + 1])
        return carry

    lax.fori_loop(0, PXN, split, 0, unroll=2)
    shi[PXN] = jnp.zeros((LEV, 128), BF16)
    slo[PXN] = jnp.zeros((LEV, 128), BF16)
    pack_edges(pq, PXN, pyk)
    p_edges = edge_copies(pq, PXN, pyk, pys, 1)
    edges_start(p_edges)


    def asked(g):
        part = reqin.at[pl.ds(g * (128 // GROUPS), 128 // GROUPS)]
        pltpu.make_async_copy(part, part, sem_req_r.at[g]).wait()

    sub256 = lax.broadcasted_iota(jnp.int32, (256, 128), 0)
    left48 = lax.broadcasted_iota(jnp.int32, (48, 128), 1) < 64
    left4 = lax.broadcasted_iota(jnp.int32, (4, 128), 1) < 64

    def answer(n, tx, ty):
        a, b = reqin[2 * n], reqin[2 * n + 1]
        place = jnp.where(left4, a, pltpu.roll(b, 64, 1)).astype(jnp.int32)
        amount = jnp.where(left4, pltpu.roll(a, 64, 1), b)
        table = jnp.zeros((256, 128), F32)
        for j in range(4):
            table = jnp.where(sub256 == place[j : j + 1], amount[j : j + 1], table)
        right = jnp.concatenate(halves(table), axis=1)
        base = (tx * 8 + ty) * 2
        rows = []
        for core in range(2):
            first, second = slots_ref[base + 2 * core], slots_ref[base + 2 * core + 1]
            rows.append(jnp.concatenate([shi[first], shi[second]], axis=1))
            rows.append(jnp.concatenate([slo[first], slo[second]], axis=1))
        out = jnp.dot(jnp.concatenate(rows, axis=0), right, preferred_element_type=F32)
        v0 = out[0:96, :128] + out[0:96, 128:] + out[96:192, :128]
        v1 = out[192:288, :128] + out[192:288, 128:] + out[288:384, :128]
        return (
            jnp.where(left48, v0[:48], pltpu.roll(v0[48:], 64, 1)),
            jnp.where(left48, pltpu.roll(v1[:48], 64, 1), v1[48:]),
        )

    def reply(base, count):
        places = [chip(base + u, -1) for u in range(count)]
        made = [answer(base + u, *places[u]) for u in range(count)]
        for u in range(count):
            ans[2 * (base + u)], ans[2 * (base + u) + 1] = made[u]
        for u in range(count):
            n = base + u
            tx, ty = places[u]
            for core in range(2):
                pltpu.make_async_remote_copy(
                    src_ref=ans.at[2 * n + core],
                    dst_ref=ansin.at[2 * n + mc],
                    send_sem=sem_ans_s,
                    recv_sem=sem_ans_r.at[lax.div(n, 64 // GROUPS)],
                    device_id=(tx, ty + core),
                    device_id_type=MESH,
                ).start()

    def replies(r, carry):
        asked(r)
        reply(8 * r, 4)
        reply(8 * r + 4, 4)
        return carry

    asked(0)
    ans[0], ans[1] = answer(0, gx, mx * 2)
    pltpu.make_async_remote_copy(
        src_ref=ans.at[1 - mc],
        dst_ref=ansin.at[mc],
        send_sem=sem_ans_s,
        recv_sem=sem_ans_r.at[0],
        device_id=(gx, mx * 2 + 1 - mc),
        device_id_type=MESH,
    ).start()
    pltpu.make_async_copy(ans.at[mc], ansin.at[mc], sem_ans_r.at[0]).start()
    reply(jnp.int32(1), 3)
    reply(jnp.int32(4), 4)
    lax.fori_loop(1, GROUPS, replies, 0)

    for k, (target, count) in enumerate(
        ((cxs, NX), (cys, NX), (czs, NX), (pcxs, PXN), (pcys, PXN))
    ):
        loaded(target, 0, count, k + 2)
    edges_wait(q0_edges)
    chunks = range(0, LEV, deep)

    def first_nest(x, carry):
        for l0 in chunks:
            adv1[x, pl.ds(l0, deep), :] = advance(q0, x, l0, ybuf.at[0])
        bound[x] = jnp.zeros((LEV, 128), F32)
        return carry

    lax.fori_loop(0, NX, first_nest, 0)

    edges_wait(p_edges)
    sub512 = lax.broadcasted_iota(jnp.int32, (256, 512), 0)
    ones8 = jnp.ones((8, 512), BF16)

    def parents(i, carry):
        hot = jnp.where(sub512 == fbt_ref[...] - 256 * i, 1.0, 0.0).astype(BF16)
        left = 1.0 - 0.5 * lax.dot_general(ones8, hot, NT, preferred_element_type=F32)[0:1]
        for k in range(2):
            x = 2 * i + k
            for l0 in chunks:
                edge = pl.ds(l0, deep)
                moved = across(pq, 0, x, l0, pys, pcxs[x, edge, :], pcys[x, edge, :])[1]
                keep[x, edge, :] = moved * left[:, 128 * k : 128 * k + 128]
        return carry

    lax.fori_loop(0, PXN // 2, parents, 0)
    pltpu.make_async_copy(keep, keep_out, sem_out.at[1]).start()

    sub16 = lax.broadcasted_iota(jnp.int32, (16, 128), 0)

    fbt[...] = jnp.full((128, 256), -1.0, F32)

    def turn(i, carry):
        fbt[pl.ds(i, 1), :] = fbi_ref[i].astype(F32)
        return carry

    lax.fori_loop(0, 81, turn, 0)
    fbn[...] = jnp.transpose(fbt[...]).astype(jnp.int32)

    def count(r, carry):
        made = []
        for u in range(8):
            highs, lows = [], []
            for k in range(2):
                row = fbn[pl.ds(16 * r + 2 * u + k, 1), :]
                high = jnp.where(sub16 == (row >> 7), 1.0, 0.0).astype(BF16)
                blank = jnp.zeros((16, 128), BF16)
                highs.append(jnp.concatenate([high, blank] if k == 0 else [blank, high], axis=1))
                lows.append(jnp.where(sub128 == (row & 127), 1.0, 0.0).astype(BF16))
            made.append(
                lax.dot_general(
                    jnp.concatenate(highs, axis=0),
                    jnp.concatenate(lows, axis=1),
                    NT,
                    preferred_element_type=F32,
                )
            )
        for u in range(8):
            counts[16 * r + 2 * u] = made[u][:16]
            counts[16 * r + 2 * u + 1] = made[u][16:]
        return carry

    lax.fori_loop(0, 16, count, 0)
    row256 = lax.broadcasted_iota(jnp.int32, (256, 512), 0)
    chosen = jnp.transpose(jnp.where(row256 == fbs_ref[...], 1.0, 0.0)).astype(BF16)
    for x in range(NX):
        cmat[:, 128 * x : 128 * x + 128] = jnp.dot(
            chosen, counts[:, x, :].astype(BF16), preferred_element_type=F32
        ).astype(BF16)
    qmat[...] = jnp.zeros_like(qmat)


    per = 64 // GROUPS
    for g in range(GROUPS):
        part = ansin.at[pl.ds(2 * per * g, 2 * per)]
        pltpu.make_async_copy(part, part, sem_ans_r.at[g]).wait()
        for i in range(per):
            a, b = ansin[2 * (per * g + i)], ansin[2 * (per * g + i) + 1]
            upper = jnp.where(left48, a, pltpu.roll(b, 64, 1))
            lower = jnp.where(left48, pltpu.roll(a, 64, 1), b)
            high, low = halves(jnp.concatenate([upper, lower], axis=0))
            xmat[0:96, 128 * i : 128 * i + 128] = high
            xmat[96:192, 128 * i : 128 * i + 128] = low

        def pick(x, carry, g=g):
            hots = []
            for k in range(2):
                owner = jnp.broadcast_to(relm[pl.ds(2 * x + k, 1), :], (16, 128))
                ranks = rankm[2 * x + k]
                blocks = []
                for i in range(2 * per):
                    mine = jnp.where(owner == 2 * per * g + i, 1.0, 0.0).astype(BF16)
                    blocks.append(ranks * jnp.concatenate([mine] * (KREQ // 16), axis=0))
                hots.append(jnp.concatenate(blocks, axis=0))
            got = jnp.dot(xmat[...], jnp.concatenate(hots, axis=1), preferred_element_type=F32)
            bound[2 * x] += got[:96, :128] + got[96:, :128]
            bound[2 * x + 1] += got[:96, 128:] + got[96:, 128:]
            return carry

        lax.fori_loop(0, NX // 2, pick, 0, unroll=4)

    def settle(x, l0, adv):
        terrain = terrain_ref[pl.ds(x, 1), :]
        rel = relax_ref[pl.ds(x, 1), :]
        pull = bound[x, pl.ds(l0, deep), :] - adv
        return jnp.where(levc + l0 >= terrain, adv + rel * pull, 0.0)

    def first_settle(x, carry):
        for l0 in chunks:
            q1[x + 1, pl.ds(8 + l0, deep), :] = settle(x, l0, adv1[x, pl.ds(l0, deep), :])
        return carry

    lax.fori_loop(0, NX, first_settle, 0)
    edges = [q0_edges, p_edges]

    def exchange(now, step):
        pack_edges(now, NX, ypack.at[step])
        made = edge_copies(now, NX, ypack.at[step], ybuf.at[step], step + 1)
        edges_start(made)
        edges_wait(made)
        edges.append(made)

    exchange(q1, 1)

    def second(x, carry):
        for l0 in chunks:
            q2[x + 1, pl.ds(8 + l0, deep), :] = settle(x, l0, advance(q1, x, l0, ybuf.at[1]))
        return carry

    lax.fori_loop(0, NX, second, 0, unroll=4)
    exchange(q2, 2)

    def third(x, carry):
        at = pl.ds(pl.multiple_of(128 * x, 128), 128)
        for l0 in chunks:
            value = settle(x, l0, advance(q2, x, l0, ybuf.at[2]))
            nres[x, pl.ds(l0, deep), :] = value
            high, low = halves(value)
            qmat[pl.ds(l0, deep), at] = high
            qmat[pl.ds(128 + l0, deep), at] = low
        return carry

    lax.fori_loop(0, NX, third, 0, unroll=4)

    got = lax.dot_general(cmat[...], qmat[...], NT, preferred_element_type=F32)
    rows = (got[:, :128] + got[:, 128:]) * (1.0 / 81.0)
    lane512 = lax.broadcasted_iota(jnp.int32, (512, 128), 1)
    rows = jnp.where(lane512 == LEV, flag, rows)
    fbsend[...] = rows.reshape(128, 4, 128)

    for n in range(1, 64):
        tx, ty = ahead(n)
        for core in range(2):
            pltpu.make_async_remote_copy(
                src_ref=fbsend.at[tx * 8 + ty + core],
                dst_ref=fbin.at[me],
                send_sem=sem_fb_s,
                recv_sem=sem_fb_r,
                device_id=(tx, ty + core),
                device_id_type=MESH,
            ).start()
    other = mx * 2 + 1 - mc
    pltpu.make_async_remote_copy(
        src_ref=fbsend.at[gx * 8 + other],
        dst_ref=fbin.at[me],
        send_sem=sem_fb_s,
        recv_sem=sem_fb_r,
        device_id=(gx, other),
        device_id_type=MESH,
    ).start()
    pltpu.make_async_copy(fbsend.at[me], fbin.at[me], sem_fb_r).start()

    def store_nest(x, carry):
        pltpu.make_async_copy(nres.at[x], nest_out.at[:, x], sem_out.at[0]).start()
        return carry

    lax.fori_loop(0, NX, store_nest, 0)
    pltpu.make_async_copy(fbin, fbin, sem_fb_r).wait()


    pltpu.make_async_copy(fbin, rows_out, sem_out.at[2]).start()
    values = fbin[...].reshape(512, 128)
    worst = jnp.max(jnp.where(lane512 == LEV, values, 0.0))
    flag_out[0] = jnp.where(worst > 0.5, 1, 0)
    pltpu.make_async_copy(nres, nres, sem_out.at[0]).wait()
    pltpu.make_async_copy(keep, keep_out, sem_out.at[1]).wait()
    pltpu.make_async_copy(fbin, rows_out, sem_out.at[2]).wait()

    for buffer, sem in ((req, sem_req_s), (ans, sem_ans_s), (fbsend, sem_fb_s)):
        part = buffer.at[pl.ds(0, 127)]
        pltpu.make_async_copy(part, part, sem).wait()
    for made in edges:
        edges_sent(made)


def fused_step(
    nest_field,
    courant_x,
    courant_y,
    courant_z,
    terrain,
    relax,
    interp_index,
    interp_weight,
    send_slots,
    parent_field,
    parent_cx,
    parent_cy,
    fb_index,
    fb_slot,
    fb_target,
):
    vmem = pl.BlockSpec(memory_space=pltpu.VMEM)
    smem = pl.BlockSpec(memory_space=pltpu.SMEM)
    hbm = pl.BlockSpec(memory_space=pl.ANY)
    slab = (LEV, 128)
    scratch = [
        pltpu.VMEM((NX + 2, LEV + 16, 128), F32),
        pltpu.VMEM((NX + 2, LEV + 16, 128), F32),
        pltpu.VMEM((NX + 2, LEV + 16, 128), F32),
        pltpu.VMEM((3, 2) + slab, F32),
        pltpu.VMEM((3, 2) + slab, F32),
        pltpu.VMEM((NX,) + slab, F32),
        pltpu.VMEM((NX,) + slab, F32),
        pltpu.VMEM((PXN + 2,) + slab, F32),
        pltpu.VMEM((2,) + slab, F32),
        pltpu.VMEM((2,) + slab, F32),
        pltpu.VMEM((PXN,) + slab, F32),
        pltpu.VMEM((PXN + 1,) + slab, BF16),
        pltpu.VMEM((PXN + 1,) + slab, BF16),
        pltpu.VMEM((128, 4, 128), F32),
        pltpu.VMEM((128, 4, 128), F32),
        pltpu.VMEM((128, 48, 128), F32),
        pltpu.VMEM((128, 48, 128), F32),
        pltpu.VMEM((192, 64 // GROUPS * 128), BF16),
        pltpu.VMEM((256, NX, 128), F32),
        pltpu.VMEM((512, NX * 128), BF16),
        pltpu.VMEM((256, NX * 128), BF16),
        pltpu.VMEM((128, 4, 128), F32),
        pltpu.VMEM((128, 4, 128), F32),
        pltpu.VMEM((128, NX * 128), BF16),
        pltpu.VMEM((1024, NX * 128), BF16),
        pltpu.VMEM((NX, KREQ, 128), BF16),
        pltpu.VMEM((NX, 128), jnp.int32),
        pltpu.VMEM((NX,) + slab, F32),
        pltpu.VMEM((NX,) + slab, F32),
        pltpu.VMEM((NX,) + slab, F32),
        pltpu.VMEM((NX,) + slab, F32),
        pltpu.VMEM((PXN,) + slab, F32),
        pltpu.VMEM((PXN,) + slab, F32),
        pltpu.VMEM((NX,) + slab, F32),
        pltpu.VMEM((128, 256), F32),
        pltpu.VMEM((256, 128), jnp.int32),
        pltpu.SemaphoreType.DMA((7,)),
        pltpu.SemaphoreType.DMA((3,)),
        pltpu.SemaphoreType.DMA,
        pltpu.SemaphoreType.DMA((GROUPS,)),
        pltpu.SemaphoreType.DMA,
        pltpu.SemaphoreType.DMA((GROUPS,)),
        pltpu.SemaphoreType.DMA,
        pltpu.SemaphoreType.DMA,
        pltpu.SemaphoreType.DMA((4, 4)),
        pltpu.SemaphoreType.DMA((4, 4)),
    ]
    return pl.pallas_call(
        step_kernel,
        out_shape=(
            jax.ShapeDtypeStruct(nest_field.shape, F32),
            jax.ShapeDtypeStruct((PXN,) + slab, F32),
            jax.ShapeDtypeStruct((128, 4, 128), F32),
            jax.ShapeDtypeStruct((1,), jnp.int32),
        ),
        in_specs=[smem] + [hbm] * 4 + [vmem] * 4 + [hbm] * 3 + [vmem] * 3,
        out_specs=(hbm, hbm, hbm, smem),
        scratch_shapes=scratch,
        compiler_params=pltpu.CompilerParams(
            collective_id=0, has_side_effects=True, vmem_limit_bytes=56 * 2**20
        ),
        name="step",
    )(
        send_slots[0],
        nest_field,
        courant_x,
        courant_y,
        courant_z,
        terrain,
        relax,
        interp_index,
        interp_weight,
        parent_field,
        parent_cx,
        parent_cy,
        jnp.transpose(fb_index, (2, 0, 1)),
        fb_slot,
        fb_target,
    )


def finish_kernel(
    fbt_ref, rows_ref, nest_ref, keep_ref, nest_out, parent_out, nest_buf, keep, come, go
):
    per = PXN // 8
    arriving = []
    for part in range(8):
        xs = pl.ds(per * part, per)
        arriving.append(pltpu.make_async_copy(keep_ref.at[xs], keep.at[xs], come.at[0, part]))
        arriving[-1].start()
    nest = []
    for part in range(4):
        rows = pl.ds(24 * part, 24)
        nest.append(pltpu.make_async_copy(nest_ref.at[rows], nest_buf.at[rows], come.at[1, part]))
        nest[-1].start()
    sub512 = lax.broadcasted_iota(jnp.int32, (256, 512), 0)
    high, low = halves(jnp.transpose(rows_ref[...].reshape(512, 128))[:96])
    both = jnp.concatenate([high, low], axis=0)
    for i in range(PXN // 2):
        hot = jnp.where(sub512 == fbt_ref[...] - 256 * i, 1.0, 0.0).astype(BF16)
        got = lax.dot_general(both, hot, NT, preferred_element_type=F32)
        if 2 * i % per == 0:
            arriving[2 * i // per].wait()
        for k in range(2):
            x, at = 2 * i + k, slice(128 * k, 128 * k + 128)
            keep[x] += 0.5 * (got[:96, at] + got[96:, at])
            pltpu.make_async_copy(keep.at[x], parent_out.at[:, x], go.at[0]).start()
        if i < 4:
            nest[i].wait()
            rows = pl.ds(24 * i, 24)
            pltpu.make_async_copy(nest_buf.at[rows], nest_out.at[rows], go.at[1]).start()
    pltpu.make_async_copy(nest_buf, nest_buf, go.at[1]).wait()
    pltpu.make_async_copy(keep, keep, go.at[0]).wait()


def finish(fb_target, rows, nest, keep, parent_shape):
    vmem = pl.BlockSpec(memory_space=pltpu.VMEM)
    hbm = pl.BlockSpec(memory_space=pl.ANY)
    return pl.pallas_call(
        finish_kernel,
        out_shape=(
            jax.ShapeDtypeStruct(nest.shape, F32),
            jax.ShapeDtypeStruct(parent_shape, F32),
        ),
        in_specs=[vmem, vmem, hbm, hbm],
        out_specs=(hbm, hbm),
        scratch_shapes=[
            pltpu.VMEM(nest.shape, F32),
            pltpu.VMEM(keep.shape, F32),
            pltpu.SemaphoreType.DMA((2, 8)),
            pltpu.SemaphoreType.DMA((2,)),
        ],
        compiler_params=pltpu.CompilerParams(vmem_limit_bytes=24 * 2**20),
        name="finish",
    )(fb_target, rows, nest, keep)


def on_device(*args):
    nest, keep, rows, flags = fused_step(*args)
    return lax.cond(
        flags[0] > 0,
        lambda: dense_step(*args),
        lambda: finish(args[14], rows, nest, keep, args[9].shape),
    )


def solution(mesh):
    in_specs = (
        P(None, "gx", "gy"),
        P(None, "gx", "gy"),
        P(None, "gx", "gy"),
        P(None, "gx", "gy"),
        P("gx", "gy"),
        P("gx", "gy"),
        P(None, "gx", "gy"),
        P(None, "gx", "gy"),
        P(("gx", "gy"), None),
        P(None, "gx", "gy"),
        P(None, "gx", "gy"),
        P(None, "gx", "gy"),
        P(("gx", "gy"), None, None),
        P(("gx", "gy"), None),
        P(("gx", "gy"), None),
    )
    out_specs = (P(None, "gx", "gy"), P(None, "gx", "gy"))
    return jax.shard_map(
        on_device, mesh=mesh, in_specs=in_specs, out_specs=out_specs, check_vma=False
    )
```

```python
import functools

import jax
import jax.numpy as jnp
from jax import lax
from jax.experimental import pallas as pl
from jax.experimental.pallas import tpu as pltpu
from jax.sharding import PartitionSpec as P

TILE = 128
CAP = 2
FCAP = 4
SUBSTEPS = 3


blend_rate = 0.5


def extended(block, sides, width):
    for axis, dim in sides:
        count = lax.axis_size(axis)
        forward = [(i, i + 1) for i in range(count - 1)]
        backward = [(target, source) for source, target in forward]
        low = lax.ppermute(
            lax.slice_in_dim(block, block.shape[dim] - width, None, axis=dim), axis, forward
        )
        high = lax.ppermute(lax.slice_in_dim(block, 0, width, axis=dim), axis, backward)
        block = jnp.concatenate([low, block, high], axis=dim)
    return block


def upwind(padded, field, cx, cy):
    west = padded[:, :-2, 1:-1]
    east = padded[:, 2:, 1:-1]
    south = padded[:, 1:-1, :-2]
    north = padded[:, 1:-1, 2:]
    return cx * jnp.where(cx > 0, field - west, east - field) + cy * jnp.where(
        cy > 0, field - south, north - field
    )


def vertical(field, cz, mask):
    below = jnp.concatenate([field[:1], field[:-1]], axis=0)
    mask_below = jnp.concatenate([jnp.zeros_like(mask[:1]), mask[:-1]], axis=0)
    below = jnp.where(mask_below, below, field)
    above = jnp.concatenate([field[1:], field[-1:]], axis=0)
    return cz * jnp.where(cz > 0, field - below, above - field)


def dense_step(
    nest_field,
    courant_x,
    courant_y,
    courant_z,
    terrain,
    relax,
    interp_index,
    interp_weight,
    send_slots,
    parent_field,
    parent_cx,
    parent_cy,
    fb_index,
    fb_slot,
    fb_target,
):
    n_east = lax.axis_size("gx")
    n_north = lax.axis_size("gy")
    devices = n_east * n_north
    levels, nest_x, nest_y = nest_field.shape
    parent_x, parent_y = (parent_field.shape[1], parent_field.shape[2])
    parent_cols = parent_x * parent_y
    nest_cols = nest_x * nest_y
    slabs = parent_field
    slabs = jnp.concatenate([slabs, jnp.zeros((levels, 1, TILE), jnp.float32)], axis=1)
    picked = jnp.take(slabs, send_slots[0], axis=1)
    outgoing = picked.reshape(levels, devices, CAP, TILE)
    incoming = lax.all_to_all(outgoing, ("gx", "gy"), split_axis=1, concat_axis=1, tiled=True)
    received_cols = incoming.reshape(levels, -1).T
    padded_parent = extended(parent_field, (("gx", 1), ("gy", 2)), 1)
    advected = parent_field - upwind(padded_parent, parent_field, parent_cx, parent_cy)
    index_flat = interp_index.reshape(4, -1)
    weight_flat = interp_weight.reshape(4, -1)
    boundary_cols = weight_flat[0][:, None] * jnp.take(received_cols, index_flat[0], axis=0)
    for j in range(1, 4):
        boundary_cols = boundary_cols + weight_flat[j][:, None] * jnp.take(
            received_cols, index_flat[j], axis=0
        )
    boundary = boundary_cols.T.reshape(levels, nest_x, nest_y)
    level_ids = lax.broadcasted_iota(jnp.int32, (levels, 1, 1), 0)
    mask = level_ids >= terrain[None]
    field = jnp.where(mask, nest_field, 0.0)
    for step in range(SUBSTEPS):
        padded = extended(field, (("gx", 1), ("gy", 2)), 1)
        adv = field - upwind(padded, field, courant_x, courant_y) - vertical(field, courant_z, mask)
        field = jnp.where(mask, adv + relax[None] * (boundary - adv), 0.0)
    flat_nest = field.reshape(levels, nest_cols)
    row_count = fb_index.shape[1]
    averaged = fb_index.shape[2]
    row_ids = lax.broadcasted_iota(jnp.int32, (row_count, averaged), 0)
    averaging = jnp.zeros((row_count + 1, nest_cols), jnp.float32)
    averaging = averaging.at[row_ids, fb_index[0]].add(1.0 / averaged)
    slot_weights = jnp.take(averaging, fb_slot[0], axis=0)
    chosen_rows = lax.dot_general(
        slot_weights,
        flat_nest,
        (((1,), (1,)), ((), ())),
        precision=lax.Precision.HIGHEST,
        preferred_element_type=jnp.float32,
    )
    sending = chosen_rows.reshape(devices, FCAP * levels)
    arrived = lax.all_to_all(sending, ("gx", "gy"), split_axis=0, concat_axis=0, tiled=True)
    values = arrived.reshape(-1, levels)
    flat_parent = advected.reshape(levels, parent_cols)
    target = fb_target[0]
    current = jnp.take(flat_parent, jnp.minimum(target, parent_cols - 1), axis=1)
    delta = blend_rate * (values.T - current)
    updated = flat_parent.at[:, target].add(delta, mode="drop")
    return (field, updated.reshape(levels, parent_x, parent_y))


MESH = pl.DeviceIdType.MESH
LEV = 96
NX = 16
PXN = 32
KREQ = 64
GROUPS = 8
F32 = jnp.float32
BF16 = jnp.bfloat16
NT = (((1,), (1,)), ((), ()))


def halves(value):
    high = value.astype(BF16)
    return high, (value - high.astype(F32)).astype(BF16)


def step_kernel(
    slots_ref,
    nest_ref,
    cx_ref,
    cy_ref,
    cz_ref,
    terrain_ref,
    relax_ref,
    index_ref,
    weight_ref,
    parent_ref,
    pcx_ref,
    pcy_ref,
    fbi_ref,
    fbs_ref,
    fbt_ref,
    nest_out,
    keep_out,
    rows_out,
    flag_out,
    q0,
    q1,
    q2,
    ybuf,
    ypack,
    adv1,
    bound,
    pq,
    pys,
    pyk,
    keep,
    shi,
    slo,
    req,
    reqin,
    ans,
    ansin,
    xmat,
    counts,
    cmat,
    qmat,
    fbsend,
    fbin,
    hotm,
    tabm,
    rankm,
    relm,
    nraw,
    cxs,
    cys,
    czs,
    pcxs,
    pcys,
    nres,
    fbt,
    fbn,
    sem_in,
    sem_out,
    sem_req_s,
    sem_req_r,
    sem_ans_s,
    sem_ans_r,
    sem_fb_s,
    sem_fb_r,
    hs,
    hr,
):
    gx = lax.axis_index("gx")
    gy = lax.axis_index("gy")
    mz, my, mx, mc = lax.div(gx, 4), lax.rem(gx, 4), lax.div(gy, 2), lax.rem(gy, 2)
    me = gx * 8 + gy

    def chip(n, sign):
        dx = lax.rem(n, 4)
        dy = lax.rem(lax.div(n, 4) + dx, 4)
        dz = lax.rem(lax.div(n, 16) + dy, 4)
        if sign < 0:
            dz, dy, dx = 4 - dz, 4 - dy, 4 - dx
        z, y, x = lax.rem(mz + dz, 4), lax.rem(my + dy, 4), lax.rem(mx + dx, 4)
        return z * 4 + y, x * 2

    barrier = pltpu.get_barrier_semaphore()

    zs = [lax.rem(mz + k, 4) * 4 for k in range(4)]
    ys = [lax.rem(my + k, 4) for k in range(4)]
    xs = [lax.rem(mx + k, 4) * 2 for k in range(4)]

    def ahead(n):
        dx = n % 4
        dy = (n // 4 + dx) % 4
        dz = (n // 16 + dy) % 4
        return zs[dz] + ys[dy], xs[dx]

    for n in range(1, 64):
        tx, ty = ahead(n)
        for core in range(2):
            pl.semaphore_signal(barrier, inc=1, device_id=(tx, ty + core), device_id_type=MESH)
    pl.semaphore_signal(barrier, inc=1, device_id=(gx, mx * 2 + 1 - mc), device_id_type=MESH)

    def load(source, count, target, first, k):
        def one(x, carry):
            pltpu.make_async_copy(source.at[:, x], target.at[x + first], sem_in.at[k]).start()
            return carry

        lax.fori_loop(0, count, one, 0)

    def loaded(target, first, count, k):
        part = target.at[pl.ds(first, count)]
        pltpu.make_async_copy(part, part, sem_in.at[k]).wait()

    sub128 = lax.broadcasted_iota(jnp.int32, (128, 128), 0)
    lane128 = lax.broadcasted_iota(jnp.int32, (128, 128), 1)
    sub64 = lax.broadcasted_iota(jnp.int32, (KREQ, 128), 0)

    before = jnp.concatenate(
        [jnp.where(sub128 < lane128, 1.0, 0.0), jnp.ones((128, 128), F32)], axis=1
    ).astype(BF16)
    run = jnp.zeros((128, 128), F32)
    top = jnp.zeros((1, 128), F32)
    for x in range(NX):
        idx = [index_ref[j, x : x + 1, :] for j in range(4)]
        src = idx[0] >> 8
        dz, dy, dx = (src >> 5) - mz, ((src >> 3) & 3) - my, ((src >> 1) & 3) - mx
        rel = (((dz - dy) & 3) << 5) | (((dy - dx) & 3) << 3) | ((dx & 3) << 1) | (src & 1)
        relm[x : x + 1, :] = rel
        hot = jnp.where(sub128 == rel, 1.0, 0.0)
        hotb = hot.astype(BF16)
        both = jnp.dot(hotb, before, preferred_element_type=F32)
        rank = jnp.sum(hot * (both[:, :128] + run), axis=0, keepdims=True)
        run = run + both[:, 128:]
        top = jnp.maximum(top, rank)
        here = sub64 == rank.astype(jnp.int32)
        rankm[x] = jnp.where(here, 1.0, 0.0).astype(BF16)
        at = slice(128 * x, 128 * x + 128)
        hotm[:, at] = hotb
        for j in range(4):
            low = (idx[j] & 255).astype(F32)
            w = weight_ref[j, x : x + 1, :]
            whi = w.astype(BF16).astype(F32)
            tabm[128 * j : 128 * j + 64, at] = jnp.where(here, low, 0.0).astype(BF16)
            tabm[128 * j + 64 : 128 * j + 128, at] = jnp.where(here, whi, 0.0).astype(BF16)
            tabm[512 + 128 * j : 576 + 128 * j, at] = jnp.zeros((KREQ, 128), BF16)
            tabm[576 + 128 * j : 640 + 128 * j, at] = jnp.where(here, w - whi, 0.0).astype(BF16)
    flag = jnp.max(jnp.where(top >= KREQ, 1.0, 0.0), axis=1, keepdims=True)
    racc = lax.dot_general(hotm[...], tabm[...], NT, preferred_element_type=F32)
    for j in range(4):
        req[:, j, :] = (
            racc[:, 128 * j : 128 * j + 128] + racc[:, 512 + 128 * j : 640 + 128 * j]
        )

    load(parent_ref, PXN, pq, 1, 0)
    load(nest_ref, NX, nraw, 0, 1)
    pl.semaphore_wait(barrier, 127)

    for n in range(1, 64):
        tx, ty = ahead(n)
        for core in range(2):
            pltpu.make_async_remote_copy(
                src_ref=req.at[2 * n + core],
                dst_ref=reqin.at[2 * n + mc],
                send_sem=sem_req_s,
                recv_sem=sem_req_r.at[n // (64 // GROUPS)],
                device_id=(tx, ty + core),
                device_id_type=MESH,
            ).start()
    pltpu.make_async_remote_copy(
        src_ref=req.at[1 - mc],
        dst_ref=reqin.at[mc],
        send_sem=sem_req_s,
        recv_sem=sem_req_r.at[0],
        device_id=(gx, mx * 2 + 1 - mc),
        device_id_type=MESH,
    ).start()
    pltpu.make_async_copy(req.at[mc], reqin.at[mc], sem_req_r.at[0]).start()

    load(cx_ref, NX, cxs, 0, 2)
    load(cy_ref, NX, cys, 0, 3)
    load(cz_ref, NX, czs, 0, 4)
    load(pcx_ref, PXN, pcxs, 0, 5)
    load(pcy_ref, PXN, pcys, 0, 6)

    lev = lax.broadcasted_iota(jnp.int32, (LEV, 128), 0)
    lane = lax.broadcasted_iota(jnp.int32, (LEV, 128), 1)

    def edge_copies(field, count, packed, landing, at):
        def face(x):
            return field.at[x, pl.ds(8, LEV)] if count == NX else field.at[x]

        west = (gx > 0, face(1), face(count + 1), (gx - 1, gy))
        east = (gx < 15, face(count), face(0), (gx + 1, gy))
        south = (gy > 0, packed.at[0], landing.at[1], (gx, gy - 1))
        north = (gy < 7, packed.at[1], landing.at[0], (gx, gy + 1))
        made = []
        for k, (has, src, dst, target) in enumerate((west, east, south, north)):
            made.append(
                (
                    has,
                    pltpu.make_async_remote_copy(
                        src_ref=src,
                        dst_ref=dst,
                        send_sem=hs.at[at, k],
                        recv_sem=hr.at[at, k],
                        device_id=target,
                        device_id_type=MESH,
                    ),
                )
            )
        return made

    def edges_start(made):
        for has, copy in made:
            pl.when(has)(copy.start)

    def edges_wait(made):
        for k, other in ((0, 1), (1, 0), (2, 3), (3, 2)):
            pl.when(made[other][0])(made[k][1].wait_recv)

    def edges_sent(made):
        for has, copy in made:
            pl.when(has)(copy.wait_send)

    def clear_edges(field, count, landing):
        zero = jnp.zeros((LEV, 128), F32)

        @pl.when(gx == 0)
        def _():
            field[0, pl.ds(8 if count == NX else 0, LEV), :] = zero

        @pl.when(gx == 15)
        def _():
            field[count + 1, pl.ds(8 if count == NX else 0, LEV), :] = zero

        @pl.when(gy == 0)
        def _():
            landing[0] = zero

        @pl.when(gy == 7)
        def _():
            landing[1] = zero

    def pack_edges(field, count, packed):
        base = 8 if count == NX else 0

        def one(x, carry):
            low, high = carry
            here = field[x + 1, pl.ds(base, LEV), :]
            low = jnp.where(lane == x, pltpu.roll(here, x, 1), low)
            high = jnp.where(lane == x, pltpu.roll(here, x + 1, 1), high)
            return low, high

        zero = jnp.zeros((LEV, 128), F32)
        low, high = lax.fori_loop(0, count, one, (zero, zero), unroll=16)
        packed[0] = low
        packed[1] = high

    deep = 32
    lanec = lax.broadcasted_iota(jnp.int32, (deep, 128), 1)
    levc = lax.broadcasted_iota(jnp.int32, (deep, 128), 0)

    def across(field, base, x, l0, landing, cx, cy):
        rows = pl.ds(base + l0, deep)
        here = field[x + 1, rows, :]
        west, east = field[x, rows, :], field[x + 2, rows, :]
        edge = pl.ds(l0, deep)
        south = jnp.where(
            lanec == 0,
            pltpu.roll(landing[0, edge, :], lax.rem(128 - x, 128), 1),
            pltpu.roll(here, 1, 1),
        )
        north = jnp.where(
            lanec == 127, pltpu.roll(landing[1, edge, :], 127 - x, 1), pltpu.roll(here, 127, 1)
        )
        return here, here - cx * jnp.where(cx > 0, here - west, east - here) - cy * jnp.where(
            cy > 0, here - south, north - here
        )

    def advance(field, x, l0, landing):
        edge = pl.ds(l0, deep)
        here, adv = across(field, 8, x, l0, landing, cxs[x, edge, :], cys[x, edge, :])
        cz = czs[x, edge, :]
        lower, upper = field[x + 1, pl.ds(7 + l0, deep), :], field[x + 1, pl.ds(9 + l0, deep), :]
        below = jnp.where(levc + (l0 - 1) >= terrain_ref[pl.ds(x, 1), :], lower, here)
        above = jnp.where(levc == LEV - 1 - l0, here, upper)
        return adv - cz * jnp.where(cz > 0, here - below, above - here)

    clear_edges(pq, PXN, pys)
    clear_edges(q0, NX, ybuf.at[0])
    clear_edges(q1, NX, ybuf.at[1])
    clear_edges(q2, NX, ybuf.at[2])

    blank8 = jnp.zeros((8, 128), F32)
    loaded(nraw, 0, NX, 1)

    def start_nest(x, carry):
        for field in (q0, q1, q2):
            field[x + 1, 0:8, :] = blank8
            field[x + 1, LEV + 8 : LEV + 16, :] = blank8
        q0[x + 1, 8 : LEV + 8, :] = jnp.where(lev >= terrain_ref[pl.ds(x, 1), :], nraw[x], 0.0)
        return carry

    lax.fori_loop(0, NX, start_nest, 0)
    pack_edges(q0, NX, ypack.at[0])
    q0_edges = edge_copies(q0, NX, ypack.at[0], ybuf.at[0], 0)
    edges_start(q0_edges)

    loaded(pq, 1, PXN, 0)

    def split(x, carry):
        shi[x], slo[x] = halves(pq[x + 1])
        return carry

    lax.fori_loop(0, PXN, split, 0, unroll=2)
    shi[PXN] = jnp.zeros((LEV, 128), BF16)
    slo[PXN] = jnp.zeros((LEV, 128), BF16)
    pack_edges(pq, PXN, pyk)
    p_edges = edge_copies(pq, PXN, pyk, pys, 1)
    edges_start(p_edges)


    def asked(g):
        part = reqin.at[pl.ds(g * (128 // GROUPS), 128 // GROUPS)]
        pltpu.make_async_copy(part, part, sem_req_r.at[g]).wait()

    sub256 = lax.broadcasted_iota(jnp.int32, (256, 128), 0)
    left48 = lax.broadcasted_iota(jnp.int32, (48, 128), 1) < 64
    left4 = lax.broadcasted_iota(jnp.int32, (4, 128), 1) < 64

    def answer(n, tx, ty):
        a, b = reqin[2 * n], reqin[2 * n + 1]
        place = jnp.where(left4, a, pltpu.roll(b, 64, 1)).astype(jnp.int32)
        amount = jnp.where(left4, pltpu.roll(a, 64, 1), b)
        table = jnp.zeros((256, 128), F32)
        for j in range(4):
            table = jnp.where(sub256 == place[j : j + 1], amount[j : j + 1], table)
        right = jnp.concatenate(halves(table), axis=1)
        base = (tx * 8 + ty) * 2
        rows = []
        for core in range(2):
            first, second = slots_ref[base + 2 * core], slots_ref[base + 2 * core + 1]
            rows.append(jnp.concatenate([shi[first], shi[second]], axis=1))
            rows.append(jnp.concatenate([slo[first], slo[second]], axis=1))
        out = jnp.dot(jnp.concatenate(rows, axis=0), right, preferred_element_type=F32)
        v0 = out[0:96, :128] + out[0:96, 128:] + out[96:192, :128]
        v1 = out[192:288, :128] + out[192:288, 128:] + out[288:384, :128]
        return (
            jnp.where(left48, v0[:48], pltpu.roll(v0[48:], 64, 1)),
            jnp.where(left48, pltpu.roll(v1[:48], 64, 1), v1[48:]),
        )

    def reply(base, count):
        places = [chip(base + u, -1) for u in range(count)]
        made = [answer(base + u, *places[u]) for u in range(count)]
        for u in range(count):
            ans[2 * (base + u)], ans[2 * (base + u) + 1] = made[u]
        for u in range(count):
            n = base + u
            tx, ty = places[u]
            for core in range(2):
                pltpu.make_async_remote_copy(
                    src_ref=ans.at[2 * n + core],
                    dst_ref=ansin.at[2 * n + mc],
                    send_sem=sem_ans_s,
                    recv_sem=sem_ans_r.at[lax.div(n, 64 // GROUPS)],
                    device_id=(tx, ty + core),
                    device_id_type=MESH,
                ).start()

    def replies(r, carry):
        asked(r)
        reply(8 * r, 4)
        reply(8 * r + 4, 4)
        return carry

    asked(0)
    ans[0], ans[1] = answer(0, gx, mx * 2)
    pltpu.make_async_remote_copy(
        src_ref=ans.at[1 - mc],
        dst_ref=ansin.at[mc],
        send_sem=sem_ans_s,
        recv_sem=sem_ans_r.at[0],
        device_id=(gx, mx * 2 + 1 - mc),
        device_id_type=MESH,
    ).start()
    pltpu.make_async_copy(ans.at[mc], ansin.at[mc], sem_ans_r.at[0]).start()
    reply(jnp.int32(1), 3)
    reply(jnp.int32(4), 4)
    lax.fori_loop(1, GROUPS, replies, 0)

    for k, (target, count) in enumerate(
        ((cxs, NX), (cys, NX), (czs, NX), (pcxs, PXN), (pcys, PXN))
    ):
        loaded(target, 0, count, k + 2)
    edges_wait(q0_edges)
    chunks = range(0, LEV, deep)

    def first_nest(x, carry):
        for l0 in chunks:
            adv1[x, pl.ds(l0, deep), :] = advance(q0, x, l0, ybuf.at[0])
        bound[x] = jnp.zeros((LEV, 128), F32)
        return carry

    lax.fori_loop(0, NX, first_nest, 0)

    edges_wait(p_edges)
    sub512 = lax.broadcasted_iota(jnp.int32, (256, 512), 0)
    ones8 = jnp.ones((8, 512), BF16)

    def parents(i, carry):
        hot = jnp.where(sub512 == fbt_ref[...] - 256 * i, 1.0, 0.0).astype(BF16)
        left = 1.0 - 0.5 * lax.dot_general(ones8, hot, NT, preferred_element_type=F32)[0:1]
        for k in range(2):
            x = 2 * i + k
            for l0 in chunks:
                edge = pl.ds(l0, deep)
                moved = across(pq, 0, x, l0, pys, pcxs[x, edge, :], pcys[x, edge, :])[1]
                keep[x, edge, :] = moved * left[:, 128 * k : 128 * k + 128]
        return carry

    lax.fori_loop(0, PXN // 2, parents, 0)
    pltpu.make_async_copy(keep, keep_out, sem_out.at[1]).start()

    sub16 = lax.broadcasted_iota(jnp.int32, (16, 128), 0)

    fbt[...] = jnp.full((128, 256), -1.0, F32)

    def turn(i, carry):
        fbt[pl.ds(i, 1), :] = fbi_ref[i].astype(F32)
        return carry

    lax.fori_loop(0, 81, turn, 0)
    fbn[...] = jnp.transpose(fbt[...]).astype(jnp.int32)

    def count(r, carry):
        made = []
        for u in range(8):
            highs, lows = [], []
            for k in range(2):
                row = fbn[pl.ds(16 * r + 2 * u + k, 1), :]
                high = jnp.where(sub16 == (row >> 7), 1.0, 0.0).astype(BF16)
                blank = jnp.zeros((16, 128), BF16)
                highs.append(jnp.concatenate([high, blank] if k == 0 else [blank, high], axis=1))
                lows.append(jnp.where(sub128 == (row & 127), 1.0, 0.0).astype(BF16))
            made.append(
                lax.dot_general(
                    jnp.concatenate(highs, axis=0),
                    jnp.concatenate(lows, axis=1),
                    NT,
                    preferred_element_type=F32,
                )
            )
        for u in range(8):
            counts[16 * r + 2 * u] = made[u][:16]
            counts[16 * r + 2 * u + 1] = made[u][16:]
        return carry

    lax.fori_loop(0, 16, count, 0)
    row256 = lax.broadcasted_iota(jnp.int32, (256, 512), 0)
    chosen = jnp.transpose(jnp.where(row256 == fbs_ref[...], 1.0, 0.0)).astype(BF16)
    for x in range(NX):
        cmat[:, 128 * x : 128 * x + 128] = jnp.dot(
            chosen, counts[:, x, :].astype(BF16), preferred_element_type=F32
        ).astype(BF16)
    qmat[...] = jnp.zeros_like(qmat)


    per = 64 // GROUPS
    for g in range(GROUPS):
        part = ansin.at[pl.ds(2 * per * g, 2 * per)]
        pltpu.make_async_copy(part, part, sem_ans_r.at[g]).wait()
        for i in range(per):
            a, b = ansin[2 * (per * g + i)], ansin[2 * (per * g + i) + 1]
            upper = jnp.where(left48, a, pltpu.roll(b, 64, 1))
            lower = jnp.where(left48, pltpu.roll(a, 64, 1), b)
            high, low = halves(jnp.concatenate([upper, lower], axis=0))
            xmat[0:96, 128 * i : 128 * i + 128] = high
            xmat[96:192, 128 * i : 128 * i + 128] = low

        def pick(x, carry, g=g):
            hots = []
            for k in range(2):
                owner = jnp.broadcast_to(relm[pl.ds(2 * x + k, 1), :], (16, 128))
                ranks = rankm[2 * x + k]
                blocks = []
                for i in range(2 * per):
                    mine = jnp.where(owner == 2 * per * g + i, 1.0, 0.0).astype(BF16)
                    blocks.append(ranks * jnp.concatenate([mine] * (KREQ // 16), axis=0))
                hots.append(jnp.concatenate(blocks, axis=0))
            got = jnp.dot(xmat[...], jnp.concatenate(hots, axis=1), preferred_element_type=F32)
            bound[2 * x] += got[:96, :128] + got[96:, :128]
            bound[2 * x + 1] += got[:96, 128:] + got[96:, 128:]
            return carry

        lax.fori_loop(0, NX // 2, pick, 0, unroll=4)

    def settle(x, l0, adv):
        terrain = terrain_ref[pl.ds(x, 1), :]
        rel = relax_ref[pl.ds(x, 1), :]
        pull = bound[x, pl.ds(l0, deep), :] - adv
        return jnp.where(levc + l0 >= terrain, adv + rel * pull, 0.0)

    def first_settle(x, carry):
        for l0 in chunks:
            q1[x + 1, pl.ds(8 + l0, deep), :] = settle(x, l0, adv1[x, pl.ds(l0, deep), :])
        return carry

    lax.fori_loop(0, NX, first_settle, 0)
    edges = [q0_edges, p_edges]

    def exchange(now, step):
        pack_edges(now, NX, ypack.at[step])
        made = edge_copies(now, NX, ypack.at[step], ybuf.at[step], step + 1)
        edges_start(made)
        edges_wait(made)
        edges.append(made)

    exchange(q1, 1)

    def second(x, carry):
        for l0 in chunks:
            q2[x + 1, pl.ds(8 + l0, deep), :] = settle(x, l0, advance(q1, x, l0, ybuf.at[1]))
        return carry

    lax.fori_loop(0, NX, second, 0, unroll=4)
    exchange(q2, 2)

    def third(x, carry):
        at = pl.ds(pl.multiple_of(128 * x, 128), 128)
        for l0 in chunks:
            value = settle(x, l0, advance(q2, x, l0, ybuf.at[2]))
            nres[x, pl.ds(l0, deep), :] = value
            high, low = halves(value)
            qmat[pl.ds(l0, deep), at] = high
            qmat[pl.ds(128 + l0, deep), at] = low
        return carry

    lax.fori_loop(0, NX, third, 0, unroll=4)

    got = lax.dot_general(cmat[...], qmat[...], NT, preferred_element_type=F32)
    rows = (got[:, :128] + got[:, 128:]) * (1.0 / 81.0)
    lane512 = lax.broadcasted_iota(jnp.int32, (512, 128), 1)
    rows = jnp.where(lane512 == LEV, flag, rows)
    fbsend[...] = rows.reshape(128, 4, 128)

    for n in range(1, 64):
        tx, ty = ahead(n)
        for core in range(2):
            pltpu.make_async_remote_copy(
                src_ref=fbsend.at[tx * 8 + ty + core],
                dst_ref=fbin.at[me],
                send_sem=sem_fb_s,
                recv_sem=sem_fb_r,
                device_id=(tx, ty + core),
                device_id_type=MESH,
            ).start()
    other = mx * 2 + 1 - mc
    pltpu.make_async_remote_copy(
        src_ref=fbsend.at[gx * 8 + other],
        dst_ref=fbin.at[me],
        send_sem=sem_fb_s,
        recv_sem=sem_fb_r,
        device_id=(gx, other),
        device_id_type=MESH,
    ).start()
    pltpu.make_async_copy(fbsend.at[me], fbin.at[me], sem_fb_r).start()

    def store_nest(x, carry):
        pltpu.make_async_copy(nres.at[x], nest_out.at[:, x], sem_out.at[0]).start()
        return carry

    lax.fori_loop(0, NX, store_nest, 0)
    pltpu.make_async_copy(fbin, fbin, sem_fb_r).wait()


    pltpu.make_async_copy(fbin, rows_out, sem_out.at[2]).start()
    values = fbin[...].reshape(512, 128)
    worst = jnp.max(jnp.where(lane512 == LEV, values, 0.0))
    flag_out[0] = jnp.where(worst > 0.5, 1, 0)
    pltpu.make_async_copy(nres, nres, sem_out.at[0]).wait()
    pltpu.make_async_copy(keep, keep_out, sem_out.at[1]).wait()
    pltpu.make_async_copy(fbin, rows_out, sem_out.at[2]).wait()

    for buffer, sem in ((req, sem_req_s), (ans, sem_ans_s), (fbsend, sem_fb_s)):
        part = buffer.at[pl.ds(0, 127)]
        pltpu.make_async_copy(part, part, sem).wait()
    for made in edges:
        edges_sent(made)


def fused_step(
    nest_field,
    courant_x,
    courant_y,
    courant_z,
    terrain,
    relax,
    interp_index,
    interp_weight,
    send_slots,
    parent_field,
    parent_cx,
    parent_cy,
    fb_index,
    fb_slot,
    fb_target,
):
    vmem = pl.BlockSpec(memory_space=pltpu.VMEM)
    smem = pl.BlockSpec(memory_space=pltpu.SMEM)
    hbm = pl.BlockSpec(memory_space=pl.ANY)
    slab = (LEV, 128)
    scratch = [
        pltpu.VMEM((NX + 2, LEV + 16, 128), F32),
        pltpu.VMEM((NX + 2, LEV + 16, 128), F32),
        pltpu.VMEM((NX + 2, LEV + 16, 128), F32),
        pltpu.VMEM((3, 2) + slab, F32),
        pltpu.VMEM((3, 2) + slab, F32),
        pltpu.VMEM((NX,) + slab, F32),
        pltpu.VMEM((NX,) + slab, F32),
        pltpu.VMEM((PXN + 2,) + slab, F32),
        pltpu.VMEM((2,) + slab, F32),
        pltpu.VMEM((2,) + slab, F32),
        pltpu.VMEM((PXN,) + slab, F32),
        pltpu.VMEM((PXN + 1,) + slab, BF16),
        pltpu.VMEM((PXN + 1,) + slab, BF16),
        pltpu.VMEM((128, 4, 128), F32),
        pltpu.VMEM((128, 4, 128), F32),
        pltpu.VMEM((128, 48, 128), F32),
        pltpu.VMEM((128, 48, 128), F32),
        pltpu.VMEM((192, 64 // GROUPS * 128), BF16),
        pltpu.VMEM((256, NX, 128), F32),
        pltpu.VMEM((512, NX * 128), BF16),
        pltpu.VMEM((256, NX * 128), BF16),
        pltpu.VMEM((128, 4, 128), F32),
        pltpu.VMEM((128, 4, 128), F32),
        pltpu.VMEM((128, NX * 128), BF16),
        pltpu.VMEM((1024, NX * 128), BF16),
        pltpu.VMEM((NX, KREQ, 128), BF16),
        pltpu.VMEM((NX, 128), jnp.int32),
        pltpu.VMEM((NX,) + slab, F32),
        pltpu.VMEM((NX,) + slab, F32),
        pltpu.VMEM((NX,) + slab, F32),
        pltpu.VMEM((NX,) + slab, F32),
        pltpu.VMEM((PXN,) + slab, F32),
        pltpu.VMEM((PXN,) + slab, F32),
        pltpu.VMEM((NX,) + slab, F32),
        pltpu.VMEM((128, 256), F32),
        pltpu.VMEM((256, 128), jnp.int32),
        pltpu.SemaphoreType.DMA((7,)),
        pltpu.SemaphoreType.DMA((3,)),
        pltpu.SemaphoreType.DMA,
        pltpu.SemaphoreType.DMA((GROUPS,)),
        pltpu.SemaphoreType.DMA,
        pltpu.SemaphoreType.DMA((GROUPS,)),
        pltpu.SemaphoreType.DMA,
        pltpu.SemaphoreType.DMA,
        pltpu.SemaphoreType.DMA((4, 4)),
        pltpu.SemaphoreType.DMA((4, 4)),
    ]
    return pl.pallas_call(
        step_kernel,
        out_shape=(
            jax.ShapeDtypeStruct(nest_field.shape, F32),
            jax.ShapeDtypeStruct((PXN,) + slab, F32),
            jax.ShapeDtypeStruct((128, 4, 128), F32),
            jax.ShapeDtypeStruct((1,), jnp.int32),
        ),
        in_specs=[smem] + [hbm] * 4 + [vmem] * 4 + [hbm] * 3 + [vmem] * 3,
        out_specs=(hbm, hbm, hbm, smem),
        scratch_shapes=scratch,
        compiler_params=pltpu.CompilerParams(
            collective_id=0, has_side_effects=True, vmem_limit_bytes=56 * 2**20
        ),
        name="step",
    )(
        send_slots[0],
        nest_field,
        courant_x,
        courant_y,
        courant_z,
        terrain,
        relax,
        interp_index,
        interp_weight,
        parent_field,
        parent_cx,
        parent_cy,
        jnp.transpose(fb_index, (2, 0, 1)),
        fb_slot,
        fb_target,
    )


def finish_kernel(
    fbt_ref, rows_ref, nest_ref, keep_ref, nest_out, parent_out, nest_buf, keep, got_rows, tmat, come, go
):
    per = PXN // 8
    arriving = []
    rows_in = pltpu.make_async_copy(rows_ref, got_rows, come.at[1, 4])
    rows_in.start()
    for part in range(8):
        xs = pl.ds(per * part, per)
        arriving.append(pltpu.make_async_copy(keep_ref.at[xs], keep.at[xs], come.at[0, part]))
        arriving[-1].start()
    nest = []
    for part in range(4):
        rows = pl.ds(24 * part, 24)
        nest.append(pltpu.make_async_copy(nest_ref.at[rows], nest_buf.at[rows], come.at[1, part]))
        nest[-1].start()
    sub512 = lax.broadcasted_iota(jnp.int32, (256, 512), 0)
    for i in range(PXN // 2):
        tmat[i] = jnp.where(sub512 == fbt_ref[...] - 256 * i, 1.0, 0.0).astype(BF16)
    rows_in.wait()
    high, low = halves(jnp.transpose(got_rows[...].reshape(512, 128))[:96])
    both = jnp.concatenate([high, low], axis=0)
    for i in range(PXN // 2):
        got = lax.dot_general(both, tmat[i], NT, preferred_element_type=F32)
        if 2 * i % per == 0:
            arriving[2 * i // per].wait()
        for k in range(2):
            x, at = 2 * i + k, slice(128 * k, 128 * k + 128)
            keep[x] += 0.5 * (got[:96, at] + got[96:, at])
            pltpu.make_async_copy(keep.at[x], parent_out.at[:, x], go.at[0]).start()
        if i < 4:
            nest[i].wait()
            rows = pl.ds(24 * i, 24)
            pltpu.make_async_copy(nest_buf.at[rows], nest_out.at[rows], go.at[1]).start()
    pltpu.make_async_copy(nest_buf, nest_buf, go.at[1]).wait()
    pltpu.make_async_copy(keep, keep, go.at[0]).wait()


def finish(fb_target, rows, nest, keep, parent_shape):
    vmem = pl.BlockSpec(memory_space=pltpu.VMEM)
    hbm = pl.BlockSpec(memory_space=pl.ANY)
    return pl.pallas_call(
        finish_kernel,
        out_shape=(
            jax.ShapeDtypeStruct(nest.shape, F32),
            jax.ShapeDtypeStruct(parent_shape, F32),
        ),
        in_specs=[vmem, hbm, hbm, hbm],
        out_specs=(hbm, hbm),
        scratch_shapes=[
            pltpu.VMEM(nest.shape, F32),
            pltpu.VMEM(keep.shape, F32),
            pltpu.VMEM(rows.shape, F32),
            pltpu.VMEM((PXN // 2, 256, 512), BF16),
            pltpu.SemaphoreType.DMA((2, 8)),
            pltpu.SemaphoreType.DMA((2,)),
        ],
        compiler_params=pltpu.CompilerParams(vmem_limit_bytes=24 * 2**20),
        name="finish",
    )(fb_target, rows, nest, keep)


def on_device(*args):
    nest, keep, rows, flags = fused_step(*args)
    return lax.cond(
        flags[0] > 0,
        lambda: dense_step(*args),
        lambda: finish(args[14], rows, nest, keep, args[9].shape),
    )


def solution(mesh):
    in_specs = (
        P(None, "gx", "gy"),
        P(None, "gx", "gy"),
        P(None, "gx", "gy"),
        P(None, "gx", "gy"),
        P("gx", "gy"),
        P("gx", "gy"),
        P(None, "gx", "gy"),
        P(None, "gx", "gy"),
        P(("gx", "gy"), None),
        P(None, "gx", "gy"),
        P(None, "gx", "gy"),
        P(None, "gx", "gy"),
        P(("gx", "gy"), None, None),
        P(("gx", "gy"), None),
        P(("gx", "gy"), None),
    )
    out_specs = (P(None, "gx", "gy"), P(None, "gx", "gy"))
    return jax.shard_map(
        on_device, mesh=mesh, in_specs=in_specs, out_specs=out_specs, check_vma=False
    )
```
